128 devices in a mesh: vb: 8 (over z, core), ob: 16 (over x, y).
Axes of the slice: x: 4, y: 4, z: 4, core: 2. Of those that a mesh axis runs over, the one named last changes fastest.
Arguments:
- amplitudes: float32 [768, 8, 6144], P(('vb', 'ob')), may hold values from -6 to 6
- ovov: float32 [8, 6144, 6144], P(None, 'ob', 'vb'), may hold values from -0.109375 to 0.109375
- row_sizes: int32 [8], replicated, may hold values from 192 to 768, as said below
- pair_sizes: int32 [8], replicated, may hold values from 1536 to 6144, as said below
Outputs:
- residual: float32 [768, 8, 6144], P('ob', None, 'vb')
The draws below stay inside these ranges and needn't reach their ends.
Inputs may be any that keep to these rules, and one draw needn't show every extreme that they name: `row_sizes`: one irrep fills all 768 row slots. `pair_sizes`: multiples of 64; one irrep fills all 6144 slots.
All inputs are finite; a program needn't handle non-finite values.
Results may differ from the reference program's by a relative error of at most 0.0003.
Values sent between devices are 32-bit elements; how exact they have to be, the bound alone decides.
No kernel may reach another device: no remote copies, remote signals or barrier semaphores. Data moves between devices by JAX's collectives and lax.ppermute only.
A program may use at most 192 MiB of HBM per device.

```python
import jax
import jax.numpy as jnp
from jax import lax

IRREPS = 8
TILE = 64
MC = 768
PC = 6144


def draw_row_sizes(key, part):
    key = jax.random.fold_in(key, 11)
    count_key, pick_key = jax.random.split(key)
    counts = jax.random.randint(count_key, (IRREPS,), MC // 4, MC + 1, dtype=jnp.int32)
    chosen = jax.random.randint(pick_key, (), 0, IRREPS, dtype=jnp.int32)
    return jnp.where(jnp.arange(IRREPS, dtype=jnp.int32) == chosen, MC, counts).astype(jnp.int32)


def draw_pair_sizes(key, part):
    key = jax.random.fold_in(key, 23)
    count_key, pick_key = jax.random.split(key)
    counts = jax.random.randint(count_key, (IRREPS,), PC // (4 * TILE), PC // TILE + 1, dtype=jnp.int32) * TILE
    chosen = jax.random.randint(pick_key, (), 0, IRREPS, dtype=jnp.int32)
    return jnp.where(jnp.arange(IRREPS, dtype=jnp.int32) == chosen, PC, counts).astype(jnp.int32)


def levels(own_key, shape, pieces, smallest, high):
    gain, own = 1.0, jax.random.fold_in(own_key, 6)
    for position, shards_of in pieces:
        heights = jnp.exp(jax.random.uniform(jax.random.fold_in(own, position), (shards_of,), jnp.float32, smallest / len(pieces), high / len(pieces)))
        gain = gain * jnp.repeat(heights, shape[position] // shards_of).reshape([-1 if axis == position else 1 for axis in range(len(shape))])
    return gain


def scatter_about(stream_key, extent, width, most, cuts=(), kind=jnp.bfloat16):
    loudness = levels(stream_key, extent, cuts, -0.22, 0.18) if cuts else 1.0
    drawn = jax.random.normal(stream_key, extent, jnp.float32) * width * loudness
    return jnp.minimum(jnp.maximum(drawn, -most), most).astype(kind)


def setup_inputs(seed: int = 0) -> dict:
    splits = jax.random.split(jax.random.key(seed), 5)
    return {
        "amplitudes": scatter_about(splits[0], (MC, IRREPS, PC), 1.0, 6.0, ((0, 128),), jnp.float32),
        "ovov": scatter_about(splits[1], (IRREPS, PC, PC), (PC // 2) ** -0.5, 0.109375, ((1, 16), (2, 8)), jnp.float32),
        "row_sizes": draw_row_sizes(jax.random.fold_in(splits[4], 71), 0),
        "pair_sizes": draw_pair_sizes(jax.random.fold_in(splits[4], 71), 0),
    }


def one_irrep(blocks):
    amp_block, ovov_block, row_count, pair_count = blocks
    row_ids = lax.broadcasted_iota(jnp.int32, amp_block.shape, 0)
    pair_ids = lax.broadcasted_iota(jnp.int32, amp_block.shape, 1)
    live_amp = jnp.where((row_ids < row_count) & (pair_ids < pair_count), amp_block, jnp.zeros_like(amp_block))
    left_ids = lax.broadcasted_iota(jnp.int32, ovov_block.shape, 0)
    right_ids = lax.broadcasted_iota(jnp.int32, ovov_block.shape, 1)
    live_ovov = jnp.where((left_ids < pair_count) & (right_ids < pair_count), ovov_block, jnp.zeros_like(ovov_block))
    return jnp.dot(live_amp, live_ovov, precision=lax.Precision.HIGHEST, preferred_element_type=jnp.float32)


def reference(amplitudes, ovov, row_sizes, pair_sizes):
    result = lax.map(one_irrep, (jnp.transpose(amplitudes, (1, 0, 2)), ovov, row_sizes, pair_sizes))
    return jnp.transpose(result, (1, 0, 2))
```

```python
import functools

import jax
import jax.numpy as jnp
from jax import lax
from jax.experimental import pallas as pl
from jax.experimental.pallas import tpu as pltpu
from jax.sharding import PartitionSpec as P

SIDE = 4
VMEM = 48 * 1024 * 1024


def hops(stride, delta):
    pairs = []
    for i in range(SIDE * SIDE):
        d = (i // stride) % SIDE
        pairs.append((i, i + ((d + delta) % SIDE - d) * stride))
    return pairs


def split_kernel(sizes, origin, v_ref, hi_ref, lo_ref):
    g = pl.program_id(0)
    size = sizes[g]
    shape = v_ref.shape[1:]
    p = origin[0] + lax.broadcasted_iota(jnp.int32, shape, 0)
    q = origin[1] + lax.broadcasted_iota(jnp.int32, shape, 1)
    v = jnp.where((p < size) & (q < size), v_ref[0], 0.0)
    hi = v.astype(jnp.bfloat16)
    hi_ref[0] = hi
    lo_ref[0] = (v - hi.astype(jnp.float32)).astype(jnp.bfloat16)


def split_ovov(ovov, pair_sizes, origin):
    g, p, q = ovov.shape
    spec = pl.BlockSpec((1, p, q), lambda i, *_: (i, 0, 0))
    return pl.pallas_call(
        split_kernel,
        grid_spec=pltpu.PrefetchScalarGridSpec(
            num_scalar_prefetch=2, grid=(g,), in_specs=[spec], out_specs=[spec, spec]
        ),
        out_shape=[jax.ShapeDtypeStruct(ovov.shape, jnp.bfloat16)] * 2,
        compiler_params=pltpu.CompilerParams(vmem_limit_bytes=VMEM),
        cost_estimate=pl.CostEstimate(flops=0, bytes_accessed=2 * ovov.size * 4, transcendentals=0),
        name="split_ovov",
    )(pair_sizes, origin, ovov)


def product(a_refs, hi_ref, lo_ref):
    a = jnp.concatenate([r[0, 0, 0] for r in a_refs], axis=0)
    a_hi = a.astype(jnp.bfloat16)
    a_lo = (a - a_hi.astype(jnp.float32)).astype(jnp.bfloat16)
    dot = functools.partial(jnp.dot, preferred_element_type=jnp.float32)
    return dot(a_hi, hi_ref[0]) + (dot(a_lo, hi_ref[0]) + dot(a_hi, lo_ref[0]))


def first_kernel(blocks, a0, a1, a2, a3, hi, lo, out_a, out_b):
    rows = a0.shape[3]
    acc = product((a0, a1, a2, a3), hi, lo)
    for k in range(2):
        out_a[k, 0] = acc[k * rows : (k + 1) * rows]
        out_b[k, 0] = acc[(k + 2) * rows : (k + 3) * rows]


def second_kernel(half, blocks, a0, a1, a2, a3, hi, lo, recv, out):
    rows = a0.shape[3]
    acc = product((a0, a1, a2, a3), hi, lo)
    for k in range(SIDE):
        part = acc[k * rows : (k + 1) * rows]
        if k // 2 == half:
            part = part + recv[k % 2, 0]
        out[k, 0] = part


def third_kernel(blocks, a0, a1, a2, a3, hi, lo, recv_p, recv_m, o0, o1, o2, o3):
    rows = a0.shape[3]
    acc = product((a0, a1, a2, a3), hi, lo)
    for k, out in enumerate((o0, o1, o2, o3)):
        j = blocks[SIDE + k]
        out[0] = acc[k * rows : (k + 1) * rows] + recv_p[j, 0] + recv_m[j, 0]


def chunk_call(kernel, amp, a_first, split, v_first, count, blocks, recvs, outs, name):
    rows, depth = amp.shape[3:]
    hi, lo = split
    cols = hi.shape[2]

    def a_spec(k):
        return pl.BlockSpec(
            (1, 1, 1, rows, depth), lambda g, b: (b[k] // 2, a_first + g, b[k] % 2, 0, 0)
        )

    v_spec = pl.BlockSpec((1, depth, cols), lambda g, b: (v_first + g, 0, 0))

    def io_spec(lead):
        if lead == 0:
            return pl.BlockSpec((1, rows, cols), lambda g, b: (g, 0, 0))
        return pl.BlockSpec((lead, 1, rows, cols), lambda g, b: (0, g, 0, 0))

    def io_shape(lead):
        shape = (count, rows, cols) if lead == 0 else (lead, count, rows, cols)
        return jax.ShapeDtypeStruct(shape, jnp.float32)

    recv_bytes = sum(r.size * 4 for r in recvs)
    return pl.pallas_call(
        kernel,
        grid_spec=pltpu.PrefetchScalarGridSpec(
            num_scalar_prefetch=1,
            grid=(count,),
            in_specs=[a_spec(k) for k in range(SIDE)]
            + [v_spec, v_spec]
            + [io_spec(r.shape[0]) for r in recvs],
            out_specs=[io_spec(lead) for lead in outs],
        ),
        out_shape=[io_shape(lead) for lead in outs],
        compiler_params=pltpu.CompilerParams(vmem_limit_bytes=VMEM),
        cost_estimate=pl.CostEstimate(
            flops=3 * 2 * SIDE * rows * depth * cols * count,
            bytes_accessed=count * (depth * cols * 4 + SIDE * rows * (depth + cols) * 4) + recv_bytes,
            transcendentals=0,
        ),
        name=name,
    )(blocks, amp, amp, amp, amp, hi, lo, *recvs)


def finish_kernel(counts, sizes, origin, *refs):
    out = refs[-1]
    rows, _, cols = out.shape
    row = origin[0] + lax.broadcasted_iota(jnp.int32, (rows, cols), 0)
    at = 0
    for first, count in counts:
        parts = refs[at : at + 4]
        at += 4
        for g in range(count):
            total = (parts[0][g] + parts[1][g]) + (parts[2][g] + parts[3][g])
            out[:, first + g, :] = jnp.where(row < sizes[first + g], total, 0.0)


def finish(groups, row_sizes, origin, shape):
    counts = [(first, parts[0].shape[0]) for first, parts in groups]
    flat = [p for _, parts in groups for p in parts]
    vmem = pl.BlockSpec(memory_space=pltpu.VMEM)
    smem = pl.BlockSpec(memory_space=pltpu.SMEM)
    return pl.pallas_call(
        functools.partial(finish_kernel, counts),
        in_specs=[smem, smem] + [vmem] * len(flat),
        out_specs=vmem,
        out_shape=jax.ShapeDtypeStruct(shape, jnp.float32),
        compiler_params=pltpu.CompilerParams(vmem_limit_bytes=VMEM),
        name="finish",
    )(row_sizes, origin, *flat)


X_HOPS = {d: hops(SIDE, d) for d in (1, 2, -1)}
Y_HOPS = {d: hops(1, d) for d in (1, 2, -1)}


def local(amplitudes, ovov, row_sizes, pair_sizes):
    ob = lax.axis_index("ob")
    vb = lax.axis_index("vb")
    x, y = ob // SIDE, ob % SIDE
    local_rows, irreps, pairs = amplitudes.shape
    obs = lax.axis_size("ob")
    depth, cols = ovov.shape[1:]
    out_rows = local_rows * lax.axis_size("vb")

    origin = jnp.stack([ob * depth, vb * cols]).astype(jnp.int32)
    split = split_ovov(ovov, pair_sizes, origin)

    mine = jnp.transpose(amplitudes.reshape(local_rows, irreps, obs, depth), (2, 0, 1, 3))
    mine = lax.all_to_all(
        mine.reshape(obs, local_rows * irreps, depth), "ob", split_axis=0, concat_axis=0, tiled=True
    )
    mine = jnp.transpose(mine.reshape(obs * local_rows, irreps, depth), (1, 0, 2))

    def dest(axis, delta):
        k = jnp.arange(SIDE, dtype=jnp.int32)
        if axis == "x":
            return ((x + delta) % SIDE) * SIDE + k
        return k * SIDE + (y + delta) % SIDE

    def own(axis):
        other = y if axis == "x" else x
        k = (other + jnp.arange(SIDE, dtype=jnp.int32)) % SIDE
        b = x * SIDE + k if axis == "x" else k * SIDE + y
        return jnp.concatenate([b, k]).astype(jnp.int32)

    chains = []
    for first, size in ((0, 4), (4, 4)):
        gathered = lax.all_gather(mine[first : first + size], "vb", axis=0)
        gathered = gathered.reshape(-1, size, 2, out_rows, depth)
        half = size // 2
        for axis, at in (("x", 0), ("y", half)):
            chains.append((axis, gathered, at, first + at, half))

    groups = []
    for axis, amp, a_first, v_first, count in chains:
        here = X_HOPS if axis == "x" else Y_HOPS
        there = Y_HOPS if axis == "x" else X_HOPS
        call = functools.partial(
            lambda kernel, blocks, recvs, outs, name, a=amp, f=a_first, v=v_first, c=count: chunk_call(
                kernel, a, f, split, v, c, blocks, recvs, outs, name
            )
        )
        far_a, far_b = call(first_kernel, dest(axis, 2), [], [2, 2], f"{axis}_far")
        from_left = lax.ppermute(far_a, "ob", here[1])
        from_right = lax.ppermute(far_b, "ob", here[-1])
        (up,) = call(functools.partial(second_kernel, 0), dest(axis, 1), [from_left], [4], f"{axis}_up")
        (down,) = call(functools.partial(second_kernel, 1), dest(axis, -1), [from_right], [4], f"{axis}_down")
        from_left = lax.ppermute(up, "ob", here[1])
        from_right = lax.ppermute(down, "ob", here[-1])
        parts = call(third_kernel, own(axis), [from_left, from_right], [0, 0, 0, 0], f"{axis}_own")
        groups.append(
            (
                v_first,
                [
                    parts[0],
                    lax.ppermute(parts[1], "ob", there[1]),
                    lax.ppermute(parts[2], "ob", there[2]),
                    lax.ppermute(parts[3], "ob", there[-1]),
                ],
            )
        )
    origin = jnp.stack([ob * out_rows, vb * cols]).astype(jnp.int32)
    return finish(groups, row_sizes, origin, (out_rows, irreps, cols))


def solution(mesh):
    placed = (P(("vb", "ob"), None, None), P(None, "ob", "vb"), P(), P())
    return jax.shard_map(
        local, mesh=mesh, in_specs=placed, out_specs=P("ob", None, "vb"), check_vma=False
    )
```

```python
import functools

import jax
import jax.numpy as jnp
import numpy as np
from jax import lax
from jax.experimental import pallas as pl
from jax.experimental.pallas import tpu as pltpu
from jax.sharding import PartitionSpec as P

SIDE = 4
VMEM = 48 * 1024 * 1024
SOURCES = [(dz, dc) for dz in (0, -1, 1, 2) for dc in (0, 1)]


def hops(count, stride, delta):
    pairs = []
    for i in range(count):
        d = (i // stride) % SIDE
        pairs.append((i, i + ((d + delta) % SIDE - d) * stride))
    return pairs


X_HOPS = {d: hops(16, SIDE, d) for d in (1, 2, -1)}
Y_HOPS = {d: hops(16, 1, d) for d in (1, 2, -1)}
Z_HOPS = {d: hops(8, 2, d) for d in (1, 2, -1)}
SWAP = [(i, i ^ 1) for i in range(8)]


def places(axis):
    table = np.zeros((8, 16, 16), np.int32)
    for vb in range(8):
        for ob in range(16):
            x, y = divmod(ob, SIDE)
            for a, (dz, dc) in enumerate(SOURCES):
                source = 2 * ((vb // 2 + dz) % SIDE) + ((vb % 2) ^ dc)
                for h in range(2):
                    to_x, to_y = divmod(2 * source + h, SIDE)
                    rel_x, rel_y = (to_x - x) % SIDE, (to_y - y) % SIDE
                    first, second = (rel_x, rel_y) if axis == "x" else (rel_y, rel_x)
                    table[vb, ob, 2 * a + h] = SIDE * first + second
    return table


PLACES = np.concatenate([places("x"), places("y")], axis=2)


def product_kernel(v_first, place_at, place, sizes, origin, *refs):
    pieces, (v_ref, send_p, send_m, up, down, own, a_all, v_all) = refs[:8], refs[8:]
    rows = send_p.shape[2]
    depth = v_ref.shape[1]
    for a, piece in enumerate(pieces):
        for h in range(2):
            block = piece[0, h * rows : (h + 1) * rows]
            hi = block.astype(jnp.bfloat16)
            lo = (block - hi.astype(jnp.float32)).astype(jnp.bfloat16)
            at = pl.ds(pl.multiple_of(place[place_at + 2 * a + h] * rows, rows), rows)
            a_all[at, 0:depth] = hi
            a_all[at, depth : 2 * depth] = lo
            a_all[at, 2 * depth : 3 * depth] = hi
    size = sizes[v_first + pl.program_id(0)]
    shape = v_ref.shape[1:]
    p = origin[0] + lax.broadcasted_iota(jnp.int32, shape, 0)
    q = origin[1] + lax.broadcasted_iota(jnp.int32, shape, 1)
    v = jnp.where((p < size) & (q < size), v_ref[0], 0.0)
    hi = v.astype(jnp.bfloat16)
    v_all[0:depth] = hi
    v_all[depth : 2 * depth] = hi
    v_all[2 * depth : 3 * depth] = (v - hi.astype(jnp.float32)).astype(jnp.bfloat16)

    def chunk(k):
        acc = jnp.dot(
            a_all[SIDE * rows * k : SIDE * rows * (k + 1)], v_all[...], preferred_element_type=jnp.float32
        )
        return [acc[rows * s : rows * (s + 1)] for s in range(SIDE)]

    far = chunk(2)
    send_p[0, 0], send_p[1, 0], send_m[0, 0], send_m[1, 0] = far
    up[0, 0], up[1, 0], send_p[2, 0], send_p[3, 0] = chunk(1)
    send_m[2, 0], send_m[3, 0], down[0, 0], down[1, 0] = chunk(3)
    own[0, 0], own[1, 0], own[2, 0], own[3, 0] = chunk(0)


def product(pieces, a_first, ovov, v_first, count, place, place_at, sizes, origin, name):
    rows2, depth = pieces[0].shape[1:]
    rows = rows2 // 2
    cols = ovov.shape[2]
    leads = (4, 4, 2, 2, 4)
    total = 16 * rows
    return pl.pallas_call(
        functools.partial(product_kernel, v_first, place_at),
        grid_spec=pltpu.PrefetchScalarGridSpec(
            num_scalar_prefetch=3,
            grid=(count,),
            in_specs=[pl.BlockSpec((1, rows2, depth), lambda g, *_: (a_first + g, 0, 0))] * 8
            + [pl.BlockSpec((1, depth, cols), lambda g, *_: (v_first + g, 0, 0))],
            out_specs=[pl.BlockSpec((n, 1, rows, cols), lambda g, *_: (0, g, 0, 0)) for n in leads],
            scratch_shapes=[
                pltpu.VMEM((total, 3 * depth), jnp.bfloat16),
                pltpu.VMEM((3 * depth, cols), jnp.bfloat16),
            ],
        ),
        out_shape=[jax.ShapeDtypeStruct((n, count, rows, cols), jnp.float32) for n in leads],
        compiler_params=pltpu.CompilerParams(vmem_limit_bytes=VMEM),
        cost_estimate=pl.CostEstimate(
            flops=6 * total * depth * cols * count,
            bytes_accessed=4 * count * (depth * cols + total * (depth + cols)),
            transcendentals=0,
        ),
        name=name,
    )(place, sizes, origin, *pieces, ovov)


def add_kernel(up, down, recv_p, recv_m, out_p, out_m):
    out_p[...] = up[...] + recv_p[...]
    out_m[...] = down[...] + recv_m[...]


def add_far(up, down, recv_p, recv_m, name):
    lead, count, rows, cols = up.shape
    spec = pl.BlockSpec((lead, 1, rows, cols), lambda g: (0, g, 0, 0))
    return pl.pallas_call(
        add_kernel,
        grid=(count,),
        in_specs=[spec] * 4,
        out_specs=[spec] * 2,
        out_shape=[jax.ShapeDtypeStruct(up.shape, jnp.float32)] * 2,
        compiler_params=pltpu.CompilerParams(vmem_limit_bytes=VMEM),
        cost_estimate=pl.CostEstimate(flops=2 * up.size, bytes_accessed=24 * up.size, transcendentals=0),
        name=name,
    )(up, down, recv_p, recv_m)


def own_kernel(counts, *refs):
    ins, outs = refs[:-4], refs[-4:]
    at = 0
    for i, count in enumerate(counts):
        own, p1, m1, p2, m2 = ins[5 * i : 5 * i + 5]
        for g in range(count):
            outs[0][at + g] = own[0, g] + (p2[0, g] + m1[2, g])
            outs[1][at + g] = own[1, g] + (p2[1, g] + m1[3, g])
            outs[2][at + g] = own[2, g] + (m2[0, g] + p1[2, g])
            outs[3][at + g] = own[3, g] + (m2[1, g] + p1[3, g])
        at += count


def add_own(groups, name):
    counts = [group[0].shape[1] for group in groups]
    rows, cols = groups[0][0].shape[2:]
    flat = [r for group in groups for r in group]
    vmem = pl.BlockSpec(memory_space=pltpu.VMEM)
    shape = jax.ShapeDtypeStruct((sum(counts), rows, cols), jnp.float32)
    return pl.pallas_call(
        functools.partial(own_kernel, counts),
        in_specs=[vmem] * len(flat),
        out_specs=[vmem] * 4,
        out_shape=[shape] * 4,
        compiler_params=pltpu.CompilerParams(vmem_limit_bytes=VMEM),
        cost_estimate=pl.CostEstimate(
            flops=2 * 4 * shape.size, bytes_accessed=4 * (4 * shape.size + sum(r.size for r in flat)), transcendentals=0
        ),
        name=name,
    )(*flat)


def finish_kernel(order, sizes, origin, *refs):
    out = refs[-1]
    rows, _, cols = out.shape
    row = origin[0] + lax.broadcasted_iota(jnp.int32, (rows, cols), 0)
    for i, irreps in enumerate(order):
        parts = refs[4 * i : 4 * i + 4]
        for at, g in enumerate(irreps):
            total = (parts[0][at] + parts[1][at]) + (parts[2][at] + parts[3][at])
            out[:, g, :] = jnp.where(row < sizes[g], total, 0.0)


def finish(order, parts, row_sizes, origin, shape):
    flat = [p for four in parts for p in four]
    vmem = pl.BlockSpec(memory_space=pltpu.VMEM)
    smem = pl.BlockSpec(memory_space=pltpu.SMEM)
    return pl.pallas_call(
        functools.partial(finish_kernel, order),
        in_specs=[smem, smem] + [vmem] * len(flat),
        out_specs=vmem,
        out_shape=jax.ShapeDtypeStruct(shape, jnp.float32),
        compiler_params=pltpu.CompilerParams(vmem_limit_bytes=VMEM),
        name="finish",
    )(row_sizes, origin, *flat)


GROUPS = ((0, 2, 2), (4, 2, 2))


def local(amplitudes, ovov, row_sizes, pair_sizes):
    ob = lax.axis_index("ob")
    vb = lax.axis_index("vb")
    local_rows, irreps, pairs = amplitudes.shape
    obs = lax.axis_size("ob")
    depth, cols = ovov.shape[1:]
    out_rows = local_rows * lax.axis_size("vb")
    place = lax.dynamic_slice(jnp.asarray(PLACES), (vb, ob, 0), (1, 1, 32)).reshape(32)

    origin = jnp.stack([ob * depth, vb * cols]).astype(jnp.int32)

    mine = jnp.transpose(amplitudes.reshape(local_rows, irreps, obs, depth), (2, 0, 1, 3))
    mine = lax.all_to_all(
        mine.reshape(obs, local_rows * irreps, depth), "ob", split_axis=0, concat_axis=0, tiled=True
    )
    mine = jnp.transpose(mine.reshape(obs * local_rows, irreps, depth), (1, 0, 2))

    own = {"x": [], "y": []}
    order = {"x": [], "y": []}
    for i, (first, nx, ny) in enumerate(GROUPS):
        held = mine[first : first + nx + ny]
        pieces = []
        for dz in (0, -1, 1, 2):
            moved = lax.ppermute(held, "vb", Z_HOPS[-dz if dz != 2 else 2]) if dz else held
            pieces += [moved, lax.ppermute(moved, "vb", SWAP)]
        for axis, at, count in (("x", 0, nx), ("y", nx, ny)):
            here = X_HOPS if axis == "x" else Y_HOPS
            send_p, send_m, up, down, mid = product(
                pieces, at, ovov, first + at, count, place, 16 * (axis == "y"), pair_sizes, origin, f"{axis}_product"
            )
            p1 = lax.ppermute(send_p, "ob", here[1])
            m1 = lax.ppermute(send_m, "ob", here[-1])
            send_p, send_m = add_far(up, down, p1, m1, f"{axis}_add")
            p2 = lax.ppermute(send_p, "ob", here[1])
            m2 = lax.ppermute(send_m, "ob", here[-1])
            own[axis].append((mid, p1, m1, p2, m2))
            order[axis] += range(first + at, first + at + count)

    parts = []
    for axis in ("x", "y"):
        there = Y_HOPS if axis == "x" else X_HOPS
        four = add_own(own[axis], f"{axis}_own")
        parts.append([four[0]] + [lax.ppermute(four[k], "ob", there[d]) for k, d in ((1, 1), (2, 2), (3, -1))])
    origin = jnp.stack([ob * out_rows, vb * cols]).astype(jnp.int32)
    return finish([order["x"], order["y"]], parts, row_sizes, origin, (out_rows, irreps, cols))


def solution(mesh):
    placed = (P(("vb", "ob"), None, None), P(None, "ob", "vb"), P(), P())
    return jax.shard_map(
        local, mesh=mesh, in_specs=placed, out_specs=P("ob", None, "vb"), check_vma=False
    )
```

```python
import functools

import jax
import jax.numpy as jnp
import numpy as np
from jax import lax
from jax.experimental import pallas as pl
from jax.experimental.pallas import tpu as pltpu
from jax.sharding import PartitionSpec as P

SIDE = 4
VMEM = 20 * 1024 * 1024
LIGHT = pl.CostEstimate(flops=0, bytes_accessed=0, transcendentals=0)
SOURCES = [(dz, dc) for dz in (0, -1, 1, 2) for dc in (0, 1)]


def hops(count, stride, delta):
    pairs = []
    for i in range(count):
        d = (i // stride) % SIDE
        pairs.append((i, i + ((d + delta) % SIDE - d) * stride))
    return pairs


Z_HOPS = {d: hops(8, 2, d) for d in (1, 2, -1)}
SWAP = [(i, i ^ 1) for i in range(8)]


def apart(count, stride, delta, cores):
    up, down = hops(count, stride, delta), hops(count, stride, -delta)
    return [(down if cores(i) else up)[i] for i in range(count)]


Z_APART = [apart(8, 2, d, lambda i: i % 2) for d in (1, -1)]
X_HOPS = {d: apart(128, SIDE, d, lambda i: i // 16 % 2) for d in (1, 2, -1)}
Y_HOPS = {d: apart(128, 1, d, lambda i: i // 16 % 2) for d in (1, 2, -1)}
BOTH = ("vb", "ob")


def places(axis):
    table = np.zeros((8, 16, 16), np.int32)
    for vb in range(8):
        for ob in range(16):
            x, y = divmod(ob, SIDE)
            for a, (dz, dc) in enumerate(SOURCES):
                core = (vb % 2) ^ dc
                source = 2 * ((vb // 2 + (-dz if core else dz)) % SIDE) + core
                for h in range(2):
                    to_x, to_y = divmod(2 * source + h, SIDE)
                    sign = -1 if vb % 2 else 1
                    rel_x, rel_y = sign * (to_x - x) % SIDE, sign * (to_y - y) % SIDE
                    first, second = (rel_x, rel_y) if axis == "x" else (rel_y, rel_x)
                    table[vb, ob, 2 * a + h] = SIDE * first + second
    return table


PLACES = np.concatenate([places("x"), places("y")], axis=2)


def product_kernel(v_first, place_at, place, sizes, origin, *refs):
    pieces, (v_ref, send_p, send_m, up, down, own, a_all, v_all) = refs[:8], refs[8:]
    rows = send_p.shape[1]
    depth = v_ref.shape[1]
    for a, piece in enumerate(pieces):
        for h in range(2):
            block = piece[0, h * rows : (h + 1) * rows]
            hi = block.astype(jnp.bfloat16)
            lo = (block - hi.astype(jnp.float32)).astype(jnp.bfloat16)
            at = pl.ds(pl.multiple_of(place[place_at + 2 * a + h] * rows, rows), rows)
            a_all[at, 0:depth] = hi
            a_all[at, depth : 2 * depth] = lo
            a_all[at, 2 * depth : 3 * depth] = hi
    size = sizes[v_first + pl.program_id(0)]
    shape = v_ref.shape[1:]
    p = origin[0] + lax.broadcasted_iota(jnp.int32, shape, 0)
    q = origin[1] + lax.broadcasted_iota(jnp.int32, shape, 1)
    v = jnp.where((p < size) & (q < size), v_ref[0], 0.0)
    hi = v.astype(jnp.bfloat16)
    v_all[0:depth] = hi
    v_all[depth : 2 * depth] = hi
    v_all[2 * depth : 3 * depth] = (v - hi.astype(jnp.float32)).astype(jnp.bfloat16)

    def chunk(k):
        acc = jnp.dot(
            a_all[SIDE * rows * k : SIDE * rows * (k + 1)], v_all[...], preferred_element_type=jnp.float32
        )
        return [acc[rows * s : rows * (s + 1)] for s in range(SIDE)]

    far = chunk(2)
    send_p[0], send_p[1], send_m[0], send_m[1] = far
    up[0], up[1], send_p[2], send_p[3] = chunk(1)
    send_m[2], send_m[3], down[0], down[1] = chunk(3)
    own[0], own[1], own[2], own[3] = chunk(0)


def product(pieces, skip, ovov, v_first, count, place, place_at, sizes, origin, name):
    rows2, depth = pieces[0][0].shape[1:]
    rows = rows2 // 2
    cols = ovov.shape[2]
    leads = (4, 4, 2, 2, 4)
    total = 16 * rows
    return pl.pallas_call(
        functools.partial(product_kernel, v_first, place_at),
        grid_spec=pltpu.PrefetchScalarGridSpec(
            num_scalar_prefetch=3,
            grid=(count,),
            in_specs=[
                pl.BlockSpec((1, rows2, depth), lambda g, *_, at=at: (at + skip + g, 0, 0)) for _, at in pieces
            ]
            + [pl.BlockSpec((1, depth, cols), lambda g, *_: (v_first + g, 0, 0))],
            out_specs=[pl.BlockSpec((n, rows, cols), lambda g, *_: (g, 0, 0)) for n in leads],
            scratch_shapes=[
                pltpu.VMEM((total, 3 * depth), jnp.bfloat16),
                pltpu.VMEM((3 * depth, cols), jnp.bfloat16),
            ],
        ),
        out_shape=[
            jax.ShapeDtypeStruct((n * count, rows, cols), jnp.float32) for n in leads
        ],
        compiler_params=pltpu.CompilerParams(vmem_limit_bytes=VMEM),
        cost_estimate=LIGHT,
        name=name,
    )(place, sizes, origin, *[piece for piece, _ in pieces], ovov)


def add_kernel(mid, recv, out):
    out[...] = mid[...] + recv[...]


def add_far(mid, recv, name):
    lead, rows, cols = mid.shape
    spec = pl.BlockSpec((2, rows, cols), lambda g: (g, 0, 0))
    return pl.pallas_call(
        add_kernel,
        grid=(lead // 2,),
        in_specs=[spec, pl.BlockSpec((2, rows, cols), lambda g: (2 * g, 0, 0))],
        out_specs=spec,
        out_shape=jax.ShapeDtypeStruct(mid.shape, jnp.float32),
        compiler_params=pltpu.CompilerParams(vmem_limit_bytes=VMEM),
        cost_estimate=LIGHT,
        name=name,
    )(mid, recv)


def own_kernel(counts, *refs):
    ins, outs = refs[:-4], refs[-4:]
    at = 0
    for i, count in enumerate(counts):
        own, p1, m1, p2, m2 = ins[5 * i : 5 * i + 5]
        for g in range(count):
            a, b = 4 * g, 2 * g
            outs[0][at + g] = own[a] + (p2[b] + m1[a + 2])
            outs[1][at + g] = own[a + 1] + (p2[b + 1] + m1[a + 3])
            outs[2][at + g] = own[a + 2] + (m2[b] + p1[a + 2])
            outs[3][at + g] = own[a + 3] + (m2[b + 1] + p1[a + 3])
        at += count


def add_own(groups, name):
    counts = [group[0].shape[0] // 4 for group in groups]
    rows, cols = groups[0][0].shape[1:]
    flat = [r for group in groups for r in group]
    vmem = pl.BlockSpec(memory_space=pltpu.VMEM)
    return pl.pallas_call(
        functools.partial(own_kernel, counts),
        in_specs=[vmem] * len(flat),
        out_specs=[vmem] * 4,
        out_shape=[jax.ShapeDtypeStruct((sum(counts), rows, cols), jnp.float32)] * 4,
        compiler_params=pltpu.CompilerParams(vmem_limit_bytes=VMEM),
        cost_estimate=LIGHT,
        name=name,
    )(*flat)


def finish_kernel(order, sizes, origin, *refs):
    out = refs[-1]
    rows, _, cols = out.shape
    row = origin[0] + lax.broadcasted_iota(jnp.int32, (rows, cols), 0)
    for i, irreps in enumerate(order):
        parts = refs[4 * i : 4 * i + 4]
        for at, g in enumerate(irreps):
            total = (parts[0][at] + parts[1][at]) + (parts[2][at] + parts[3][at])
            out[:, g, :] = jnp.where(row < sizes[g], total, 0.0)


def finish(order, parts, row_sizes, origin, shape):
    flat = [p for four in parts for p in four]
    vmem = pl.BlockSpec(memory_space=pltpu.VMEM)
    smem = pl.BlockSpec(memory_space=pltpu.SMEM)
    return pl.pallas_call(
        functools.partial(finish_kernel, order),
        in_specs=[smem, smem] + [vmem] * len(flat),
        out_specs=vmem,
        out_shape=jax.ShapeDtypeStruct(shape, jnp.float32),
        compiler_params=pltpu.CompilerParams(vmem_limit_bytes=VMEM),
        cost_estimate=LIGHT,
        name="finish",
    )(row_sizes, origin, *flat)


GROUPS = ((0, 1, 1), (2, 1, 1), (4, 2, 2))


def tie_kernel(*refs):
    pass


def tie(values, after):
    if not after:
        return list(values)
    anywhere = pl.BlockSpec(memory_space=pl.ANY)
    return pl.pallas_call(
        tie_kernel,
        in_specs=[anywhere] * (len(values) + len(after)),
        out_specs=[anywhere] * len(values),
        out_shape=[jax.ShapeDtypeStruct(v.shape, v.dtype) for v in values],
        input_output_aliases={i: i for i in range(len(values))},
        cost_estimate=LIGHT,
        name="tie",
    )(*values, *after)


def local(amplitudes, ovov, row_sizes, pair_sizes):
    ob = lax.axis_index("ob")
    vb = lax.axis_index("vb")
    local_rows, irreps, pairs = amplitudes.shape
    obs = lax.axis_size("ob")
    depth, cols = ovov.shape[1:]
    out_rows = local_rows * lax.axis_size("vb")
    place = lax.dynamic_slice(jnp.asarray(PLACES), (vb, ob, 0), (1, 1, 32)).reshape(32)

    origin = jnp.stack([ob * depth, vb * cols]).astype(jnp.int32)

    mine = jnp.transpose(amplitudes.reshape(local_rows, irreps, obs, depth), (2, 0, 1, 3))
    mine = lax.all_to_all(
        mine.reshape(obs, local_rows * irreps, depth), "ob", split_axis=0, concat_axis=0, tiled=True
    )
    mine = jnp.transpose(mine.reshape(obs * local_rows, irreps, depth), (1, 0, 2))

    mine_swapped = lax.ppermute(mine, "vb", SWAP)
    axes = (("x", X_HOPS, Y_HOPS, 0), ("y", Y_HOPS, X_HOPS, 16))
    order = {axis: [] for axis, *_ in axes}
    sums = {axis: [] for axis, *_ in axes}
    parts_of = [mine[first : first + nx + ny] for first, nx, ny in GROUPS]
    landed, sent, got, newer, older = [], [], [], [], []

    def gather(held):
        return [lax.ppermute(held, "vb", pairs) for pairs in (*Z_APART, Z_HOPS[2])]

    landed = gather(parts_of[0])
    for t, (first, nx, ny) in enumerate(GROUPS):
        if t + 1 < len(GROUPS):
            following, *landed = tie([parts_of[t + 1], *landed], sent) if sent else (parts_of[t + 1], *landed)
            (following,) = tie([following], landed)
        else:
            landed = tie(landed, sent + got)
        pieces = [(mine, first), (mine_swapped, first)]
        (swapped,) = tie([lax.ppermute(jnp.concatenate(landed), "vb", SWAP)], older if t > 1 else got)
        for i, moved in enumerate(landed):
            pieces += [(moved, 0), (swapped, i * (nx + ny))]
        if t + 1 < len(GROUPS):
            landed = gather(following)
        sent, got, older = [], [], newer
        newer = []
        for axis, here, there, place_at in axes:
            skip, count = (0, nx) if axis == "x" else (nx, ny)
            order[axis] += range(first + skip, first + skip + count)
            send_p, send_m, up, down, mid = product(
                pieces, skip, ovov, first + skip, count, place, place_at, pair_sizes, origin, f"{axis}_product"
            )
            sent.append(send_p)
            p1 = lax.ppermute(send_p, BOTH, here[1])
            m1 = lax.ppermute(send_m, BOTH, here[-1])
            got += [p1, m1]
            p2 = lax.ppermute(add_far(up, p1, f"{axis}_add"), BOTH, here[1])
            m2 = lax.ppermute(add_far(down, m1, f"{axis}_add"), BOTH, here[-1])
            newer += [p2, m2]
            sums[axis].append((mid, p1, m1, p2, m2))

    parts = []
    for axis, here, there, _ in axes:
        four = add_own(sums[axis], f"{axis}_own")
        parts.append([four[0]] + [lax.ppermute(four[k], BOTH, there[d]) for k, d in ((1, 1), (2, 2), (3, -1))])
    origin = jnp.stack([ob * out_rows, vb * cols]).astype(jnp.int32)
    return finish([order[axis] for axis, *_ in axes], parts, row_sizes, origin, (out_rows, irreps, cols))


def solution(mesh):
    placed = (P(("vb", "ob"), None, None), P(None, "ob", "vb"), P(), P())
    return jax.shard_map(
        local, mesh=mesh, in_specs=placed, out_specs=P("ob", None, "vb"), check_vma=False
    )
```

```python
import functools

import jax
import jax.numpy as jnp
import numpy as np
from jax import lax
from jax.experimental import pallas as pl
from jax.experimental.pallas import tpu as pltpu
from jax.sharding import PartitionSpec as P

SIDE = 4
VMEM = 63 * 1024 * 1024
LIGHT = pl.CostEstimate(flops=0, bytes_accessed=0, transcendentals=0)
def hops(count, stride, delta):
    pairs = []
    for i in range(count):
        d = (i // stride) % SIDE
        pairs.append((i, i + ((d + delta) % SIDE - d) * stride))
    return pairs


def apart(count, stride, delta, cores):
    up, down = hops(count, stride, delta), hops(count, stride, -delta)
    return [(down if cores(i) else up)[i] for i in range(count)]


X_HOPS = {d: apart(128, SIDE, d, lambda i: i // 16 % 2) for d in (1, 2, -1)}
Y_HOPS = {d: apart(128, 1, d, lambda i: i // 16 % 2) for d in (1, 2, -1)}
BOTH = ("vb", "ob")


def places(axis):
    table = np.zeros((8, 16, 16), np.int32)
    for vb in range(8):
        for ob in range(16):
            x, y = divmod(ob, SIDE)
            sign = -1 if vb % 2 else 1
            for block in range(16):
                to_x, to_y = divmod(block, SIDE)
                rel_x, rel_y = sign * (to_x - x) % SIDE, sign * (to_y - y) % SIDE
                first, second = (rel_x, rel_y) if axis == "x" else (rel_y, rel_x)
                table[vb, ob, block] = SIDE * first + second
    return table


PLACES = np.concatenate([places("x"), places("y")], axis=2)


def product_kernel(v_first, place_at, place, sizes, origin, *refs):
    pieces, v_ref, (send_p, send_m, up, down, own, a_all, v_all) = refs[:8], refs[8], refs[-7:]
    rows = send_p.shape[1]
    depth = v_ref.shape[1]
    for a, piece in enumerate(pieces):
        for h in range(2):
            block = piece[0, 0, h * rows : (h + 1) * rows]
            hi = block.astype(jnp.bfloat16)
            lo = (block - hi.astype(jnp.float32)).astype(jnp.bfloat16)
            at = pl.ds(pl.multiple_of(place[place_at + 2 * a + h] * rows, rows), rows)
            a_all[at, 0:depth] = hi
            a_all[at, depth : 2 * depth] = lo
            a_all[at, 2 * depth : 3 * depth] = hi
    size = sizes[v_first + pl.program_id(0)]
    shape = v_ref.shape[1:]
    p = origin[0] + lax.broadcasted_iota(jnp.int32, shape, 0)
    q = origin[1] + lax.broadcasted_iota(jnp.int32, shape, 1)
    v = jnp.where((p < size) & (q < size), v_ref[0], 0.0)
    hi = v.astype(jnp.bfloat16)
    v_all[0:depth] = hi
    v_all[depth : 2 * depth] = hi
    v_all[2 * depth : 3 * depth] = (v - hi.astype(jnp.float32)).astype(jnp.bfloat16)

    def chunk(k):
        acc = jnp.dot(
            a_all[SIDE * rows * k : SIDE * rows * (k + 1)], v_all[...], preferred_element_type=jnp.float32
        )
        return [acc[rows * s : rows * (s + 1)] for s in range(SIDE)]

    far = chunk(2)
    send_p[0], send_p[1], send_m[0], send_m[1] = far
    up[0], up[1], send_p[2], send_p[3] = chunk(1)
    send_m[2], send_m[3], down[0], down[1] = chunk(3)
    own[0], own[1], own[2], own[3] = chunk(0)


def product(amp, skip, ovov, v_first, count, place, place_at, sizes, origin, after, name):
    sources, _, rows2, depth = amp.shape
    rows = rows2 // 2
    cols = ovov.shape[2]
    leads = (4, 4, 2, 2, 4)
    total = 16 * rows
    return pl.pallas_call(
        functools.partial(product_kernel, v_first, place_at),
        grid_spec=pltpu.PrefetchScalarGridSpec(
            num_scalar_prefetch=3,
            grid=(count,),
            in_specs=[
                pl.BlockSpec((1, 1, rows2, depth), lambda g, *_, s=s: (s, skip + g, 0, 0)) for s in range(sources)
            ]
            + [pl.BlockSpec((1, depth, cols), lambda g, *_: (v_first + g, 0, 0))]
            + [pl.BlockSpec(memory_space=pl.ANY)] * len(after),
            out_specs=[pl.BlockSpec((n, rows, cols), lambda g, *_: (g, 0, 0)) for n in leads],
            scratch_shapes=[
                pltpu.VMEM((total, 3 * depth), jnp.bfloat16),
                pltpu.VMEM((3 * depth, cols), jnp.bfloat16),
            ],
        ),
        out_shape=[
            jax.ShapeDtypeStruct((n * count, rows, cols), jnp.float32) for n in leads
        ],
        compiler_params=pltpu.CompilerParams(vmem_limit_bytes=VMEM),
        cost_estimate=LIGHT,
        name=name,
    )(place, sizes, origin, *[amp] * sources, ovov, *after)


def add_kernel(mid, recv, out):
    out[...] = mid[...] + recv[...]


def add_far(mid, recv, name):
    lead, rows, cols = mid.shape
    spec = pl.BlockSpec((2, rows, cols), lambda g: (g, 0, 0))
    return pl.pallas_call(
        add_kernel,
        grid=(lead // 2,),
        in_specs=[spec, pl.BlockSpec((2, rows, cols), lambda g: (2 * g, 0, 0))],
        out_specs=spec,
        out_shape=jax.ShapeDtypeStruct(mid.shape, jnp.float32),
        compiler_params=pltpu.CompilerParams(vmem_limit_bytes=VMEM),
        cost_estimate=LIGHT,
        name=name,
    )(mid, recv)


def own_kernel(own, p1, m1, p2, m2, *refs):
    outs = refs[-4:]
    outs[0][0] = own[0] + (p2[0] + m1[0])
    outs[1][0] = own[1] + (p2[1] + m1[1])
    outs[2][0] = own[2] + (m2[0] + p1[0])
    outs[3][0] = own[3] + (m2[1] + p1[1])


def add_own(own, p1, m1, p2, m2, at, total, into, name):
    rows, cols = own.shape[1:]
    half = pl.BlockSpec((2, rows, cols), lambda g: (2 * g + 1, 0, 0))
    last = pl.BlockSpec((2, rows, cols), lambda g: (g, 0, 0))
    return pl.pallas_call(
        own_kernel,
        grid=(own.shape[0] // 4,),
        in_specs=[pl.BlockSpec((4, rows, cols), lambda g: (g, 0, 0)), half, half, last, last]
        + [pl.BlockSpec(memory_space=pl.ANY)] * len(into),
        out_specs=[pl.BlockSpec((1, rows, cols), lambda g: (at + g, 0, 0))] * 4,
        out_shape=[jax.ShapeDtypeStruct((total, rows, cols), jnp.float32)] * 4,
        input_output_aliases={5 + i: i for i in range(len(into))},
        compiler_params=pltpu.CompilerParams(vmem_limit_bytes=VMEM),
        cost_estimate=LIGHT,
        name=name,
    )(own, p1, m1, p2, m2, *into)


def finish_kernel(order, sizes, origin, *refs):
    out = refs[-1]
    rows, _, cols = out.shape
    row = origin[0] + lax.broadcasted_iota(jnp.int32, (rows, cols), 0)
    for i, irreps in enumerate(order):
        parts = refs[4 * i : 4 * i + 4]
        for at, g in enumerate(irreps):
            total = (parts[0][at] + parts[1][at]) + (parts[2][at] + parts[3][at])
            out[:, g, :] = jnp.where(row < sizes[g], total, 0.0)


def finish(order, parts, row_sizes, origin, shape):
    rows, irreps, cols = shape
    width = 256
    flat = [p for four in parts for p in four]
    return pl.pallas_call(
        functools.partial(finish_kernel, order),
        grid_spec=pltpu.PrefetchScalarGridSpec(
            num_scalar_prefetch=2,
            grid=(cols // width,),
            in_specs=[pl.BlockSpec((p.shape[0], rows, width), lambda c, *_: (0, 0, c)) for p in flat],
            out_specs=pl.BlockSpec((rows, irreps, width), lambda c, *_: (0, 0, c)),
        ),
        out_shape=jax.ShapeDtypeStruct(shape, jnp.float32),
        compiler_params=pltpu.CompilerParams(vmem_limit_bytes=VMEM),
        cost_estimate=LIGHT,
        name="finish",
    )(row_sizes, origin, *flat)


GROUPS = ((0, 2, 2), (4, 2, 2))


def local(amplitudes, ovov, row_sizes, pair_sizes):
    ob = lax.axis_index("ob")
    vb = lax.axis_index("vb")
    local_rows, irreps, pairs = amplitudes.shape
    obs = lax.axis_size("ob")
    depth, cols = ovov.shape[1:]
    out_rows = local_rows * lax.axis_size("vb")
    place = lax.dynamic_slice(jnp.asarray(PLACES), (vb, ob, 0), (1, 1, 32)).reshape(32)

    origin = jnp.stack([ob * depth, vb * cols]).astype(jnp.int32)

    axes = (("x", X_HOPS, Y_HOPS, 0), ("y", Y_HOPS, X_HOPS, 16))
    order = {axis: [] for axis, *_ in axes}
    sums = {axis: [] for axis, *_ in axes}
    got = {}

    gathered = []
    for first, nx, ny in GROUPS:
        count = nx + ny
        mine = amplitudes[:, first : first + count].reshape(local_rows, count, obs, depth)
        mine = jnp.transpose(mine, (2, 0, 1, 3)).reshape(obs, local_rows * count, depth)
        mine = lax.all_to_all(mine, "ob", split_axis=0, concat_axis=0, tiled=True)
        mine = jnp.transpose(mine.reshape(obs * local_rows, count, depth), (1, 0, 2))
        gathered.append(lax.all_gather(mine, "vb", axis=0))

    for (first, nx, ny), amp in zip(GROUPS, gathered):
        for axis, here, there, place_at in axes:
            skip, count = (0, nx) if axis == "x" else (nx, ny)
            order[axis] += range(first + skip, first + skip + count)
            send_p, send_m, up, down, mid = product(
                amp, skip, ovov, first + skip, count, place, place_at, pair_sizes, origin, got.get(axis, []), f"{axis}_product"
            )
            p1 = lax.ppermute(send_p, BOTH, here[1])
            m1 = lax.ppermute(send_m, BOTH, here[-1])
            got[axis] = [p1, m1]
            p2 = lax.ppermute(add_far(up, p1, f"{axis}_add"), BOTH, here[1])
            m2 = lax.ppermute(add_far(down, m1, f"{axis}_add"), BOTH, here[-1])
            sums[axis].append((mid, p1, m1, p2, m2))

    parts = []
    for axis, here, there, _ in axes:
        four, at = [], 0
        for group in sums[axis]:
            four = add_own(*group, at, len(order[axis]), four, f"{axis}_own")
            at += group[0].shape[0] // 4
        parts.append([four[0]] + [lax.ppermute(four[k], BOTH, there[d]) for k, d in ((1, 1), (2, 2), (3, -1))])
    origin = jnp.stack([ob * out_rows, vb * cols]).astype(jnp.int32)
    return finish([order[axis] for axis, *_ in axes], parts, row_sizes, origin, (out_rows, irreps, cols))


def solution(mesh):
    placed = (P(("vb", "ob"), None, None), P(None, "ob", "vb"), P(), P())
    return jax.shard_map(
        local, mesh=mesh, in_specs=placed, out_specs=P("ob", None, "vb"), check_vma=False
    )
```

```python
import functools

import jax
import jax.numpy as jnp
import numpy as np
from jax import lax
from jax.experimental import pallas as pl
from jax.experimental.pallas import tpu as pltpu
from jax.sharding import PartitionSpec as P

SIDE = 4
VMEM = 63 * 1024 * 1024
WIDTH = 256
LIGHT = pl.CostEstimate(flops=0, bytes_accessed=0, transcendentals=0)
def hops(count, stride, delta):
    pairs = []
    for i in range(count):
        d = (i // stride) % SIDE
        pairs.append((i, i + ((d + delta) % SIDE - d) * stride))
    return pairs


def apart(count, stride, delta, cores):
    up, down = hops(count, stride, delta), hops(count, stride, -delta)
    return [(down if cores(i) else up)[i] for i in range(count)]


X_HOPS = {d: apart(128, SIDE, d, lambda i: i // 16 % 2) for d in (1, 2, -1)}
Y_HOPS = {d: apart(128, 1, d, lambda i: i // 16 % 2) for d in (1, 2, -1)}
BOTH = ("vb", "ob")


def places(axis):
    table = np.zeros((8, 16, 16), np.int32)
    for vb in range(8):
        for ob in range(16):
            x, y = divmod(ob, SIDE)
            sign = -1 if vb % 2 else 1
            for block in range(16):
                to_x, to_y = divmod(block, SIDE)
                rel_x, rel_y = sign * (to_x - x) % SIDE, sign * (to_y - y) % SIDE
                first, second = (rel_x, rel_y) if axis == "x" else (rel_y, rel_x)
                table[vb, ob, block] = SIDE * first + second
    return table


PLACES = np.concatenate([places("x"), places("y")], axis=2)


def product_kernel(v_first, place_at, place, sizes, origin, *refs):
    pieces, v_ref, (send_p, send_m, up, down, own, a_all, v_all) = refs[:8], refs[8], refs[-7:]
    rows = send_p.shape[1]
    depth, width = v_ref.shape[1:]

    @pl.when(pl.program_id(1) == 0)
    def _():
        for a, piece in enumerate(pieces):
            for h in range(2):
                block = piece[0, 0, h * rows : (h + 1) * rows]
                hi = block.astype(jnp.bfloat16)
                lo = (block - hi.astype(jnp.float32)).astype(jnp.bfloat16)
                at = pl.ds(pl.multiple_of(place[place_at + 2 * a + h] * rows, rows), rows)
                a_all[at, 0:depth] = hi
                a_all[at, depth : 2 * depth] = lo
                a_all[at, 2 * depth : 3 * depth] = hi

    size = sizes[v_first + pl.program_id(0)]
    p = origin[0] + lax.broadcasted_iota(jnp.int32, (depth, width), 0)
    q = origin[1] + pl.program_id(1) * width + lax.broadcasted_iota(jnp.int32, (depth, width), 1)
    v = jnp.where((p < size) & (q < size), v_ref[0], 0.0)
    hi = v.astype(jnp.bfloat16)
    v_all[0:depth] = hi
    v_all[depth : 2 * depth] = hi
    v_all[2 * depth : 3 * depth] = (v - hi.astype(jnp.float32)).astype(jnp.bfloat16)

    def chunk(k):
        acc = jnp.dot(
            a_all[SIDE * rows * k : SIDE * rows * (k + 1)], v_all[...], preferred_element_type=jnp.float32
        )
        return [acc[rows * s : rows * (s + 1)] for s in range(SIDE)]

    far = chunk(2)
    send_p[0], send_p[1], send_m[0], send_m[1] = far
    up[0], up[1], send_p[2], send_p[3] = chunk(1)
    send_m[2], send_m[3], down[0], down[1] = chunk(3)
    own[0], own[1], own[2], own[3] = chunk(0)


def product(amp, skip, ovov, v_first, count, place, place_at, sizes, origin, after, name):
    sources, _, rows2, depth = amp.shape
    rows = rows2 // 2
    cols = ovov.shape[2]
    leads = (4, 4, 2, 2, 4)
    total = 16 * rows
    return pl.pallas_call(
        functools.partial(product_kernel, v_first, place_at),
        grid_spec=pltpu.PrefetchScalarGridSpec(
            num_scalar_prefetch=3,
            grid=(count, cols // WIDTH),
            in_specs=[
                pl.BlockSpec((1, 1, rows2, depth), lambda g, *_, s=s: (s, skip + g, 0, 0)) for s in range(sources)
            ]
            + [pl.BlockSpec((1, depth, WIDTH), lambda g, c, *_: (v_first + g, 0, c))]
            + [pl.BlockSpec(memory_space=pl.ANY)] * len(after),
            out_specs=[pl.BlockSpec((n, rows, WIDTH), lambda g, c, *_: (g, 0, c)) for n in leads],
            scratch_shapes=[
                pltpu.VMEM((total, 3 * depth), jnp.bfloat16),
                pltpu.VMEM((3 * depth, WIDTH), jnp.bfloat16),
            ],
        ),
        out_shape=[
            jax.ShapeDtypeStruct((n * count, rows, cols), jnp.float32) for n in leads
        ],
        compiler_params=pltpu.CompilerParams(vmem_limit_bytes=VMEM),
        cost_estimate=LIGHT,
        name=name,
    )(place, sizes, origin, *[amp] * sources, ovov, *after)


def add_kernel(mid, recv, *refs):
    refs[-1][...] = mid[...] + recv[...]


def add_far(mid, recv, after, name):
    lead, rows, cols = mid.shape
    spec = pl.BlockSpec((2, rows, cols), lambda g: (g, 0, 0))
    return pl.pallas_call(
        add_kernel,
        grid=(lead // 2,),
        in_specs=[spec, pl.BlockSpec((2, rows, cols), lambda g: (2 * g, 0, 0))]
        + [pl.BlockSpec(memory_space=pl.ANY)] * len(after),
        out_specs=spec,
        out_shape=jax.ShapeDtypeStruct(mid.shape, jnp.float32),
        compiler_params=pltpu.CompilerParams(vmem_limit_bytes=VMEM),
        cost_estimate=LIGHT,
        name=name,
    )(mid, recv, *after)


def own_kernel(own, p1, m1, p2, m2, *refs):
    outs = refs[-4:]
    outs[0][0] = own[0] + (p2[0] + m1[0])
    outs[1][0] = own[1] + (p2[1] + m1[1])
    outs[2][0] = own[2] + (m2[0] + p1[0])
    outs[3][0] = own[3] + (m2[1] + p1[1])


def add_own(own, p1, m1, p2, m2, at, total, into, name):
    rows, cols = own.shape[1:]
    half = pl.BlockSpec((2, rows, cols), lambda g: (2 * g + 1, 0, 0))
    last = pl.BlockSpec((2, rows, cols), lambda g: (g, 0, 0))
    return pl.pallas_call(
        own_kernel,
        grid=(own.shape[0] // 4,),
        in_specs=[pl.BlockSpec((4, rows, cols), lambda g: (g, 0, 0)), half, half, last, last]
        + [pl.BlockSpec(memory_space=pl.ANY)] * len(into),
        out_specs=[pl.BlockSpec((1, rows, cols), lambda g: (at + g, 0, 0))] * 4,
        out_shape=[jax.ShapeDtypeStruct((total, rows, cols), jnp.float32)] * 4,
        input_output_aliases={5 + i: i for i in range(len(into))},
        compiler_params=pltpu.CompilerParams(vmem_limit_bytes=VMEM),
        cost_estimate=LIGHT,
        name=name,
    )(own, p1, m1, p2, m2, *into)


def finish_kernel(order, sizes, origin, *refs):
    out = refs[-1]
    rows, _, cols = out.shape
    row = origin[0] + lax.broadcasted_iota(jnp.int32, (rows, cols), 0)
    for i, irreps in enumerate(order):
        parts = refs[4 * i : 4 * i + 4]
        for at, g in enumerate(irreps):
            total = (parts[0][at] + parts[1][at]) + (parts[2][at] + parts[3][at])
            out[:, g, :] = jnp.where(row < sizes[g], total, 0.0)


def finish(order, parts, row_sizes, origin, shape):
    rows, irreps, cols = shape
    flat = [p for four in parts for p in four]
    return pl.pallas_call(
        functools.partial(finish_kernel, order),
        grid_spec=pltpu.PrefetchScalarGridSpec(
            num_scalar_prefetch=2,
            grid=(cols // WIDTH,),
            in_specs=[pl.BlockSpec((p.shape[0], rows, WIDTH), lambda c, *_: (0, 0, c)) for p in flat],
            out_specs=pl.BlockSpec((rows, irreps, WIDTH), lambda c, *_: (0, 0, c)),
        ),
        out_shape=jax.ShapeDtypeStruct(shape, jnp.float32),
        compiler_params=pltpu.CompilerParams(vmem_limit_bytes=VMEM),
        cost_estimate=LIGHT,
        name="finish",
    )(row_sizes, origin, *flat)


GROUPS = ((0, 2, 2), (4, 2, 2))


def local(amplitudes, ovov, row_sizes, pair_sizes):
    ob = lax.axis_index("ob")
    vb = lax.axis_index("vb")
    local_rows, irreps, pairs = amplitudes.shape
    obs = lax.axis_size("ob")
    depth, cols = ovov.shape[1:]
    out_rows = local_rows * lax.axis_size("vb")
    place = lax.dynamic_slice(jnp.asarray(PLACES), (vb, ob, 0), (1, 1, 32)).reshape(32)

    origin = jnp.stack([ob * depth, vb * cols]).astype(jnp.int32)

    axes = {"y": (Y_HOPS, X_HOPS, 16), "x": (X_HOPS, Y_HOPS, 0)}
    order = {axis: [] for axis in axes}
    sums = {axis: [] for axis in axes}

    gathered = []
    for first, nx, ny in GROUPS:
        count = nx + ny
        mine = amplitudes[:, first : first + count].reshape(local_rows, count, obs, depth)
        mine = jnp.transpose(mine, (2, 0, 1, 3)).reshape(obs, local_rows * count, depth)
        mine = lax.all_to_all(mine, "ob", split_axis=0, concat_axis=0, tiled=True)
        mine = jnp.transpose(mine.reshape(obs * local_rows, count, depth), (1, 0, 2))
        gathered.append(lax.all_gather(mine, "vb", axis=0))

    def first_step(axis, t, waits):
        first, nx, ny = GROUPS[t]
        skip, count = (0, nx) if axis == "x" else (nx, ny)
        order[axis] += range(first + skip, first + skip + count)
        here, _, place_at = axes[axis]
        send_p, send_m, up, down, mid = product(
            gathered[t], skip, ovov, first + skip, count, place, place_at, pair_sizes, origin, waits, f"{axis}_product"
        )
        p1 = lax.ppermute(send_p, BOTH, here[1])
        m1 = lax.ppermute(send_m, BOTH, here[-1])
        return send_p, up, down, mid, p1, m1

    def second_step(axis, now, waits):
        here = axes[axis][0]
        _, up, down, mid, p1, m1 = now
        added = [add_far(up, p1, waits, f"{axis}_add"), add_far(down, m1, waits, f"{axis}_add")]
        handed = [lax.ppermute(added[0], BOTH, here[1]), lax.ppermute(added[1], BOTH, here[-1])]
        sums[axis].append((mid, p1, m1, *handed))
        return added, handed

    y1 = first_step("y", 0, [])
    x1 = first_step("x", 0, [])
    y1_added, y1_handed = second_step("y", y1, [])
    y2 = first_step("y", 1, y1_added)
    x1_added, x1_handed = second_step("x", x1, [y2[0]])
    x2 = first_step("x", 1, x1_added + y1_handed)
    second_step("y", y2, x1_handed)
    second_step("x", x2, [])

    parts = []
    for axis, (_, there, _) in axes.items():
        four, at = [], 0
        for group in sums[axis]:
            four = add_own(*group, at, len(order[axis]), four, f"{axis}_own")
            at += group[0].shape[0] // 4
        parts.append([four[0]] + [lax.ppermute(four[k], BOTH, there[d]) for k, d in ((1, 1), (2, 2), (3, -1))])
    origin = jnp.stack([ob * out_rows, vb * cols]).astype(jnp.int32)
    return finish([order[axis] for axis in axes], parts, row_sizes, origin, (out_rows, irreps, cols))


def solution(mesh):
    placed = (P(("vb", "ob"), None, None), P(None, "ob", "vb"), P(), P())
    return jax.shard_map(
        local, mesh=mesh, in_specs=placed, out_specs=P("ob", None, "vb"), check_vma=False
    )
```

```python
import functools

import jax
import jax.numpy as jnp
import numpy as np
from jax import lax
from jax.experimental import pallas as pl
from jax.experimental.pallas import tpu as pltpu
from jax.sharding import PartitionSpec as P

SIDE = 4
VMEM = 63 * 1024 * 1024
WIDTH = 256
LIGHT = pl.CostEstimate(flops=0, bytes_accessed=0, transcendentals=0)
def hops(count, stride, delta):
    pairs = []
    for i in range(count):
        d = (i // stride) % SIDE
        pairs.append((i, i + ((d + delta) % SIDE - d) * stride))
    return pairs


def apart(count, stride, delta, cores):
    up, down = hops(count, stride, delta), hops(count, stride, -delta)
    return [(down if cores(i) else up)[i] for i in range(count)]


X_HOPS = {d: apart(128, SIDE, d, lambda i: i // 16 % 2) for d in (1, 2, -1)}
Y_HOPS = {d: apart(128, 1, d, lambda i: i // 16 % 2) for d in (1, 2, -1)}
BOTH = ("vb", "ob")


ORDER = [(2, 0), (2, 1), (1, 2), (1, 3)] + [(2, 2), (2, 3), (3, 0), (3, 1)]
ORDER += [(1, 0), (1, 1)] + [(3, 2), (3, 3)] + [(0, k) for k in range(SIDE)]


def block_table():
    table = np.zeros((8, 16, 32), np.int32)
    for vb in range(8):
        for ob in range(16):
            x, y = divmod(ob, SIDE)
            sign = -1 if vb % 2 else 1
            for i, (near, far) in enumerate(ORDER):
                table[vb, ob, i] = (x + sign * near) % SIDE * SIDE + (y + sign * far) % SIDE
                table[vb, ob, 16 + i] = (x + sign * far) % SIDE * SIDE + (y + sign * near) % SIDE
    return table


BLOCKS = block_table()


def product_kernel(first, x_count, leads, blocks, sizes, origin, *refs):
    pieces, v_ref, outs, (a_all, v_all) = refs[:8], refs[8], refs[-2 - 2 * len(leads) : -2], refs[-2:]
    rows, depth = pieces[0].shape[3:]
    for i, piece in enumerate(pieces):
        block = piece[0, 0, 0]
        hi = block.astype(jnp.bfloat16)
        at = slice(rows * i, rows * (i + 1))
        a_all[at, 0:depth] = hi
        a_all[at, depth : 2 * depth] = (block - hi.astype(jnp.float32)).astype(jnp.bfloat16)
        a_all[at, 2 * depth : 3 * depth] = hi
    size = sizes[first + pl.program_id(0)]
    shape = v_ref.shape[1:]
    p = origin[0] + lax.broadcasted_iota(jnp.int32, shape, 0)
    q = origin[1] + lax.broadcasted_iota(jnp.int32, shape, 1)
    v = jnp.where((p < size) & (q < size), v_ref[0], 0.0)
    hi = v.astype(jnp.bfloat16)
    v_all[0:depth] = hi
    v_all[depth : 2 * depth] = hi
    v_all[2 * depth : 3 * depth] = (v - hi.astype(jnp.float32)).astype(jnp.bfloat16)

    def write(targets):
        at = 0
        for lead, out in zip(leads, targets):
            acc = jnp.dot(
                a_all[rows * at : rows * (at + lead)], v_all[...], preferred_element_type=jnp.float32
            )
            for k in range(lead):
                out[k, 0] = acc[rows * k : rows * (k + 1)]
            at += lead

    @pl.when(pl.program_id(0) < x_count)
    def _():
        write(outs[: len(leads)])

    @pl.when(pl.program_id(0) >= x_count)
    def _():
        write(outs[len(leads) :])


def product(amp, ovov, first, x_count, y_count, half, leads, blocks, sizes, origin, after, name):
    rows, depth = amp.shape[3:]
    cols = ovov.shape[2]

    def a_spec(i):
        def index(g, blocks, *_):
            block = blocks[jnp.where(g < x_count, 0, 16) + 8 * half + i]
            return block // 2, g, block % 2, 0, 0

        return pl.BlockSpec((1, 1, 1, rows, depth), index)

    def x_spec(lead):
        return pl.BlockSpec((lead, 1, rows, cols), lambda g, *_: (0, jnp.minimum(g, x_count - 1), 0, 0))

    def y_spec(lead):
        return pl.BlockSpec((lead, 1, rows, cols), lambda g, *_: (0, jnp.maximum(g - x_count, 0), 0, 0))

    shapes = [(lead, count, rows, cols) for count in (x_count, y_count) for lead in leads]
    outs = pl.pallas_call(
        functools.partial(product_kernel, first, x_count, leads),
        grid_spec=pltpu.PrefetchScalarGridSpec(
            num_scalar_prefetch=3,
            grid=(x_count + y_count,),
            in_specs=[a_spec(i) for i in range(8)]
            + [pl.BlockSpec((1, depth, cols), lambda g, *_: (first + g, 0, 0))]
            + [pl.BlockSpec(memory_space=pl.ANY)] * len(after),
            out_specs=[x_spec(lead) for lead in leads] + [y_spec(lead) for lead in leads],
            scratch_shapes=[
                pltpu.VMEM((8 * rows, 3 * depth), jnp.bfloat16),
                pltpu.VMEM((3 * depth, cols), jnp.bfloat16),
            ],
        ),
        out_shape=[jax.ShapeDtypeStruct(shape, jnp.float32) for shape in shapes],
        compiler_params=pltpu.CompilerParams(vmem_limit_bytes=VMEM),
        cost_estimate=LIGHT,
        name=name,
    )(blocks, sizes, origin, *[amp] * 8, ovov, *after)
    return {"x": outs[: len(leads)], "y": outs[len(leads) :]}


def add_kernel(up, down, recv_p, recv_m, *refs):
    refs[-2][...] = up[...] + recv_p[...]
    refs[-1][...] = down[...] + recv_m[...]


def add_far(up, down, recv_p, recv_m, after, name):
    lead, count, rows, cols = up.shape
    spec = pl.BlockSpec((lead, 1, rows, cols), lambda g: (0, g, 0, 0))
    return pl.pallas_call(
        add_kernel,
        grid=(count,),
        in_specs=[spec] * 4 + [pl.BlockSpec(memory_space=pl.ANY)] * len(after),
        out_specs=[spec] * 2,
        out_shape=[jax.ShapeDtypeStruct(up.shape, jnp.float32)] * 2,
        compiler_params=pltpu.CompilerParams(vmem_limit_bytes=VMEM),
        cost_estimate=LIGHT,
        name=name,
    )(up, down, recv_p, recv_m, *after)


def own_kernel(own, p1, m1, p2, m2, *refs):
    outs = refs[-4:]
    outs[0][0] = own[0, 0] + (p2[0, 0] + m1[0, 0])
    outs[1][0] = own[1, 0] + (p2[1, 0] + m1[1, 0])
    outs[2][0] = own[2, 0] + (m2[0, 0] + p1[0, 0])
    outs[3][0] = own[3, 0] + (m2[1, 0] + p1[1, 0])


def add_own(own, p1, m1, p2, m2, at, total, into, name):
    count, rows, cols = own.shape[1:]

    def spec(lead, first):
        return pl.BlockSpec((lead, 1, rows, cols), lambda g: (first, g, 0, 0))

    return pl.pallas_call(
        own_kernel,
        grid=(count,),
        in_specs=[spec(4, 0), spec(2, 1), spec(2, 1), spec(2, 0), spec(2, 0)]
        + [pl.BlockSpec(memory_space=pl.ANY)] * len(into),
        out_specs=[pl.BlockSpec((1, rows, cols), lambda g: (at + g, 0, 0))] * 4,
        out_shape=[jax.ShapeDtypeStruct((total, rows, cols), jnp.float32)] * 4,
        input_output_aliases={5 + i: i for i in range(len(into))},
        compiler_params=pltpu.CompilerParams(vmem_limit_bytes=VMEM),
        cost_estimate=LIGHT,
        name=name,
    )(own, p1, m1, p2, m2, *into)


def finish_kernel(order, sizes, origin, *refs):
    out = refs[-1]
    rows, _, cols = out.shape
    row = origin[0] + lax.broadcasted_iota(jnp.int32, (rows, cols), 0)
    for i, irreps in enumerate(order):
        parts = refs[4 * i : 4 * i + 4]
        for at, g in enumerate(irreps):
            total = (parts[0][at] + parts[1][at]) + (parts[2][at] + parts[3][at])
            out[:, g, :] = jnp.where(row < sizes[g], total, 0.0)


def finish(order, parts, row_sizes, origin, shape):
    rows, irreps, cols = shape
    flat = [p for four in parts for p in four]
    return pl.pallas_call(
        functools.partial(finish_kernel, order),
        grid_spec=pltpu.PrefetchScalarGridSpec(
            num_scalar_prefetch=2,
            grid=(cols // WIDTH,),
            in_specs=[pl.BlockSpec((p.shape[0], rows, WIDTH), lambda c, *_: (0, 0, c)) for p in flat],
            out_specs=pl.BlockSpec((rows, irreps, WIDTH), lambda c, *_: (0, 0, c)),
        ),
        out_shape=jax.ShapeDtypeStruct(shape, jnp.float32),
        compiler_params=pltpu.CompilerParams(vmem_limit_bytes=VMEM),
        cost_estimate=LIGHT,
        name="finish",
    )(row_sizes, origin, *flat)


GROUPS = ((0, 2, 2), (4, 2, 2))


def exchange(amplitudes, first, count, depth):
    rows, _, pairs = amplitudes.shape
    parts = pairs // depth
    mine = amplitudes[:, first : first + count].reshape(rows, count, parts, depth)
    mine = jnp.transpose(mine, (2, 0, 1, 3)).reshape(parts, rows * count, depth)
    mine = lax.all_to_all(mine, "ob", split_axis=0, concat_axis=0, tiled=True)
    return jnp.transpose(mine.reshape(parts * rows, count, depth), (1, 0, 2))


def contract(first_mine, amplitudes, ovov, row_sizes, pair_sizes):
    ob = lax.axis_index("ob")
    vb = lax.axis_index("vb")
    local_rows, irreps, _ = amplitudes.shape
    depth, cols = ovov.shape[1:]
    out_rows = local_rows * lax.axis_size("vb")
    blocks = lax.dynamic_slice(jnp.asarray(BLOCKS), (vb, ob, 0), (1, 1, 32)).reshape(32)
    origin = jnp.stack([ob * depth, vb * cols]).astype(jnp.int32)

    hops_of = {"x": (X_HOPS, Y_HOPS), "y": (Y_HOPS, X_HOPS)}
    order = {axis: [] for axis in hops_of}
    sums = {axis: [] for axis in hops_of}
    gathered = []
    for t, (first, nx, ny) in enumerate(GROUPS):
        mine = exchange(amplitudes, first, nx + ny, depth) if t else first_mine
        order["x"] += range(first, first + nx)
        order["y"] += range(first + nx, first + nx + ny)
        gathered.append(lax.all_gather(mine, "vb", axis=0).reshape(-1, nx + ny, 2, out_rows, depth))

    after, behind = [], []
    for t, (first, nx, ny) in enumerate(GROUPS):
        leads = {"send": (4, 4), "rest": (2, 2, 4)}
        args = (gathered[t], ovov, first, nx, ny)
        send = product(*args, 0, leads["send"], blocks, pair_sizes, origin, after, "send")
        recv = {
            axis: (lax.ppermute(send[axis][0], BOTH, here[1]), lax.ppermute(send[axis][1], BOTH, here[-1]))
            for axis, (here, _) in hops_of.items()
        }
        rest = product(*args, 1, leads["rest"], blocks, pair_sizes, origin, [*send["y"], *behind], "rest")
        after, behind = [], []
        for axis, (here, _) in hops_of.items():
            up, down, own = rest[axis]
            added = add_far(up, down, *recv[axis], [], f"{axis}_add")
            after += added
            handed = lax.ppermute(added[0], BOTH, here[1]), lax.ppermute(added[1], BOTH, here[-1])
            behind += handed
            sums[axis].append((own, *recv[axis], *handed))

    parts = []
    for axis, (_, there) in hops_of.items():
        four, at = [], 0
        for group in sums[axis]:
            four = add_own(*group, at, len(order[axis]), four, f"{axis}_own")
            at += group[0].shape[1]
        parts.append([four[0]] + [lax.ppermute(four[k], BOTH, there[d]) for k, d in ((1, 1), (2, 2), (3, -1))])
    origin = jnp.stack([ob * out_rows, vb * cols]).astype(jnp.int32)
    return finish([order[axis] for axis in hops_of], parts, row_sizes, origin, (out_rows, irreps, cols))


def local(amplitudes, ovov, row_sizes, pair_sizes):
    local_rows, irreps, _ = amplitudes.shape
    depth, cols = ovov.shape[1:]
    first, nx, ny = GROUPS[0]
    mine = exchange(amplitudes, first, nx + ny, depth)
    nothing = jnp.zeros((local_rows * lax.axis_size("vb"), irreps, cols), jnp.float32)
    return lax.cond(
        jnp.max(row_sizes) > 0,
        contract,
        lambda *_: nothing,
        mine, amplitudes, ovov, row_sizes, pair_sizes,
    )


def solution(mesh):
    placed = (P(("vb", "ob"), None, None), P(None, "ob", "vb"), P(), P())
    return jax.shard_map(
        local, mesh=mesh, in_specs=placed, out_specs=P("ob", None, "vb"), check_vma=False
    )
```

```python
import functools

import jax
import jax.numpy as jnp
import numpy as np
from jax import lax
from jax.experimental import pallas as pl
from jax.experimental.pallas import tpu as pltpu
from jax.sharding import PartitionSpec as P

SIDE = 4
VMEM = 63 * 1024 * 1024
WIDTH = 256
LIGHT = pl.CostEstimate(flops=0, bytes_accessed=0, transcendentals=0)
def hops(count, stride, delta):
    pairs = []
    for i in range(count):
        d = (i // stride) % SIDE
        pairs.append((i, i + ((d + delta) % SIDE - d) * stride))
    return pairs


def apart(count, stride, delta, cores):
    up, down = hops(count, stride, delta), hops(count, stride, -delta)
    return [(down if cores(i) else up)[i] for i in range(count)]


SWAP = [(i, i ^ 1) for i in range(8)]
Z_STEPS = [apart(8, 2, d, lambda i: i % 2) for d in (1, -1, 2)]
X_HOPS = {d: apart(128, SIDE, d, lambda i: i // 16 % 2) for d in (1, 2, -1)}
Y_HOPS = {d: apart(128, 1, d, lambda i: i // 16 % 2) for d in (1, 2, -1)}
BOTH = ("vb", "ob")


ORDER = [(2, 0), (2, 1), (1, 2), (1, 3)] + [(2, 2), (2, 3), (3, 0), (3, 1)]
ORDER += [(1, 0), (1, 1)] + [(3, 2), (3, 3)] + [(0, k) for k in range(SIDE)]


SOURCES = [(dz, dc) for dz in (0, -1, 1, 2) for dc in (0, 1)]


def place_table():
    table = np.zeros((8, 16, 32), np.int32)
    for vb in range(8):
        for ob in range(16):
            x, y = divmod(ob, SIDE)
            sign = -1 if vb % 2 else 1
            for a, (dz, dc) in enumerate(SOURCES):
                core = (vb % 2) ^ dc
                source = 2 * ((vb // 2 + (-dz if core else dz)) % SIDE) + core
                for h in range(2):
                    to_x, to_y = divmod(2 * source + h, SIDE)
                    rel_x, rel_y = sign * (to_x - x) % SIDE, sign * (to_y - y) % SIDE
                    table[vb, ob, 2 * a + h] = ORDER.index((rel_x, rel_y))
                    table[vb, ob, 16 + 2 * a + h] = ORDER.index((rel_y, rel_x))
    return table


PLACES = place_table()
LEADS = (4, 4, 2, 2, 4)


def product_kernel(first, x_count, place, sizes, origin, *refs):
    pieces, v_ref, outs, (a_all, v_all) = refs[:8], refs[8], refs[-12:-2], refs[-2:]
    rows = pieces[0].shape[1] // 2
    depth = pieces[0].shape[2]
    table = jnp.where(pl.program_id(0) < x_count, 0, 16)
    for a, piece in enumerate(pieces):
        for h in range(2):
            block = piece[0, h * rows : (h + 1) * rows]
            hi = block.astype(jnp.bfloat16)
            at = pl.ds(pl.multiple_of(place[table + 2 * a + h] * rows, rows), rows)
            a_all[at, 0:depth] = hi
            a_all[at, depth : 2 * depth] = (block - hi.astype(jnp.float32)).astype(jnp.bfloat16)
            a_all[at, 2 * depth : 3 * depth] = hi
    size = sizes[first + pl.program_id(0)]
    shape = v_ref.shape[1:]
    p = origin[0] + lax.broadcasted_iota(jnp.int32, shape, 0)
    q = origin[1] + lax.broadcasted_iota(jnp.int32, shape, 1)
    v = jnp.where((p < size) & (q < size), v_ref[0], 0.0)
    hi = v.astype(jnp.bfloat16)
    v_all[0:depth] = hi
    v_all[depth : 2 * depth] = hi
    v_all[2 * depth : 3 * depth] = (v - hi.astype(jnp.float32)).astype(jnp.bfloat16)

    def write(targets):
        at = 0
        for lead, out in zip(LEADS, targets):
            acc = jnp.dot(
                a_all[rows * at : rows * (at + lead)], v_all[...], preferred_element_type=jnp.float32
            )
            for k in range(lead):
                out[k, 0] = acc[rows * k : rows * (k + 1)]
            at += lead

    @pl.when(pl.program_id(0) < x_count)
    def _():
        write(outs[:5])

    @pl.when(pl.program_id(0) >= x_count)
    def _():
        write(outs[5:])


def product(pieces, ovov, first, x_count, y_count, place, sizes, origin, after, name):
    rows2, depth = pieces[0][0].shape[1:]
    rows = rows2 // 2
    cols = ovov.shape[2]

    def x_spec(lead):
        return pl.BlockSpec((lead, 1, rows, cols), lambda g, *_: (0, jnp.minimum(g, x_count - 1), 0, 0))

    def y_spec(lead):
        return pl.BlockSpec((lead, 1, rows, cols), lambda g, *_: (0, jnp.maximum(g - x_count, 0), 0, 0))

    shapes = [(lead, count, rows, cols) for count in (x_count, y_count) for lead in LEADS]
    outs = pl.pallas_call(
        functools.partial(product_kernel, first, x_count),
        grid_spec=pltpu.PrefetchScalarGridSpec(
            num_scalar_prefetch=3,
            grid=(x_count + y_count,),
            in_specs=[pl.BlockSpec((1, rows2, depth), lambda g, *_, at=at: (at + g, 0, 0)) for _, at in pieces]
            + [pl.BlockSpec((1, depth, cols), lambda g, *_: (first + g, 0, 0))]
            + [pl.BlockSpec(memory_space=pl.ANY)] * len(after),
            out_specs=[x_spec(lead) for lead in LEADS] + [y_spec(lead) for lead in LEADS],
            scratch_shapes=[
                pltpu.VMEM((16 * rows, 3 * depth), jnp.bfloat16),
                pltpu.VMEM((3 * depth, cols), jnp.bfloat16),
            ],
        ),
        out_shape=[jax.ShapeDtypeStruct(shape, jnp.float32) for shape in shapes],
        compiler_params=pltpu.CompilerParams(vmem_limit_bytes=VMEM),
        cost_estimate=LIGHT,
        name=name,
    )(place, sizes, origin, *[piece for piece, _ in pieces], ovov, *after)
    return {"x": outs[:5], "y": outs[5:]}


def tie_kernel(*refs):
    pass


def tie(values, after):
    anywhere = pl.BlockSpec(memory_space=pl.ANY)
    return pl.pallas_call(
        tie_kernel,
        in_specs=[anywhere] * (len(values) + len(after)),
        out_specs=[anywhere] * len(values),
        out_shape=[jax.ShapeDtypeStruct(v.shape, v.dtype) for v in values],
        input_output_aliases={i: i for i in range(len(values))},
        compiler_params=pltpu.CompilerParams(vmem_limit_bytes=VMEM),
        cost_estimate=LIGHT,
        name="tie",
    )(*values, *after)


def add_kernel(up, down, recv_p, recv_m, *refs):
    refs[-2][...] = up[...] + recv_p[...]
    refs[-1][...] = down[...] + recv_m[...]


def add_far(up, down, recv_p, recv_m, after, name):
    lead, count, rows, cols = up.shape
    spec = pl.BlockSpec((lead, 1, rows, cols), lambda g: (0, g, 0, 0))
    return pl.pallas_call(
        add_kernel,
        grid=(count,),
        in_specs=[spec] * 4 + [pl.BlockSpec(memory_space=pl.ANY)] * len(after),
        out_specs=[spec] * 2,
        out_shape=[jax.ShapeDtypeStruct(up.shape, jnp.float32)] * 2,
        compiler_params=pltpu.CompilerParams(vmem_limit_bytes=VMEM),
        cost_estimate=LIGHT,
        name=name,
    )(up, down, recv_p, recv_m, *after)


def own_kernel(own, p1, m1, p2, m2, *refs):
    outs = refs[-4:]
    outs[0][0] = own[0, 0] + (p2[0, 0] + m1[0, 0])
    outs[1][0] = own[1, 0] + (p2[1, 0] + m1[1, 0])
    outs[2][0] = own[2, 0] + (m2[0, 0] + p1[0, 0])
    outs[3][0] = own[3, 0] + (m2[1, 0] + p1[1, 0])


def add_own(own, p1, m1, p2, m2, at, total, into, name):
    count, rows, cols = own.shape[1:]

    def spec(lead, first):
        return pl.BlockSpec((lead, 1, rows, cols), lambda g: (first, g, 0, 0))

    return pl.pallas_call(
        own_kernel,
        grid=(count,),
        in_specs=[spec(4, 0), spec(2, 1), spec(2, 1), spec(2, 0), spec(2, 0)]
        + [pl.BlockSpec(memory_space=pl.ANY)] * len(into),
        out_specs=[pl.BlockSpec((1, rows, cols), lambda g: (at + g, 0, 0))] * 4,
        out_shape=[jax.ShapeDtypeStruct((total, rows, cols), jnp.float32)] * 4,
        input_output_aliases={5 + i: i for i in range(len(into))},
        compiler_params=pltpu.CompilerParams(vmem_limit_bytes=VMEM),
        cost_estimate=LIGHT,
        name=name,
    )(own, p1, m1, p2, m2, *into)


def finish_kernel(order, sizes, origin, *refs):
    out = refs[-1]
    rows, _, cols = out.shape
    row = origin[0] + lax.broadcasted_iota(jnp.int32, (rows, cols), 0)
    for i, irreps in enumerate(order):
        parts = refs[4 * i : 4 * i + 4]
        for at, g in enumerate(irreps):
            total = (parts[0][at] + parts[1][at]) + (parts[2][at] + parts[3][at])
            out[:, g, :] = jnp.where(row < sizes[g], total, 0.0)


def finish(order, parts, row_sizes, origin, shape):
    rows, irreps, cols = shape
    flat = [p for four in parts for p in four]
    return pl.pallas_call(
        functools.partial(finish_kernel, order),
        grid_spec=pltpu.PrefetchScalarGridSpec(
            num_scalar_prefetch=2,
            grid=(cols // WIDTH,),
            in_specs=[pl.BlockSpec((p.shape[0], rows, WIDTH), lambda c, *_: (0, 0, c)) for p in flat],
            out_specs=pl.BlockSpec((rows, irreps, WIDTH), lambda c, *_: (0, 0, c)),
        ),
        out_shape=jax.ShapeDtypeStruct(shape, jnp.float32),
        compiler_params=pltpu.CompilerParams(vmem_limit_bytes=VMEM),
        cost_estimate=LIGHT,
        name="finish",
    )(row_sizes, origin, *flat)


GROUPS = ((0, 2, 2), (4, 2, 2))


def local(amplitudes, ovov, row_sizes, pair_sizes):
    ob = lax.axis_index("ob")
    vb = lax.axis_index("vb")
    local_rows, irreps, _ = amplitudes.shape
    obs = lax.axis_size("ob")
    depth, cols = ovov.shape[1:]
    out_rows = local_rows * lax.axis_size("vb")
    place = lax.dynamic_slice(jnp.asarray(PLACES), (vb, ob, 0), (1, 1, 32)).reshape(32)
    origin = jnp.stack([ob * depth, vb * cols]).astype(jnp.int32)

    mine = jnp.transpose(amplitudes.reshape(local_rows, irreps, obs, depth), (2, 0, 1, 3))
    mine = mine.reshape(obs, local_rows * irreps, depth)
    mine = lax.all_to_all(mine, "ob", split_axis=0, concat_axis=0, tiled=True)
    mine = jnp.transpose(mine.reshape(obs * local_rows, irreps, depth), (1, 0, 2))
    mine_swapped = lax.ppermute(mine, "vb", SWAP)

    hops_of = {"x": (X_HOPS, Y_HOPS), "y": (Y_HOPS, X_HOPS)}
    order = {axis: [] for axis in hops_of}
    sums = {axis: [] for axis in hops_of}
    landed, sent, handed = [], [], []
    for t, (first, nx, ny) in enumerate(GROUPS):
        order["x"] += range(first, first + nx)
        order["y"] += range(first + nx, first + nx + ny)
        held = mine[first : first + nx + ny]
        if t:
            (held,) = tie([held], landed)
        landed = [lax.ppermute(held, "vb", steps) for steps in Z_STEPS]
        pieces = [(mine, first), (mine_swapped, first)]
        for piece in tie(landed, sent) if t else landed:
            pieces += [(piece, 0), (lax.ppermute(piece, "vb", SWAP), 0)]
        made = product(pieces, ovov, first, nx, ny, place, pair_sizes, origin, [], "product")
        sent = []
        waits, handed = handed, []
        for axis, (here, _) in hops_of.items():
            send_p, send_m, up, down, own = made[axis]
            p1 = lax.ppermute(send_p, BOTH, here[1])
            m1 = lax.ppermute(send_m, BOTH, here[-1])
            added = add_far(up, down, p1, m1, waits, f"{axis}_add")
            sent += [p1, m1]
            p2, m2 = lax.ppermute(added[0], BOTH, here[1]), lax.ppermute(added[1], BOTH, here[-1])
            handed += [p2, m2]
            sums[axis].append((own, p1, m1, p2, m2))

    parts = []
    for axis, (_, there) in hops_of.items():
        four, at = [], 0
        for group in sums[axis]:
            four = add_own(*group, at, len(order[axis]), four, f"{axis}_own")
            at += group[0].shape[1]
        parts.append([four[0]] + [lax.ppermute(four[k], BOTH, there[d]) for k, d in ((1, 1), (2, 2), (3, -1))])
    origin = jnp.stack([ob * out_rows, vb * cols]).astype(jnp.int32)
    return finish([order[axis] for axis in hops_of], parts, row_sizes, origin, (out_rows, irreps, cols))


def solution(mesh):
    placed = (P(("vb", "ob"), None, None), P(None, "ob", "vb"), P(), P())
    return jax.shard_map(
        local, mesh=mesh, in_specs=placed, out_specs=P("ob", None, "vb"), check_vma=False
    )
```

```python
import functools

import jax
import jax.numpy as jnp
import numpy as np
from jax import lax
from jax.experimental import pallas as pl
from jax.experimental.pallas import tpu as pltpu
from jax.sharding import PartitionSpec as P

SIDE = 4
VMEM = 64 * 1024 * 1024 - 256 * 1024
WIDTH = 256
LIGHT = pl.CostEstimate(flops=0, bytes_accessed=0, transcendentals=0)
def hops(count, steps):
    pairs = []
    for i in range(count):
        stride, delta = steps(i)
        at = (i // stride) % SIDE
        pairs.append((i, i + ((at + delta) % SIDE - at) * stride))
    return pairs


Z_STEPS = [hops(8, lambda i, d=d: (2, -d if i % 2 else d)) for d in (1, -1, 2)]
SWAP = [(i, i ^ 1) for i in range(8)]
BOTH = ("vb", "ob")
NEAR = {d: hops(128, lambda i, d=d: (1 if i // 16 % 2 else SIDE, d)) for d in (1, -1)}
FAR = {d: hops(128, lambda i, d=d: (SIDE if i // 16 % 2 else 1, d)) for d in (1, 2, -1)}


ORDER = [(2, 0), (2, 1)] + [(2, 2), (2, 3)] + [(1, 2), (1, 3)] + [(3, 0), (3, 1)]
ORDER += [(1, 0), (1, 1)] + [(3, 2), (3, 3)] + [(0, k) for k in range(SIDE)]


SOURCES = [(dz, dc) for dz in (0, -1, 1, 2) for dc in (0, 1)]


def place_table():
    table = np.zeros((8, 16, 16), np.int32)
    for vb in range(8):
        for ob in range(16):
            for a, (dz, dc) in enumerate(SOURCES):
                core = (vb % 2) ^ dc
                source = 2 * ((vb // 2 + (-dz if core else dz)) % SIDE) + core
                for h in range(2):
                    to = 2 * source + h
                    rel = (to // SIDE - ob // SIDE) % SIDE, (to - ob) % SIDE
                    table[vb, ob, 2 * a + h] = ORDER.index(rel[::-1] if vb % 2 else rel)
    return table


PLACES = place_table()
LEADS = (2, 2, 2, 2, 2, 2, 4)


def product_kernel(first, place, sizes, origin, *refs):
    pieces, v_ref, outs, (a_all, v_all) = refs[:8], refs[8], refs[-9:-2], refs[-2:]
    rows = pieces[0].shape[1] // 2
    depth = pieces[0].shape[2]
    for a, piece in enumerate(pieces):
        for h in range(2):
            block = piece[0, h * rows : (h + 1) * rows]
            hi = block.astype(jnp.bfloat16)
            at = pl.ds(pl.multiple_of(place[2 * a + h] * rows, rows), rows)
            a_all[at, 0:depth] = hi
            a_all[at, depth : 2 * depth] = (block - hi.astype(jnp.float32)).astype(jnp.bfloat16)
            a_all[at, 2 * depth : 3 * depth] = hi
    size = sizes[first + pl.program_id(0)]
    shape = v_ref.shape[1:]
    p = origin[0] + lax.broadcasted_iota(jnp.int32, shape, 0)
    q = origin[1] + lax.broadcasted_iota(jnp.int32, shape, 1)
    v = jnp.where((p < size) & (q < size), v_ref[0], 0.0)
    hi = v.astype(jnp.bfloat16)
    v_all[0:depth] = hi
    v_all[depth : 2 * depth] = hi
    v_all[2 * depth : 3 * depth] = (v - hi.astype(jnp.float32)).astype(jnp.bfloat16)
    blocks = [(out, k) for lead, out in zip(LEADS, outs) for k in range(lead)]
    for at in range(0, len(blocks), SIDE):
        acc = jnp.dot(a_all[rows * at : rows * (at + SIDE)], v_all[...], preferred_element_type=jnp.float32)
        for i, (out, k) in enumerate(blocks[at : at + SIDE]):
            out[k, 0] = acc[rows * i : rows * (i + 1)]


def product(pieces, ovov, first, count, place, sizes, origin, after):
    rows2, depth = pieces[0][0].shape[1:]
    rows = rows2 // 2
    cols = ovov.shape[2]
    return pl.pallas_call(
        functools.partial(product_kernel, first),
        grid_spec=pltpu.PrefetchScalarGridSpec(
            num_scalar_prefetch=3,
            grid=(count,),
            in_specs=[pl.BlockSpec((1, rows2, depth), lambda g, *_, at=at: (at + g, 0, 0)) for _, at in pieces]
            + [pl.BlockSpec((1, depth, cols), lambda g, *_: (first + g, 0, 0))]
            + [pl.BlockSpec(memory_space=pl.ANY)] * len(after),
            out_specs=[pl.BlockSpec((lead, 1, rows, cols), lambda g, *_: (0, g, 0, 0)) for lead in LEADS],
            scratch_shapes=[
                pltpu.VMEM((16 * rows, 3 * depth), jnp.bfloat16),
                pltpu.VMEM((3 * depth, cols), jnp.bfloat16),
            ],
        ),
        out_shape=[jax.ShapeDtypeStruct((lead, count, rows, cols), jnp.float32) for lead in LEADS],
        compiler_params=pltpu.CompilerParams(vmem_limit_bytes=VMEM),
        cost_estimate=LIGHT,
        name="product",
    )(place, sizes, origin, *[piece for piece, _ in pieces], ovov, *after)


def tie_kernel(*refs):
    pass


def tie(values, after):
    anywhere = pl.BlockSpec(memory_space=pl.ANY)
    return pl.pallas_call(
        tie_kernel,
        in_specs=[anywhere] * (len(values) + len(after)),
        out_specs=[anywhere] * len(values),
        out_shape=[jax.ShapeDtypeStruct(v.shape, v.dtype) for v in values],
        input_output_aliases={i: i for i in range(len(values))},
        compiler_params=pltpu.CompilerParams(vmem_limit_bytes=VMEM),
        cost_estimate=LIGHT,
        name="tie",
    )(*values, *after)


def add_kernel(up, down, recv_p, recv_m, *refs):
    refs[-2][...] = up[...] + recv_p[...]
    refs[-1][...] = down[...] + recv_m[...]


def add_far(up, down, recv_p, recv_m, after):
    lead, count, rows, cols = up.shape
    spec = pl.BlockSpec((lead, 1, rows, cols), lambda g: (0, g, 0, 0))
    return pl.pallas_call(
        add_kernel,
        grid=(count,),
        in_specs=[spec] * 4 + [pl.BlockSpec(memory_space=pl.ANY)] * len(after),
        out_specs=[spec] * 2,
        out_shape=[jax.ShapeDtypeStruct(up.shape, jnp.float32)] * 2,
        compiler_params=pltpu.CompilerParams(vmem_limit_bytes=VMEM),
        cost_estimate=LIGHT,
        name="add_far",
    )(up, down, recv_p, recv_m, *after)


def own_kernel(own, n1, n2, p2, m2, *refs):
    outs = refs[-4:]
    outs[0][0] = own[0, 0] + (p2[0, 0] + n2[0, 0])
    outs[1][0] = own[1, 0] + (p2[1, 0] + n2[1, 0])
    outs[2][0] = own[2, 0] + (m2[0, 0] + n1[0, 0])
    outs[3][0] = own[3, 0] + (m2[1, 0] + n1[1, 0])


def add_own(own, n1, n2, p2, m2, at, total, into):
    count, rows, cols = own.shape[1:]

    def spec(lead):
        return pl.BlockSpec((lead, 1, rows, cols), lambda g: (0, g, 0, 0))

    return pl.pallas_call(
        own_kernel,
        grid=(count,),
        in_specs=[spec(4)] + [spec(2)] * 4
        + [pl.BlockSpec(memory_space=pl.ANY)] * len(into),
        out_specs=[pl.BlockSpec((1, rows, cols), lambda g: (at + g, 0, 0))] * 4,
        out_shape=[jax.ShapeDtypeStruct((total, rows, cols), jnp.float32)] * 4,
        input_output_aliases={5 + i: i for i in range(len(into))},
        compiler_params=pltpu.CompilerParams(vmem_limit_bytes=VMEM),
        cost_estimate=LIGHT,
        name="add_own",
    )(own, n1, n2, p2, m2, *into)


def finish_kernel(sizes, origin, a, b, c, d, out):
    rows, irreps, cols = out.shape
    row = origin[0] + lax.broadcasted_iota(jnp.int32, (rows, cols), 0)
    for g in range(irreps):
        out[:, g, :] = jnp.where(row < sizes[g], (a[g] + b[g]) + (c[g] + d[g]), 0.0)


def finish(parts, row_sizes, origin):
    irreps, rows, cols = parts[0].shape
    part = pl.BlockSpec((irreps, rows, WIDTH), lambda c, *_: (0, 0, c))
    return pl.pallas_call(
        finish_kernel,
        grid_spec=pltpu.PrefetchScalarGridSpec(
            num_scalar_prefetch=2,
            grid=(cols // WIDTH,),
            in_specs=[part] * 4,
            out_specs=pl.BlockSpec((rows, irreps, WIDTH), lambda c, *_: (0, 0, c)),
        ),
        out_shape=jax.ShapeDtypeStruct((rows, irreps, cols), jnp.float32),
        compiler_params=pltpu.CompilerParams(vmem_limit_bytes=VMEM),
        cost_estimate=LIGHT,
        name="finish",
    )(row_sizes, origin, *parts)


GROUPS = ((0, 4), (4, 4))


def local(amplitudes, ovov, row_sizes, pair_sizes):
    ob = lax.axis_index("ob")
    vb = lax.axis_index("vb")
    local_rows, irreps, _ = amplitudes.shape
    obs = lax.axis_size("ob")
    depth, cols = ovov.shape[1:]
    out_rows = local_rows * lax.axis_size("vb")
    place = lax.dynamic_slice(jnp.asarray(PLACES), (vb, ob, 0), (1, 1, 16)).reshape(16)
    origin = jnp.stack([ob * depth, vb * cols]).astype(jnp.int32)

    mine = jnp.transpose(amplitudes.reshape(local_rows, irreps, obs, depth), (2, 0, 1, 3))
    mine = mine.reshape(obs, local_rows * irreps, depth)
    mine = lax.all_to_all(mine, "ob", split_axis=0, concat_axis=0, tiled=True)
    mine = jnp.transpose(mine.reshape(obs * local_rows, irreps, depth), (1, 0, 2))
    mine_swapped = lax.ppermute(mine, "vb", SWAP)

    gathered, landed = [], []
    for first, count in GROUPS:
        held = mine[first : first + count]
        if landed:
            (held,) = tie([held], landed)
        landed = [lax.ppermute(held, "vb", steps) for steps in Z_STEPS]
        pieces = [(mine, first), (mine_swapped, first)]
        for piece in landed:
            pieces += [(piece, 0), (lax.ppermute(piece, "vb", SWAP), 0)]
        gathered.append(pieces)

    swapped = [piece for piece, _ in gathered[-1][3::2]]
    sums, added = [], []
    for (first, count), pieces in zip(GROUPS, gathered):
        far_p, far_m, near_p, near_m, up, down, own = product(
            pieces, ovov, first, count, place, pair_sizes, origin, added
        )
        far_p = lax.ppermute(far_p, BOTH, NEAR[1])
        far_m = lax.ppermute(far_m, BOTH, NEAR[-1])
        near_p = lax.ppermute(near_p, BOTH, NEAR[1])
        near_m = lax.ppermute(near_m, BOTH, NEAR[-1])
        added = add_far(up, down, far_p, far_m, sums[-1][1:] if sums else swapped)
        sums.append((own, near_p, near_m, lax.ppermute(added[0], BOTH, NEAR[1]), lax.ppermute(added[1], BOTH, NEAR[-1])))

    four = []
    for (first, _), group in zip(GROUPS, sums):
        four = add_own(*group, first, irreps, four)
    parts = [four[0]] + [lax.ppermute(four[k], BOTH, FAR[d]) for k, d in ((1, 1), (2, 2), (3, -1))]
    origin = jnp.stack([ob * out_rows, vb * cols]).astype(jnp.int32)
    return finish(parts, row_sizes, origin)


def solution(mesh):
    placed = (P(("vb", "ob"), None, None), P(None, "ob", "vb"), P(), P())
    return jax.shard_map(
        local, mesh=mesh, in_specs=placed, out_specs=P("ob", None, "vb"), check_vma=False
    )
```

```python
import functools

import jax
import jax.numpy as jnp
import numpy as np
from jax import lax
from jax.experimental import pallas as pl
from jax.experimental.pallas import tpu as pltpu
from jax.sharding import PartitionSpec as P

SIDE = 4
VMEM = 64 * 1024 * 1024 - 256 * 1024
WIDTH = 256
LIGHT = pl.CostEstimate(flops=0, bytes_accessed=0, transcendentals=0)
def hops(count, steps):
    pairs = []
    for i in range(count):
        stride, delta = steps(i)
        at = (i // stride) % SIDE
        pairs.append((i, i + ((at + delta) % SIDE - at) * stride))
    return pairs


Z_STEPS = [hops(8, lambda i, d=d: (2, -d if i % 2 else d)) for d in (1, -1, 2)]
SWAP = [(i, i ^ 1) for i in range(8)]
BOTH = ("vb", "ob")
NEAR = {d: hops(128, lambda i, d=d: (1 if i // 16 % 2 else SIDE, d)) for d in (1, -1)}
FAR = {d: hops(128, lambda i, d=d: (SIDE if i // 16 % 2 else 1, d)) for d in (1, 2, -1)}


ORDER = [(2, 0), (2, 1)] + [(2, 2), (2, 3)] + [(1, 2), (1, 3)] + [(3, 0), (3, 1)]
ORDER += [(1, 0), (1, 1)] + [(3, 2), (3, 3)] + [(0, k) for k in range(SIDE)]


SOURCES = [(dz, dc) for dz in (0, -1, 1, 2) for dc in (0, 1)]


def place_table():
    table = np.zeros((8, 16, 16), np.int32)
    for vb in range(8):
        for ob in range(16):
            for a, (dz, dc) in enumerate(SOURCES):
                core = (vb % 2) ^ dc
                source = 2 * ((vb // 2 + (-dz if core else dz)) % SIDE) + core
                for h in range(2):
                    to = 2 * source + h
                    rel = (to // SIDE - ob // SIDE) % SIDE, (to - ob) % SIDE
                    table[vb, ob, 2 * a + h] = ORDER.index(rel[::-1] if vb % 2 else rel)
    return table


PLACES = place_table()
LEADS = (2, 2, 2, 2, 2, 2, 4)


def product_kernel(first, place, sizes, origin, *refs):
    pieces, v_ref, outs, (a_all, v_all) = refs[:8], refs[8], refs[-9:-2], refs[-2:]
    rows = pieces[0].shape[1] // 2
    depth = pieces[0].shape[2]
    for a, piece in enumerate(pieces):
        for h in range(2):
            block = piece[0, h * rows : (h + 1) * rows]
            hi = block.astype(jnp.bfloat16)
            at = pl.ds(pl.multiple_of(place[2 * a + h] * rows, rows), rows)
            a_all[at, 0:depth] = hi
            a_all[at, depth : 2 * depth] = (block - hi.astype(jnp.float32)).astype(jnp.bfloat16)
            a_all[at, 2 * depth : 3 * depth] = hi
    size = sizes[first + pl.program_id(0)]
    shape = v_ref.shape[1:]
    p = origin[0] + lax.broadcasted_iota(jnp.int32, shape, 0)
    q = origin[1] + lax.broadcasted_iota(jnp.int32, shape, 1)
    v = jnp.where((p < size) & (q < size), v_ref[0], 0.0)
    hi = v.astype(jnp.bfloat16)
    v_all[0:depth] = hi
    v_all[depth : 2 * depth] = hi
    v_all[2 * depth : 3 * depth] = (v - hi.astype(jnp.float32)).astype(jnp.bfloat16)
    blocks = [(out, k) for lead, out in zip(LEADS, outs) for k in range(lead)]
    for at in range(0, len(blocks), SIDE):
        acc = jnp.dot(a_all[rows * at : rows * (at + SIDE)], v_all[...], preferred_element_type=jnp.float32)
        for i, (out, k) in enumerate(blocks[at : at + SIDE]):
            out[k, 0] = acc[rows * i : rows * (i + 1)]


def product(pieces, ovov, first, count, place, sizes, origin, after):
    rows2, depth = pieces[0][0].shape[1:]
    rows = rows2 // 2
    cols = ovov.shape[2]
    return pl.pallas_call(
        functools.partial(product_kernel, first),
        grid_spec=pltpu.PrefetchScalarGridSpec(
            num_scalar_prefetch=3,
            grid=(count,),
            in_specs=[pl.BlockSpec((1, rows2, depth), lambda g, *_, at=at: (at + g, 0, 0)) for _, at in pieces]
            + [pl.BlockSpec((1, depth, cols), lambda g, *_: (first + g, 0, 0))]
            + [pl.BlockSpec(memory_space=pl.ANY)] * len(after),
            out_specs=[pl.BlockSpec((lead, 1, rows, cols), lambda g, *_: (0, g, 0, 0)) for lead in LEADS],
            scratch_shapes=[
                pltpu.VMEM((16 * rows, 3 * depth), jnp.bfloat16),
                pltpu.VMEM((3 * depth, cols), jnp.bfloat16),
            ],
        ),
        out_shape=[jax.ShapeDtypeStruct((lead, count, rows, cols), jnp.float32) for lead in LEADS],
        compiler_params=pltpu.CompilerParams(vmem_limit_bytes=VMEM),
        cost_estimate=LIGHT,
        name="product",
    )(place, sizes, origin, *[piece for piece, _ in pieces], ovov, *after)


def tie_kernel(*refs):
    pass


def tie(values, after):
    anywhere = pl.BlockSpec(memory_space=pl.ANY)
    return pl.pallas_call(
        tie_kernel,
        in_specs=[anywhere] * (len(values) + len(after)),
        out_specs=[anywhere] * len(values),
        out_shape=[jax.ShapeDtypeStruct(v.shape, v.dtype) for v in values],
        input_output_aliases={i: i for i in range(len(values))},
        compiler_params=pltpu.CompilerParams(vmem_limit_bytes=VMEM),
        cost_estimate=LIGHT,
        name="tie",
    )(*values, *after)


def add_kernel(up, down, recv_p, recv_m, *refs):
    refs[-2][...] = up[...] + recv_p[...]
    refs[-1][...] = down[...] + recv_m[...]


def add_far(up, down, recv_p, recv_m, after):
    lead, count, rows, cols = up.shape
    spec = pl.BlockSpec((lead, 1, rows, cols), lambda g: (0, g, 0, 0))
    return pl.pallas_call(
        add_kernel,
        grid=(count,),
        in_specs=[spec] * 4 + [pl.BlockSpec(memory_space=pl.ANY)] * len(after),
        out_specs=[spec] * 2,
        out_shape=[jax.ShapeDtypeStruct(up.shape, jnp.float32)] * 2,
        compiler_params=pltpu.CompilerParams(vmem_limit_bytes=VMEM),
        cost_estimate=LIGHT,
        name="add_far",
    )(up, down, recv_p, recv_m, *after)


def own_kernel(own, n1, n2, p2, m2, *refs):
    outs = refs[-4:]
    outs[0][0] = own[0, 0] + (p2[0, 0] + n2[0, 0])
    outs[1][0] = own[1, 0] + (p2[1, 0] + n2[1, 0])
    outs[2][0] = own[2, 0] + (m2[0, 0] + n1[0, 0])
    outs[3][0] = own[3, 0] + (m2[1, 0] + n1[1, 0])


def add_own(own, n1, n2, p2, m2, after):
    count, rows, cols = own.shape[1:]

    def spec(lead):
        return pl.BlockSpec((lead, 1, rows, cols), lambda g: (0, g, 0, 0))

    return pl.pallas_call(
        own_kernel,
        grid=(count,),
        in_specs=[spec(4)] + [spec(2)] * 4 + [pl.BlockSpec(memory_space=pl.ANY)] * len(after),
        out_specs=[pl.BlockSpec((1, rows, cols), lambda g: (g, 0, 0))] * 4,
        out_shape=[jax.ShapeDtypeStruct((count, rows, cols), jnp.float32)] * 4,
        compiler_params=pltpu.CompilerParams(vmem_limit_bytes=VMEM),
        cost_estimate=LIGHT,
        name="add_own",
    )(own, n1, n2, p2, m2, *after)


def finish_kernel(sizes, origin, *refs):
    out = refs[-1]
    rows, irreps, cols = out.shape
    row = origin[0] + lax.broadcasted_iota(jnp.int32, (rows, cols), 0)
    g = 0
    for i in range(0, len(refs) - 1, 4):
        a, b, c, d = refs[i : i + 4]
        for k in range(a.shape[0]):
            out[:, g, :] = jnp.where(row < sizes[g], (a[k] + b[k]) + (c[k] + d[k]), 0.0)
            g += 1


def finish(groups, row_sizes, origin, irreps):
    parts = [part for group in groups for part in group]
    _, rows, cols = parts[0].shape
    return pl.pallas_call(
        finish_kernel,
        grid_spec=pltpu.PrefetchScalarGridSpec(
            num_scalar_prefetch=2,
            grid=(cols // WIDTH,),
            in_specs=[pl.BlockSpec((part.shape[0], rows, WIDTH), lambda c, *_: (0, 0, c)) for part in parts],
            out_specs=pl.BlockSpec((rows, irreps, WIDTH), lambda c, *_: (0, 0, c)),
        ),
        out_shape=jax.ShapeDtypeStruct((rows, irreps, cols), jnp.float32),
        compiler_params=pltpu.CompilerParams(vmem_limit_bytes=VMEM),
        cost_estimate=LIGHT,
        name="finish",
    )(row_sizes, origin, *parts)


SPLIT = 4


def local(amplitudes, ovov, row_sizes, pair_sizes):
    ob = lax.axis_index("ob")
    vb = lax.axis_index("vb")
    local_rows, irreps, _ = amplitudes.shape
    obs = lax.axis_size("ob")
    depth, cols = ovov.shape[1:]
    out_rows = local_rows * lax.axis_size("vb")
    place = lax.dynamic_slice(jnp.asarray(PLACES), (vb, ob, 0), (1, 1, 16)).reshape(16)
    origin = jnp.stack([ob * depth, vb * cols]).astype(jnp.int32)

    mine = jnp.transpose(amplitudes.reshape(local_rows, irreps, obs, depth), (2, 0, 1, 3))
    mine = mine.reshape(obs, local_rows * irreps, depth)
    mine = lax.all_to_all(mine, "ob", split_axis=0, concat_axis=0, tiled=True)
    mine = mine.reshape(obs * local_rows, irreps, depth)
    early, late = jnp.transpose(mine[:, :SPLIT], (1, 0, 2)), jnp.transpose(mine[:, SPLIT:], (1, 0, 2))

    def swap(piece):
        return lax.ppermute(piece, "vb", SWAP)

    def along_z(held):
        return [lax.ppermute(held, "vb", steps) for steps in Z_STEPS]

    def multiply(held, moved, first):
        pieces = [(piece, 0) for whole in (held, *moved) for piece in (whole, swap(whole))]
        return product(pieces, ovov, first, held.shape[0], place, pair_sizes, origin, [])

    def to_neighbours(p, m):
        return lax.ppermute(p, BOTH, NEAR[1]), lax.ppermute(m, BOTH, NEAR[-1])

    def across(four):
        return [four[0]] + [lax.ppermute(four[k], BOTH, FAR[d]) for k, d in ((1, 1), (2, 2), (3, -1))]

    moved = along_z(early)
    (late,) = tie([late], moved)
    far_p, far_m, near_p, near_m, up, down, own = multiply(early, moved, 0)
    moved = tie(along_z(late), [far_p])
    late_far_p, late_far_m, late_near_p, late_near_m, late_up, late_down, late_own = multiply(late, moved, SPLIT)

    far, near = to_neighbours(far_p, far_m), to_neighbours(near_p, near_m)
    handed = to_neighbours(*add_far(up, down, *far, [late_far_p]))
    late_far, late_near = to_neighbours(late_far_p, late_far_m), to_neighbours(late_near_p, late_near_m)
    late_handed = to_neighbours(*add_far(late_up, late_down, *late_far, []))
    sums = across(add_own(own, *near, *handed, []))
    late_sums = across(add_own(late_own, *late_near, *late_handed, sums[1:]))
    origin = jnp.stack([ob * out_rows, vb * cols]).astype(jnp.int32)
    return finish([sums, late_sums], row_sizes, origin, irreps)


def solution(mesh):
    placed = (P(("vb", "ob"), None, None), P(None, "ob", "vb"), P(), P())
    return jax.shard_map(
        local, mesh=mesh, in_specs=placed, out_specs=P("ob", None, "vb"), check_vma=False
    )
```

```python
import functools

import jax
import jax.numpy as jnp
import numpy as np
from jax import lax
from jax.experimental import pallas as pl
from jax.experimental.pallas import tpu as pltpu
from jax.sharding import PartitionSpec as P

SIDE = 4
VMEM = 64 * 1024 * 1024 - 256 * 1024
HEIGHT = 16
LIGHT = pl.CostEstimate(flops=0, bytes_accessed=0, transcendentals=0)
def hops(count, steps):
    pairs = []
    for i in range(count):
        stride, delta = steps(i)
        at = (i // stride) % SIDE
        pairs.append((i, i + ((at + delta) % SIDE - at) * stride))
    return pairs


Z_STEPS = [hops(8, lambda i, d=d: (2, -d if i % 2 else d)) for d in (1, -1, 2)]
SWAP = [(i, i ^ 1) for i in range(8)]
BOTH = ("vb", "ob")
NEAR = {d: hops(128, lambda i, d=d: (1 if i // 16 % 2 else SIDE, d)) for d in (1, -1)}
FAR = {d: hops(128, lambda i, d=d: (SIDE if i // 16 % 2 else 1, d)) for d in (1, 2, -1)}


ORDER = [(2, 0), (2, 1), (1, 2), (1, 3)] + [(2, 2), (2, 3), (3, 0), (3, 1)]
ORDER += [(1, 0), (1, 1)] + [(3, 2), (3, 3)] + [(0, k) for k in range(SIDE)]


SOURCES = [(dz, dc) for dz in (0, -1, 1, 2) for dc in (0, 1)]


def place_table():
    table = np.zeros((8, 16, 16), np.int32)
    for vb in range(8):
        for ob in range(16):
            for a, (dz, dc) in enumerate(SOURCES):
                core = (vb % 2) ^ dc
                source = 2 * ((vb // 2 + (-dz if core else dz)) % SIDE) + core
                for h in range(2):
                    to = 2 * source + h
                    rel = (to // SIDE - ob // SIDE) % SIDE, (to - ob) % SIDE
                    table[vb, ob, 2 * a + h] = ORDER.index(rel[::-1] if vb % 2 else rel)
    return table


PLACES = place_table()
LEADS = (4, 4, 2, 2, 4)


def product_kernel(first, place, sizes, origin, *refs):
    pieces, v_ref, outs, (a_all, v_all) = refs[:8], refs[8], refs[-7:-2], refs[-2:]
    rows = pieces[0].shape[1] // 2
    depth = pieces[0].shape[2]
    for a, piece in enumerate(pieces):
        for h in range(2):
            block = piece[0, h * rows : (h + 1) * rows]
            hi = block.astype(jnp.bfloat16)
            at = pl.ds(pl.multiple_of(place[2 * a + h] * rows, rows), rows)
            a_all[at, 0:depth] = hi
            a_all[at, depth : 2 * depth] = (block - hi.astype(jnp.float32)).astype(jnp.bfloat16)
            a_all[at, 2 * depth : 3 * depth] = hi
    size = sizes[first + pl.program_id(0)]
    shape = v_ref.shape[1:]
    p = origin[0] + lax.broadcasted_iota(jnp.int32, shape, 0)
    q = origin[1] + lax.broadcasted_iota(jnp.int32, shape, 1)
    v = jnp.where((p < size) & (q < size), v_ref[0], 0.0)
    hi = v.astype(jnp.bfloat16)
    v_all[0:depth] = hi
    v_all[depth : 2 * depth] = hi
    v_all[2 * depth : 3 * depth] = (v - hi.astype(jnp.float32)).astype(jnp.bfloat16)
    blocks = [(out, k) for lead, out in zip(LEADS, outs) for k in range(lead)]
    for at in range(0, len(blocks), SIDE):
        acc = jnp.dot(a_all[rows * at : rows * (at + SIDE)], v_all[...], preferred_element_type=jnp.float32)
        for i, (out, k) in enumerate(blocks[at : at + SIDE]):
            out[k, 0] = acc[rows * i : rows * (i + 1)]


def product(pieces, ovov, first, count, place, sizes, origin, after):
    rows2, depth = pieces[0][0].shape[1:]
    rows = rows2 // 2
    cols = ovov.shape[2]
    return pl.pallas_call(
        functools.partial(product_kernel, first),
        grid_spec=pltpu.PrefetchScalarGridSpec(
            num_scalar_prefetch=3,
            grid=(count,),
            in_specs=[pl.BlockSpec((1, rows2, depth), lambda g, *_, at=at: (at + g, 0, 0)) for _, at in pieces]
            + [pl.BlockSpec((1, depth, cols), lambda g, *_: (first + g, 0, 0))]
            + [pl.BlockSpec(memory_space=pl.ANY)] * len(after),
            out_specs=[pl.BlockSpec((lead, 1, rows, cols), lambda g, *_: (0, g, 0, 0)) for lead in LEADS],
            scratch_shapes=[
                pltpu.VMEM((16 * rows, 3 * depth), jnp.bfloat16),
                pltpu.VMEM((3 * depth, cols), jnp.bfloat16),
            ],
        ),
        out_shape=[jax.ShapeDtypeStruct((lead, count, rows, cols), jnp.float32) for lead in LEADS],
        compiler_params=pltpu.CompilerParams(vmem_limit_bytes=VMEM),
        cost_estimate=LIGHT,
        name="product",
    )(place, sizes, origin, *[piece for piece, _ in pieces], ovov, *after)


def tie_kernel(*refs):
    pass


def tie(values, after):
    anywhere = pl.BlockSpec(memory_space=pl.ANY)
    return pl.pallas_call(
        tie_kernel,
        in_specs=[anywhere] * (len(values) + len(after)),
        out_specs=[anywhere] * len(values),
        out_shape=[jax.ShapeDtypeStruct(v.shape, v.dtype) for v in values],
        input_output_aliases={i: i for i in range(len(values))},
        compiler_params=pltpu.CompilerParams(vmem_limit_bytes=VMEM),
        cost_estimate=LIGHT,
        name="tie",
    )(*values, *after)


def add_kernel(up, down, recv_p, recv_m, *refs):
    refs[-2][...] = up[...] + recv_p[...]
    refs[-1][...] = down[...] + recv_m[...]


def add_far(up, down, recv_p, recv_m, after):
    lead, count, rows, cols = up.shape
    spec = pl.BlockSpec((lead, 1, rows, cols), lambda g: (0, g, 0, 0))
    return pl.pallas_call(
        add_kernel,
        grid=(count,),
        in_specs=[spec] * 4 + [pl.BlockSpec(memory_space=pl.ANY)] * len(after),
        out_specs=[spec] * 2,
        out_shape=[jax.ShapeDtypeStruct(up.shape, jnp.float32)] * 2,
        compiler_params=pltpu.CompilerParams(vmem_limit_bytes=VMEM),
        cost_estimate=LIGHT,
        name="add_far",
    )(up, down, recv_p, recv_m, *after)


def own_kernel(own, p1, m1, p2, m2, *refs):
    outs = refs[-4:]
    outs[0][0] = own[0, 0] + (p2[0, 0] + m1[0, 0])
    outs[1][0] = own[1, 0] + (p2[1, 0] + m1[1, 0])
    outs[2][0] = own[2, 0] + (m2[0, 0] + p1[0, 0])
    outs[3][0] = own[3, 0] + (m2[1, 0] + p1[1, 0])


def add_own(own, p1, m1, p2, m2, after):
    count, rows, cols = own.shape[1:]

    def spec(lead, at=0):
        return pl.BlockSpec((lead, 1, rows, cols), lambda g: (at, g, 0, 0))

    return pl.pallas_call(
        own_kernel,
        grid=(count,),
        in_specs=[spec(4), spec(2, 1), spec(2, 1), spec(2), spec(2)] + [pl.BlockSpec(memory_space=pl.ANY)] * len(after),
        out_specs=[pl.BlockSpec((1, rows, cols), lambda g: (g, 0, 0))] * 4,
        out_shape=[jax.ShapeDtypeStruct((count, rows, cols), jnp.float32)] * 4,
        compiler_params=pltpu.CompilerParams(vmem_limit_bytes=VMEM),
        cost_estimate=LIGHT,
        name="add_own",
    )(own, p1, m1, p2, m2, *after)


def finish_kernel(sizes, origin, *refs):
    out = refs[-1]
    rows, irreps, cols = out.shape
    row = origin[0] + pl.program_id(0) * HEIGHT + lax.broadcasted_iota(jnp.int32, (rows, cols), 0)
    g = 0
    for i in range(0, len(refs) - 1, 4):
        a, b, c, d = refs[i : i + 4]
        for k in range(a.shape[0]):
            out[:, g, :] = jnp.where(row < sizes[g], (a[k] + b[k]) + (c[k] + d[k]), 0.0)
            g += 1


def finish(groups, row_sizes, origin, irreps):
    parts = [part for group in groups for part in group]
    _, rows, cols = parts[0].shape
    return pl.pallas_call(
        finish_kernel,
        grid_spec=pltpu.PrefetchScalarGridSpec(
            num_scalar_prefetch=2,
            grid=(rows // HEIGHT,),
            in_specs=[pl.BlockSpec((part.shape[0], HEIGHT, cols), lambda r, *_: (0, r, 0)) for part in parts],
            out_specs=pl.BlockSpec((HEIGHT, irreps, cols), lambda r, *_: (r, 0, 0)),
        ),
        out_shape=jax.ShapeDtypeStruct((rows, irreps, cols), jnp.float32),
        compiler_params=pltpu.CompilerParams(vmem_limit_bytes=VMEM),
        cost_estimate=LIGHT,
        name="finish",
    )(row_sizes, origin, *parts)


SPLIT = 4


def local(amplitudes, ovov, row_sizes, pair_sizes):
    ob = lax.axis_index("ob")
    vb = lax.axis_index("vb")
    local_rows, irreps, _ = amplitudes.shape
    obs = lax.axis_size("ob")
    depth, cols = ovov.shape[1:]
    out_rows = local_rows * lax.axis_size("vb")
    place = lax.dynamic_slice(jnp.asarray(PLACES), (vb, ob, 0), (1, 1, 16)).reshape(16)
    origin = jnp.stack([ob * depth, vb * cols]).astype(jnp.int32)

    mine = jnp.transpose(amplitudes.reshape(local_rows, irreps, obs, depth), (2, 0, 1, 3))
    mine = mine.reshape(obs, local_rows * irreps, depth)
    mine = lax.all_to_all(mine, "ob", split_axis=0, concat_axis=0, tiled=True)
    mine = mine.reshape(obs * local_rows, irreps, depth)
    early, late = jnp.transpose(mine[:, :SPLIT], (1, 0, 2)), jnp.transpose(mine[:, SPLIT:], (1, 0, 2))

    def swap(piece):
        return lax.ppermute(piece, "vb", SWAP)

    def along_z(held):
        return [lax.ppermute(held, "vb", steps) for steps in Z_STEPS]

    def multiply(held, moved, first, after):
        pieces = [(piece, 0) for whole in (held, *moved) for piece in (whole, swap(whole))]
        return product(pieces, ovov, first, held.shape[0], place, pair_sizes, origin, after)

    def to_neighbours(p, m):
        return lax.ppermute(p, BOTH, NEAR[1]), lax.ppermute(m, BOTH, NEAR[-1])

    def across(four):
        return [four[0]] + [lax.ppermute(four[k], BOTH, FAR[d]) for k, d in ((1, 1), (2, 2), (3, -1))]

    moved = along_z(early)
    (late,) = tie([late], moved)
    send_p, send_m, up, down, own = multiply(early, moved, 0, [])
    late, *moved = tie([late, *along_z(late)], [send_p])
    late_send_p, late_send_m, late_up, late_down, late_own = multiply(late, moved, SPLIT, [])

    got = to_neighbours(send_p, send_m)
    handed = to_neighbours(*add_far(up, down, *got, [late_send_p]))
    late_got = to_neighbours(late_send_p, late_send_m)
    late_handed = to_neighbours(*add_far(late_up, late_down, *late_got, []))
    sums = across(add_own(own, *got, *handed, []))
    late_sums = across(add_own(late_own, *late_got, *late_handed, sums[1:2]))
    origin = jnp.stack([ob * out_rows, vb * cols]).astype(jnp.int32)
    return finish([sums, late_sums], row_sizes, origin, irreps)


def solution(mesh):
    placed = (P(("vb", "ob"), None, None), P(None, "ob", "vb"), P(), P())
    return jax.shard_map(
        local, mesh=mesh, in_specs=placed, out_specs=P("ob", None, "vb"), check_vma=False
    )
```

```python
import functools

import jax
import jax.numpy as jnp
import numpy as np
from jax import lax
from jax.experimental import pallas as pl
from jax.experimental.pallas import tpu as pltpu
from jax.sharding import PartitionSpec as P

SIDE = 4
VMEM = 64 * 1024 * 1024 - 256 * 1024
STEP = 2
LIGHT = pl.CostEstimate(flops=0, bytes_accessed=0, transcendentals=0)
def hops(count, steps):
    pairs = []
    for i in range(count):
        stride, delta = steps(i)
        at = (i // stride) % SIDE
        pairs.append((i, i + ((at + delta) % SIDE - at) * stride))
    return pairs


Z_STEPS = [hops(8, lambda i, d=d: (2, -d if i % 2 else d)) for d in (1, -1, 2)]
SWAP = [(i, i ^ 1) for i in range(8)]
BOTH = ("vb", "ob")
NEAR = {d: hops(128, lambda i, d=d: (1 if i // 16 % 2 else SIDE, d)) for d in (1, -1)}
FAR = {d: hops(128, lambda i, d=d: (SIDE if i // 16 % 2 else 1, d)) for d in (1, 2, -1)}


ORDER = [(2, 0), (2, 1)] + [(2, 2), (2, 3)] + [(1, 2), (1, 3)] + [(3, 0), (3, 1)]
ORDER += [(1, 0), (1, 1)] + [(3, 2), (3, 3)] + [(0, k) for k in range(SIDE)]


SOURCES = [(dz, dc) for dz in (0, -1, 1, 2) for dc in (0, 1)]


def place_table():
    table = np.zeros((8, 16, 16), np.int32)
    for vb in range(8):
        for ob in range(16):
            for a, (dz, dc) in enumerate(SOURCES):
                core = (vb % 2) ^ dc
                source = 2 * ((vb // 2 + (-dz if core else dz)) % SIDE) + core
                for h in range(2):
                    to = 2 * source + h
                    rel = (to // SIDE - ob // SIDE) % SIDE, (to - ob) % SIDE
                    table[vb, ob, 2 * a + h] = ORDER.index(rel[::-1] if vb % 2 else rel)
    return table


PLACES = place_table()
LEADS = (2, 2, 2, 2, 2, 2, 4)


def product_kernel(first, place, sizes, origin, *refs):
    pieces, v_ref, outs, (a_all, v_all) = refs[:8], refs[8], refs[-9:-2], refs[-2:]
    rows = pieces[0].shape[1] // 2
    depth = pieces[0].shape[2]
    for a, piece in enumerate(pieces):
        for h in range(2):
            block = piece[0, h * rows : (h + 1) * rows]
            hi = block.astype(jnp.bfloat16)
            at = pl.ds(pl.multiple_of(place[2 * a + h] * rows, rows), rows)
            a_all[at, 0:depth] = hi
            a_all[at, depth : 2 * depth] = (block - hi.astype(jnp.float32)).astype(jnp.bfloat16)
            a_all[at, 2 * depth : 3 * depth] = hi
    size = sizes[first + pl.program_id(0)]
    shape = v_ref.shape[1:]
    p = origin[0] + lax.broadcasted_iota(jnp.int32, shape, 0)
    q = origin[1] + lax.broadcasted_iota(jnp.int32, shape, 1)
    v = jnp.where((p < size) & (q < size), v_ref[0], 0.0)
    hi = v.astype(jnp.bfloat16)
    v_all[0:depth] = hi
    v_all[depth : 2 * depth] = hi
    v_all[2 * depth : 3 * depth] = (v - hi.astype(jnp.float32)).astype(jnp.bfloat16)
    blocks = [(out, k) for lead, out in zip(LEADS, outs) for k in range(lead)]
    for at in range(0, len(blocks), SIDE):
        acc = jnp.dot(a_all[rows * at : rows * (at + SIDE)], v_all[...], preferred_element_type=jnp.float32)
        for i, (out, k) in enumerate(blocks[at : at + SIDE]):
            out[k, 0] = acc[rows * i : rows * (i + 1)]


def product(pieces, ovov, first, count, place, sizes, origin, after):
    rows2, depth = pieces[0][0].shape[1:]
    rows = rows2 // 2
    cols = ovov.shape[2]
    return pl.pallas_call(
        functools.partial(product_kernel, first),
        grid_spec=pltpu.PrefetchScalarGridSpec(
            num_scalar_prefetch=3,
            grid=(count,),
            in_specs=[pl.BlockSpec((1, rows2, depth), lambda g, *_, at=at: (at + g, 0, 0)) for _, at in pieces]
            + [pl.BlockSpec((1, depth, cols), lambda g, *_: (first + g, 0, 0))]
            + [pl.BlockSpec(memory_space=pl.ANY)] * len(after),
            out_specs=[pl.BlockSpec((lead, 1, rows, cols), lambda g, *_: (0, g, 0, 0)) for lead in LEADS],
            scratch_shapes=[
                pltpu.VMEM((16 * rows, 3 * depth), jnp.bfloat16),
                pltpu.VMEM((3 * depth, cols), jnp.bfloat16),
            ],
        ),
        out_shape=[jax.ShapeDtypeStruct((lead, count, rows, cols), jnp.float32) for lead in LEADS],
        compiler_params=pltpu.CompilerParams(vmem_limit_bytes=VMEM),
        cost_estimate=LIGHT,
        name="product",
    )(place, sizes, origin, *[piece for piece, _ in pieces], ovov, *after)


def tie_kernel(*refs):
    pass


def tie(values, after):
    anywhere = pl.BlockSpec(memory_space=pl.ANY)
    return pl.pallas_call(
        tie_kernel,
        in_specs=[anywhere] * (len(values) + len(after)),
        out_specs=[anywhere] * len(values),
        out_shape=[jax.ShapeDtypeStruct(v.shape, v.dtype) for v in values],
        input_output_aliases={i: i for i in range(len(values))},
        compiler_params=pltpu.CompilerParams(vmem_limit_bytes=VMEM),
        cost_estimate=LIGHT,
        name="tie",
    )(*values, *after)


def add_kernel(up, down, recv_p, recv_m, *refs):
    refs[-2][...] = up[...] + recv_p[...]
    refs[-1][...] = down[...] + recv_m[...]


def add_far(up, down, recv_p, recv_m, after):
    lead, count, rows, cols = up.shape
    spec = pl.BlockSpec((lead, STEP, rows, cols), lambda g: (0, g, 0, 0))
    return pl.pallas_call(
        add_kernel,
        grid=(count // STEP,),
        in_specs=[spec] * 4 + [pl.BlockSpec(memory_space=pl.ANY)] * len(after),
        out_specs=[spec] * 2,
        out_shape=[jax.ShapeDtypeStruct(up.shape, jnp.float32)] * 2,
        compiler_params=pltpu.CompilerParams(vmem_limit_bytes=VMEM),
        cost_estimate=LIGHT,
        name="add_far",
    )(up, down, recv_p, recv_m, *after)


def own_kernel(own, n1, n2, p2, m2, *refs):
    outs = refs[-4:]
    outs[0][...] = own[0] + (p2[0] + n2[0])
    outs[1][...] = own[1] + (p2[1] + n2[1])
    outs[2][...] = own[2] + (m2[0] + n1[0])
    outs[3][...] = own[3] + (m2[1] + n1[1])


def add_own(own, n1, n2, p2, m2, after):
    count, rows, cols = own.shape[1:]

    def spec(lead):
        return pl.BlockSpec((lead, STEP, rows, cols), lambda g: (0, g, 0, 0))

    return pl.pallas_call(
        own_kernel,
        grid=(count // STEP,),
        in_specs=[spec(4)] + [spec(2)] * 4 + [pl.BlockSpec(memory_space=pl.ANY)] * len(after),
        out_specs=[pl.BlockSpec((STEP, rows, cols), lambda g: (g, 0, 0))] * 4,
        out_shape=[jax.ShapeDtypeStruct((count, rows, cols), jnp.float32)] * 4,
        compiler_params=pltpu.CompilerParams(vmem_limit_bytes=VMEM),
        cost_estimate=LIGHT,
        name="add_own",
    )(own, n1, n2, p2, m2, *after)


def finish_kernel(sizes, origin, *refs):
    out = refs[-1]
    rows, irreps, cols = out.shape
    row = origin[0] + lax.broadcasted_iota(jnp.int32, (rows, cols), 0)
    g = 0
    for i in range(0, len(refs) - 1, 4):
        a, b, c, d = refs[i : i + 4]
        for k in range(a.shape[0]):
            out[:, g, :] = jnp.where(row < sizes[g], (a[k] + b[k]) + (c[k] + d[k]), 0.0)
            g += 1


def finish(groups, row_sizes, origin, irreps):
    parts = [part for group in groups for part in group]
    _, rows, cols = parts[0].shape
    return pl.pallas_call(
        finish_kernel,
        grid_spec=pltpu.PrefetchScalarGridSpec(
            num_scalar_prefetch=2,
            grid=(1,),
            in_specs=[pl.BlockSpec(part.shape, lambda r, *_: (0, 0, 0)) for part in parts],
            out_specs=pl.BlockSpec((rows, irreps, cols), lambda r, *_: (0, 0, 0)),
        ),
        out_shape=jax.ShapeDtypeStruct((rows, irreps, cols), jnp.float32),
        compiler_params=pltpu.CompilerParams(vmem_limit_bytes=VMEM),
        cost_estimate=LIGHT,
        name="finish",
    )(row_sizes, origin, *parts)


SPLIT = 4


def local(amplitudes, ovov, row_sizes, pair_sizes):
    ob = lax.axis_index("ob")
    vb = lax.axis_index("vb")
    local_rows, irreps, _ = amplitudes.shape
    obs = lax.axis_size("ob")
    depth, cols = ovov.shape[1:]
    out_rows = local_rows * lax.axis_size("vb")
    place = lax.dynamic_slice(jnp.asarray(PLACES), (vb, ob, 0), (1, 1, 16)).reshape(16)
    origin = jnp.stack([ob * depth, vb * cols]).astype(jnp.int32)

    mine = jnp.transpose(amplitudes.reshape(local_rows, irreps, obs, depth), (2, 0, 1, 3))
    mine = mine.reshape(obs, local_rows * irreps, depth)
    mine = lax.all_to_all(mine, "ob", split_axis=0, concat_axis=0, tiled=True)
    mine = mine.reshape(obs * local_rows, irreps, depth)
    early, late = jnp.transpose(mine[:, :SPLIT], (1, 0, 2)), jnp.transpose(mine[:, SPLIT:], (1, 0, 2))

    def swap(piece):
        return lax.ppermute(piece, "vb", SWAP)

    def along_z(held):
        return [lax.ppermute(held, "vb", steps) for steps in Z_STEPS]

    def multiply(held, swapped, moved, moved_swapped, first, after):
        pieces = [(held, 0), (swapped, 0)] + [(piece, 0) for pair in zip(moved, moved_swapped) for piece in pair]
        return product(pieces, ovov, first, held.shape[0], place, pair_sizes, origin, after)

    def to_neighbours(p, m):
        return lax.ppermute(p, BOTH, NEAR[1]), lax.ppermute(m, BOTH, NEAR[-1])

    def across(four):
        return [four[0]] + [lax.ppermute(four[k], BOTH, FAR[d]) for k, d in ((1, 1), (2, 2), (3, -1))]

    late_swapped = swap(late)
    moved = along_z(early)
    (late,) = tie([late], moved)
    far_p, far_m, near_p, near_m, up, down, own = multiply(early, swap(early), moved, [swap(piece) for piece in moved], 0, [late_swapped])
    far, near = to_neighbours(far_p, far_m), to_neighbours(near_p, near_m)
    up_z, down_z, far_z = along_z(late)
    down_z, far_z = tie([down_z, far_z], [far_p])
    down_swapped, far_swapped = swap(down_z), swap(far_z)
    (up_z,) = tie([up_z], [*far, down_swapped])
    late_far_p, late_far_m, late_near_p, late_near_m, late_up, late_down, late_own = multiply(
        late, late_swapped, (up_z, down_z, far_z), (swap(up_z), down_swapped, far_swapped), SPLIT, []
    )

    handed = to_neighbours(*add_far(up, down, *far, [late_far_p, *near]))
    late_far, late_near = to_neighbours(late_far_p, late_far_m), to_neighbours(late_near_p, late_near_m)
    late_handed = to_neighbours(*add_far(late_up, late_down, *late_far, []))
    sums = across(add_own(own, *near, *handed, []))
    late_sums = across(add_own(late_own, *late_near, *late_handed, sums[1:2]))
    origin = jnp.stack([ob * out_rows, vb * cols]).astype(jnp.int32)
    return finish([sums, late_sums], row_sizes, origin, irreps)


def solution(mesh):
    placed = (P(("vb", "ob"), None, None), P(None, "ob", "vb"), P(), P())
    return jax.shard_map(
        local, mesh=mesh, in_specs=placed, out_specs=P("ob", None, "vb"), check_vma=False
    )
```

```python
import functools

import jax
import jax.numpy as jnp
import numpy as np
from jax import lax
from jax.experimental import pallas as pl
from jax.experimental.pallas import tpu as pltpu
from jax.sharding import PartitionSpec as P

SIDE = 4
VMEM = 64 * 1024 * 1024 - 256 * 1024
LIGHT = pl.CostEstimate(flops=0, bytes_accessed=0, transcendentals=0)
def hops(count, steps):
    pairs = []
    for i in range(count):
        stride, delta = steps(i)
        at = (i // stride) % SIDE
        pairs.append((i, i + ((at + delta) % SIDE - at) * stride))
    return pairs


Z_stepS = [hops(8, lambda i, d=d: (2, -d if i % 2 else d)) for d in (1, -1, 2)]
SWAP = [(i, i ^ 1) for i in range(8)]
BOTH = ("vb", "ob")
NEAR = {d: hops(128, lambda i, d=d: (1 if i // 16 % 2 else SIDE, d)) for d in (1, -1)}
FAR = {d: hops(128, lambda i, d=d: (SIDE if i // 16 % 2 else 1, d)) for d in (1, 2, -1)}


ORDER = [(2, 0), (2, 1)] + [(2, 2), (2, 3)] + [(1, 2), (1, 3)] + [(3, 0), (3, 1)]
ORDER += [(1, 0), (1, 1)] + [(3, 2), (3, 3)] + [(0, k) for k in range(SIDE)]


SOURCES = [(dz, dc) for dz in (0, -1, 1, 2) for dc in (0, 1)]


def place_table():
    table = np.zeros((8, 16, 16), np.int32)
    for vb in range(8):
        for ob in range(16):
            for a, (dz, dc) in enumerate(SOURCES):
                core = (vb % 2) ^ dc
                source = 2 * ((vb // 2 + (-dz if core else dz)) % SIDE) + core
                for h in range(2):
                    to = 2 * source + h
                    rel = (to // SIDE - ob // SIDE) % SIDE, (to - ob) % SIDE
                    table[vb, ob, 2 * a + h] = ORDER.index(rel[::-1] if vb % 2 else rel)
    return table


PLACES = place_table()
LEADS = (2, 2, 2, 2, 2, 2, 4)


def product_kernel(first, place, sizes, origin, *refs):
    pieces, v_ref, outs, (a_all, v_all) = refs[:8], refs[8], refs[-9:-2], refs[-2:]
    rows = pieces[0].shape[1] // 2
    depth = pieces[0].shape[2]
    for a, piece in enumerate(pieces):
        for h in range(2):
            block = piece[0, h * rows : (h + 1) * rows]
            hi = block.astype(jnp.bfloat16)
            at = pl.ds(pl.multiple_of(place[2 * a + h] * rows, rows), rows)
            a_all[at, 0:depth] = hi
            a_all[at, depth : 2 * depth] = (block - hi.astype(jnp.float32)).astype(jnp.bfloat16)
            a_all[at, 2 * depth : 3 * depth] = hi
    size = sizes[first + pl.program_id(0)]
    shape = v_ref.shape[1:]
    p = origin[0] + lax.broadcasted_iota(jnp.int32, shape, 0)
    q = origin[1] + lax.broadcasted_iota(jnp.int32, shape, 1)
    v = jnp.where((p < size) & (q < size), v_ref[0], 0.0)
    hi = v.astype(jnp.bfloat16)
    v_all[0:depth] = hi
    v_all[depth : 2 * depth] = hi
    v_all[2 * depth : 3 * depth] = (v - hi.astype(jnp.float32)).astype(jnp.bfloat16)
    blocks = [(out, k) for lead, out in zip(LEADS, outs) for k in range(lead)]
    for at in range(0, len(blocks), SIDE):
        acc = jnp.dot(a_all[rows * at : rows * (at + SIDE)], v_all[...], preferred_element_type=jnp.float32)
        for i, (out, k) in enumerate(blocks[at : at + SIDE]):
            out[k, 0] = acc[rows * i : rows * (i + 1)]


def product(pieces, ovov, first, count, place, sizes, origin, after):
    rows2, depth = pieces[0][0].shape[1:]
    rows = rows2 // 2
    cols = ovov.shape[2]
    return pl.pallas_call(
        functools.partial(product_kernel, first),
        grid_spec=pltpu.PrefetchScalarGridSpec(
            num_scalar_prefetch=3,
            grid=(count,),
            in_specs=[pl.BlockSpec((1, rows2, depth), lambda g, *_, at=at: (at + g, 0, 0)) for _, at in pieces]
            + [pl.BlockSpec((1, depth, cols), lambda g, *_: (first + g, 0, 0))]
            + [pl.BlockSpec(memory_space=pl.ANY)] * len(after),
            out_specs=[pl.BlockSpec((lead, 1, rows, cols), lambda g, *_: (0, g, 0, 0)) for lead in LEADS],
            scratch_shapes=[
                pltpu.VMEM((16 * rows, 3 * depth), jnp.bfloat16),
                pltpu.VMEM((3 * depth, cols), jnp.bfloat16),
            ],
        ),
        out_shape=[jax.ShapeDtypeStruct((lead, count, rows, cols), jnp.float32) for lead in LEADS],
        compiler_params=pltpu.CompilerParams(vmem_limit_bytes=VMEM),
        cost_estimate=LIGHT,
        name="product",
    )(place, sizes, origin, *[piece for piece, _ in pieces], ovov, *after)


def tie_kernel(*refs):
    pass


def tie(values, after):
    anywhere = pl.BlockSpec(memory_space=pl.ANY)
    return pl.pallas_call(
        tie_kernel,
        in_specs=[anywhere] * (len(values) + len(after)),
        out_specs=[anywhere] * len(values),
        out_shape=[jax.ShapeDtypeStruct(v.shape, v.dtype) for v in values],
        input_output_aliases={i: i for i in range(len(values))},
        compiler_params=pltpu.CompilerParams(vmem_limit_bytes=VMEM),
        cost_estimate=LIGHT,
        name="tie",
    )(*values, *after)


def add_kernel(up, down, recv_p, recv_m, *refs):
    refs[-2][...] = up[...] + recv_p[...]
    refs[-1][...] = down[...] + recv_m[...]


def add_far(up, down, recv_p, recv_m, after):
    lead, count, rows, cols = up.shape
    step = 1 if count % 2 else 2
    spec = pl.BlockSpec((lead, step, rows, cols), lambda g: (0, g, 0, 0))
    return pl.pallas_call(
        add_kernel,
        grid=(count // step,),
        in_specs=[spec] * 4 + [pl.BlockSpec(memory_space=pl.ANY)] * len(after),
        out_specs=[spec] * 2,
        out_shape=[jax.ShapeDtypeStruct(up.shape, jnp.float32)] * 2,
        compiler_params=pltpu.CompilerParams(vmem_limit_bytes=VMEM),
        cost_estimate=LIGHT,
        name="add_far",
    )(up, down, recv_p, recv_m, *after)


def own_kernel(own, n1, n2, p2, m2, *refs):
    outs = refs[-4:]
    outs[0][...] = own[0] + (p2[0] + n2[0])
    outs[1][...] = own[1] + (p2[1] + n2[1])
    outs[2][...] = own[2] + (m2[0] + n1[0])
    outs[3][...] = own[3] + (m2[1] + n1[1])


def add_own(own, n1, n2, p2, m2, after):
    count, rows, cols = own.shape[1:]
    step = 1 if count % 2 else 2

    def spec(lead):
        return pl.BlockSpec((lead, step, rows, cols), lambda g: (0, g, 0, 0))

    return pl.pallas_call(
        own_kernel,
        grid=(count // step,),
        in_specs=[spec(4)] + [spec(2)] * 4 + [pl.BlockSpec(memory_space=pl.ANY)] * len(after),
        out_specs=[pl.BlockSpec((step, rows, cols), lambda g: (g, 0, 0))] * 4,
        out_shape=[jax.ShapeDtypeStruct((count, rows, cols), jnp.float32)] * 4,
        compiler_params=pltpu.CompilerParams(vmem_limit_bytes=VMEM),
        cost_estimate=LIGHT,
        name="add_own",
    )(own, n1, n2, p2, m2, *after)


def finish_kernel(sizes, origin, *refs):
    out = refs[-1]
    rows, irreps, cols = out.shape
    row = origin[0] + lax.broadcasted_iota(jnp.int32, (rows, cols), 0)
    g = 0
    for i in range(0, len(refs) - 1, 4):
        a, b, c, d = refs[i : i + 4]
        for k in range(a.shape[0]):
            out[:, g, :] = jnp.where(row < sizes[g], (a[k] + b[k]) + (c[k] + d[k]), 0.0)
            g += 1


def finish(groups, row_sizes, origin, irreps):
    parts = [part for group in groups for part in group]
    _, rows, cols = parts[0].shape
    return pl.pallas_call(
        finish_kernel,
        grid_spec=pltpu.PrefetchScalarGridSpec(
            num_scalar_prefetch=2,
            grid=(1,),
            in_specs=[pl.BlockSpec(part.shape, lambda r, *_: (0, 0, 0)) for part in parts],
            out_specs=pl.BlockSpec((rows, irreps, cols), lambda r, *_: (0, 0, 0)),
        ),
        out_shape=jax.ShapeDtypeStruct((rows, irreps, cols), jnp.float32),
        compiler_params=pltpu.CompilerParams(vmem_limit_bytes=VMEM),
        cost_estimate=LIGHT,
        name="finish",
    )(row_sizes, origin, *parts)


SPLIT = 4


def local(amplitudes, ovov, row_sizes, pair_sizes):
    ob = lax.axis_index("ob")
    vb = lax.axis_index("vb")
    local_rows, irreps, _ = amplitudes.shape
    obs = lax.axis_size("ob")
    depth, cols = ovov.shape[1:]
    out_rows = local_rows * lax.axis_size("vb")
    place = lax.dynamic_slice(jnp.asarray(PLACES), (vb, ob, 0), (1, 1, 16)).reshape(16)
    origin = jnp.stack([ob * depth, vb * cols]).astype(jnp.int32)

    def exchange(part):
        count = part.shape[1]
        part = jnp.transpose(part.reshape(local_rows, count, obs, depth), (2, 0, 1, 3))
        part = part.reshape(obs, local_rows * count, depth)
        part = lax.all_to_all(part, "ob", split_axis=0, concat_axis=0, tiled=True)
        return jnp.transpose(part.reshape(obs * local_rows, count, depth), (1, 0, 2))

    early, late = exchange(amplitudes[:, :SPLIT]), exchange(amplitudes[:, SPLIT:])

    def swap(piece):
        return lax.ppermute(piece, "vb", SWAP)

    def along_z(held):
        return [lax.ppermute(held, "vb", steps) for steps in Z_stepS]

    def multiply(held, swapped, moved, moved_swapped, first, after):
        pieces = [(held, 0), (swapped, 0)] + [(piece, 0) for pair in zip(moved, moved_swapped) for piece in pair]
        return product(pieces, ovov, first, held.shape[0], place, pair_sizes, origin, after)

    def to_neighbours(p, m):
        return lax.ppermute(p, BOTH, NEAR[1]), lax.ppermute(m, BOTH, NEAR[-1])

    def across(four):
        return [four[0]] + [lax.ppermute(four[k], BOTH, FAR[d]) for k, d in ((1, 1), (2, 2), (3, -1))]

    late_swapped = swap(late)
    moved = along_z(early)
    (late,) = tie([late], moved)
    far_p, far_m, near_p, near_m, up, down, own = multiply(early, swap(early), moved, [swap(piece) for piece in moved], 0, [late_swapped])
    far, near = to_neighbours(far_p, far_m), to_neighbours(near_p, near_m)
    up_z, down_z, far_z = along_z(late)
    down_z, far_z = tie([down_z, far_z], [far_p])
    down_swapped, far_swapped = swap(down_z), swap(far_z)
    (up_z,) = tie([up_z], [*far, down_swapped])
    late_far_p, late_far_m, late_near_p, late_near_m, late_up, late_down, late_own = multiply(
        late, late_swapped, (up_z, down_z, far_z), (swap(up_z), down_swapped, far_swapped), SPLIT, []
    )

    handed = to_neighbours(*add_far(up, down, *far, [late_far_p, *near]))
    late_far, late_near = to_neighbours(late_far_p, late_far_m), to_neighbours(late_near_p, late_near_m)
    late_handed = to_neighbours(*add_far(late_up, late_down, *late_far, []))
    sums = across(add_own(own, *near, *handed, late_handed))
    late_sums = across(add_own(late_own, *late_near, *late_handed, []))
    origin = jnp.stack([ob * out_rows, vb * cols]).astype(jnp.int32)
    return finish([sums, late_sums], row_sizes, origin, irreps)


def solution(mesh):
    placed = (P(("vb", "ob"), None, None), P(None, "ob", "vb"), P(), P())
    return jax.shard_map(
        local, mesh=mesh, in_specs=placed, out_specs=P("ob", None, "vb"), check_vma=False
    )
```

```python
import functools

import jax
import jax.numpy as jnp
import numpy as np
from jax import lax
from jax.experimental import pallas as pl
from jax.experimental.pallas import tpu as pltpu
from jax.sharding import PartitionSpec as P

SIDE = 4
VMEM = 16 * 1024 * 1024
ROOMS = (40 * 1024 * 1024, 16 * 1024 * 1024)
LIGHT = pl.CostEstimate(flops=0, bytes_accessed=0, transcendentals=0)
def hops(count, steps):
    pairs = []
    for i in range(count):
        stride, delta = steps(i)
        at = (i // stride) % SIDE
        pairs.append((i, i + ((at + delta) % SIDE - at) * stride))
    return pairs


Z_stepS = [hops(8, lambda i, d=d: (2, -d if i % 2 else d)) for d in (1, -1, 2)]
SWAP = [(i, i ^ 1) for i in range(8)]
BOTH = ("vb", "ob")
NEAR = {d: hops(128, lambda i, d=d: (1 if i // 16 % 2 else SIDE, d)) for d in (1, -1)}
FAR = {d: hops(128, lambda i, d=d: (SIDE if i // 16 % 2 else 1, d)) for d in (1, 2, -1)}


ORDER = [(2, 0), (2, 1)] + [(2, 2), (2, 3)] + [(1, 2), (1, 3)] + [(3, 0), (3, 1)]
ORDER += [(1, 0), (1, 1)] + [(3, 2), (3, 3)] + [(0, k) for k in range(SIDE)]


SOURCES = [(dz, dc) for dz in (0, -1, 1, 2) for dc in (0, 1)]


def place_table():
    table = np.zeros((8, 16, 16), np.int32)
    for vb in range(8):
        for ob in range(16):
            for a, (dz, dc) in enumerate(SOURCES):
                core = (vb % 2) ^ dc
                source = 2 * ((vb // 2 + (-dz if core else dz)) % SIDE) + core
                for h in range(2):
                    to = 2 * source + h
                    rel = (to // SIDE - ob // SIDE) % SIDE, (to - ob) % SIDE
                    table[vb, ob, 2 * a + h] = ORDER.index(rel[::-1] if vb % 2 else rel)
    return table


PLACES = place_table()
LEADS = (2, 2, 2, 2, 2, 2, 4)


def product_kernel(first, place, sizes, origin, *refs):
    pieces, v_ref, outs, (a_all, v_all) = refs[:8], refs[8], refs[-9:-2], refs[-2:]
    rows = pieces[0].shape[1] // 2
    depth = pieces[0].shape[2]
    for a, piece in enumerate(pieces):
        for h in range(2):
            block = piece[0, h * rows : (h + 1) * rows]
            hi = block.astype(jnp.bfloat16)
            at = pl.ds(pl.multiple_of(place[2 * a + h] * rows, rows), rows)
            a_all[at, 0:depth] = hi
            a_all[at, depth : 2 * depth] = (block - hi.astype(jnp.float32)).astype(jnp.bfloat16)
            a_all[at, 2 * depth : 3 * depth] = hi
    size = sizes[first + pl.program_id(0)]
    shape = v_ref.shape[1:]
    p = origin[0] + lax.broadcasted_iota(jnp.int32, shape, 0)
    q = origin[1] + lax.broadcasted_iota(jnp.int32, shape, 1)
    v = jnp.where((p < size) & (q < size), v_ref[0], 0.0)
    hi = v.astype(jnp.bfloat16)
    v_all[0:depth] = hi
    v_all[depth : 2 * depth] = hi
    v_all[2 * depth : 3 * depth] = (v - hi.astype(jnp.float32)).astype(jnp.bfloat16)
    blocks = [(out, k) for lead, out in zip(LEADS, outs) for k in range(lead)]
    for at in range(0, len(blocks), SIDE):
        acc = jnp.dot(a_all[rows * at : rows * (at + SIDE)], v_all[...], preferred_element_type=jnp.float32)
        for i, (out, k) in enumerate(blocks[at : at + SIDE]):
            out[k, 0] = acc[rows * i : rows * (i + 1)]


def product(pieces, ovov, room, first, count, place, sizes, origin, after):
    rows2, depth = pieces[0][0].shape[1:]
    rows = rows2 // 2
    cols = ovov.shape[2]
    return pl.pallas_call(
        functools.partial(product_kernel, first),
        grid_spec=pltpu.PrefetchScalarGridSpec(
            num_scalar_prefetch=3,
            grid=(count,),
            in_specs=[pl.BlockSpec((1, rows2, depth), lambda g, *_, at=at: (at + g, 0, 0)) for _, at in pieces]
            + [pl.BlockSpec((1, depth, cols), lambda g, *_: (first + g, 0, 0))]
            + [pl.BlockSpec(memory_space=pl.ANY)] * len(after),
            out_specs=[pl.BlockSpec((lead, 1, rows, cols), lambda g, *_: (0, g, 0, 0)) for lead in LEADS],
            scratch_shapes=[
                pltpu.VMEM((16 * rows, 3 * depth), jnp.bfloat16),
                pltpu.VMEM((3 * depth, cols), jnp.bfloat16),
            ],
        ),
        out_shape=[jax.ShapeDtypeStruct((lead, count, rows, cols), jnp.float32) for lead in LEADS],
        compiler_params=pltpu.CompilerParams(vmem_limit_bytes=room),
        cost_estimate=LIGHT,
        name="product",
    )(place, sizes, origin, *[piece for piece, _ in pieces], ovov, *after)


def tie_kernel(*refs):
    pass


def tie(values, after):
    anywhere = pl.BlockSpec(memory_space=pl.ANY)
    return pl.pallas_call(
        tie_kernel,
        in_specs=[anywhere] * (len(values) + len(after)),
        out_specs=[anywhere] * len(values),
        out_shape=[jax.ShapeDtypeStruct(v.shape, v.dtype) for v in values],
        input_output_aliases={i: i for i in range(len(values))},
        compiler_params=pltpu.CompilerParams(vmem_limit_bytes=VMEM),
        cost_estimate=LIGHT,
        name="tie",
    )(*values, *after)


def add_kernel(up, down, recv_p, recv_m, *refs):
    refs[-2][...] = up[...] + recv_p[...]
    refs[-1][...] = down[...] + recv_m[...]


def add_far(up, down, recv_p, recv_m, after):
    lead, count, rows, cols = up.shape
    step = 1 if count % 2 else 2
    spec = pl.BlockSpec((lead, step, rows, cols), lambda g: (0, g, 0, 0))
    return pl.pallas_call(
        add_kernel,
        grid=(count // step,),
        in_specs=[spec] * 4 + [pl.BlockSpec(memory_space=pl.ANY)] * len(after),
        out_specs=[spec] * 2,
        out_shape=[jax.ShapeDtypeStruct(up.shape, jnp.float32)] * 2,
        compiler_params=pltpu.CompilerParams(vmem_limit_bytes=VMEM),
        cost_estimate=LIGHT,
        name="add_far",
    )(up, down, recv_p, recv_m, *after)


def own_kernel(own, n1, n2, p2, m2, *refs):
    outs = refs[-4:]
    outs[0][...] = own[0] + (p2[0] + n2[0])
    outs[1][...] = own[1] + (p2[1] + n2[1])
    outs[2][...] = own[2] + (m2[0] + n1[0])
    outs[3][...] = own[3] + (m2[1] + n1[1])


def add_own(own, n1, n2, p2, m2, after):
    count, rows, cols = own.shape[1:]
    step = 1 if count % 2 else 2

    def spec(lead):
        return pl.BlockSpec((lead, step, rows, cols), lambda g: (0, g, 0, 0))

    return pl.pallas_call(
        own_kernel,
        grid=(count // step,),
        in_specs=[spec(4)] + [spec(2)] * 4 + [pl.BlockSpec(memory_space=pl.ANY)] * len(after),
        out_specs=[pl.BlockSpec((step, rows, cols), lambda g: (g, 0, 0))] * 4,
        out_shape=[jax.ShapeDtypeStruct((count, rows, cols), jnp.float32)] * 4,
        compiler_params=pltpu.CompilerParams(vmem_limit_bytes=VMEM),
        cost_estimate=LIGHT,
        name="add_own",
    )(own, n1, n2, p2, m2, *after)


def finish_kernel(sizes, origin, *refs):
    out = refs[-1]
    rows, irreps, cols = out.shape
    row = origin[0] + lax.broadcasted_iota(jnp.int32, (rows, cols), 0)
    g = 0
    for i in range(0, len(refs) - 1, 4):
        a, b, c, d = refs[i : i + 4]
        for k in range(a.shape[0]):
            out[:, g, :] = jnp.where(row < sizes[g], (a[k] + b[k]) + (c[k] + d[k]), 0.0)
            g += 1


def finish(groups, row_sizes, origin, irreps):
    parts = [part for group in groups for part in group]
    _, rows, cols = parts[0].shape
    return pl.pallas_call(
        finish_kernel,
        grid_spec=pltpu.PrefetchScalarGridSpec(
            num_scalar_prefetch=2,
            grid=(1,),
            in_specs=[pl.BlockSpec(part.shape, lambda r, *_: (0, 0, 0)) for part in parts],
            out_specs=pl.BlockSpec((rows, irreps, cols), lambda r, *_: (0, 0, 0)),
        ),
        out_shape=jax.ShapeDtypeStruct((rows, irreps, cols), jnp.float32),
        compiler_params=pltpu.CompilerParams(vmem_limit_bytes=VMEM),
        cost_estimate=LIGHT,
        name="finish",
    )(row_sizes, origin, *parts)


SPLIT = 4


def local(amplitudes, ovov, row_sizes, pair_sizes):
    ob = lax.axis_index("ob")
    vb = lax.axis_index("vb")
    local_rows, irreps, _ = amplitudes.shape
    obs = lax.axis_size("ob")
    depth, cols = ovov.shape[1:]
    out_rows = local_rows * lax.axis_size("vb")
    place = lax.dynamic_slice(jnp.asarray(PLACES), (vb, ob, 0), (1, 1, 16)).reshape(16)
    origin = jnp.stack([ob * depth, vb * cols]).astype(jnp.int32)

    def exchange(part):
        count = part.shape[1]
        part = jnp.transpose(part.reshape(local_rows, count, obs, depth), (2, 0, 1, 3))
        part = part.reshape(obs, local_rows * count, depth)
        part = lax.all_to_all(part, "ob", split_axis=0, concat_axis=0, tiled=True)
        return jnp.transpose(part.reshape(obs * local_rows, count, depth), (1, 0, 2))

    early, late = exchange(amplitudes[:, :SPLIT]), exchange(amplitudes[:, SPLIT:])

    def swap(piece):
        return lax.ppermute(piece, "vb", SWAP)

    def along_z(held):
        return [lax.ppermute(held, "vb", steps) for steps in Z_stepS]

    def multiply(held, swapped, moved, moved_swapped, first, after):
        pieces = [(held, 0), (swapped, 0)] + [(piece, 0) for pair in zip(moved, moved_swapped) for piece in pair]
        return product(pieces, ovov, ROOMS[first > 0], first, held.shape[0], place, pair_sizes, origin, after)

    def to_neighbours(p, m):
        return lax.ppermute(p, BOTH, NEAR[1]), lax.ppermute(m, BOTH, NEAR[-1])

    def across(four):
        return [four[0]] + [lax.ppermute(four[k], BOTH, FAR[d]) for k, d in ((1, 1), (2, 2), (3, -1))]

    late_swapped = swap(late)
    moved = along_z(early)
    (late,) = tie([late], moved)
    far_p, far_m, near_p, near_m, up, down, own = multiply(early, swap(early), moved, [swap(piece) for piece in moved], 0, [late_swapped])
    far, near = to_neighbours(far_p, far_m), to_neighbours(near_p, near_m)
    up_z, down_z, far_z = along_z(late)
    down_z, far_z = tie([down_z, far_z], [far_p])
    down_swapped, far_swapped = swap(down_z), swap(far_z)
    (up_z,) = tie([up_z], [*far, down_swapped])
    late_far_p, late_far_m, late_near_p, late_near_m, late_up, late_down, late_own = multiply(
        late, late_swapped, (up_z, down_z, far_z), (swap(up_z), down_swapped, far_swapped), SPLIT, []
    )

    handed = to_neighbours(*add_far(up, down, *far, [late_far_p, *near]))
    late_far, late_near = to_neighbours(late_far_p, late_far_m), to_neighbours(late_near_p, late_near_m)
    late_handed = to_neighbours(*add_far(late_up, late_down, *late_far, []))
    sums = across(add_own(own, *near, *handed, late_handed))
    late_sums = across(add_own(late_own, *late_near, *late_handed, []))
    origin = jnp.stack([ob * out_rows, vb * cols]).astype(jnp.int32)
    return finish([sums, late_sums], row_sizes, origin, irreps)


def solution(mesh):
    placed = (P(("vb", "ob"), None, None), P(None, "ob", "vb"), P(), P())
    return jax.shard_map(
        local, mesh=mesh, in_specs=placed, out_specs=P("ob", None, "vb"), check_vma=False
    )
```

```python
import functools

import jax
import jax.numpy as jnp
import numpy as np
from jax import lax
from jax.experimental import pallas as pl
from jax.experimental.pallas import tpu as pltpu
from jax.sharding import PartitionSpec as P

SIDE = 4
VMEM = 16 * 1024 * 1024
ROOMS = (40 * 1024 * 1024, 16 * 1024 * 1024)
LIGHT = pl.CostEstimate(flops=0, bytes_accessed=0, transcendentals=0)
SPLIT = 4


def hops(count, steps):
    pairs = []
    for i in range(count):
        stride, delta = steps(i)
        at = (i // stride) % SIDE
        pairs.append((i, i + ((at + delta) % SIDE - at) * stride))
    return pairs


Z_STEPS = [hops(8, lambda i, d=d: (2, -d if i % 2 else d)) for d in (1, -1, 2)]
SWAP = [(i, i ^ 1) for i in range(8)]
BOTH = ("vb", "ob")
NEAR = {d: hops(128, lambda i, d=d: (1 if i // 16 % 2 else SIDE, d)) for d in (1, -1)}
FAR = {d: hops(128, lambda i, d=d: (SIDE if i // 16 % 2 else 1, d)) for d in (1, 2, -1)}


ORDER = [(2, 0), (2, 1)] + [(2, 2), (2, 3)] + [(1, 2), (1, 3)] + [(3, 0), (3, 1)]
ORDER += [(1, 0), (1, 1)] + [(3, 2), (3, 3)] + [(0, k) for k in range(SIDE)]


SOURCES = [(dz, dc) for dz in (0, -1, 1, 2) for dc in (0, 1)]


def place_table():
    table = np.zeros((8, 16, 16), np.int32)
    for vb in range(8):
        for ob in range(16):
            for a, (dz, dc) in enumerate(SOURCES):
                core = (vb % 2) ^ dc
                source = 2 * ((vb // 2 + (-dz if core else dz)) % SIDE) + core
                for h in range(2):
                    to = 2 * source + h
                    rel = (to // SIDE - ob // SIDE) % SIDE, (to - ob) % SIDE
                    table[vb, ob, 2 * a + h] = ORDER.index(rel[::-1] if vb % 2 else rel)
    return table


PLACES = place_table()
LEADS = (2, 2, 2, 2, 2, 2, 4)


def product_kernel(first, place, sizes, origin, *refs):
    pieces, v_ref, outs, (a_all, v_all) = refs[:8], refs[8], refs[-9:-2], refs[-2:]
    rows = pieces[0].shape[1] // 2
    depth = pieces[0].shape[2]
    for a, piece in enumerate(pieces):
        for h in range(2):
            block = piece[0, h * rows : (h + 1) * rows]
            hi = block.astype(jnp.bfloat16)
            at = pl.ds(pl.multiple_of(place[2 * a + h] * rows, rows), rows)
            a_all[at, 0:depth] = hi
            a_all[at, depth : 2 * depth] = (block - hi.astype(jnp.float32)).astype(jnp.bfloat16)
            a_all[at, 2 * depth : 3 * depth] = hi
    size = sizes[first + pl.program_id(0)]
    shape = v_ref.shape[1:]
    p = origin[0] + lax.broadcasted_iota(jnp.int32, shape, 0)
    q = origin[1] + lax.broadcasted_iota(jnp.int32, shape, 1)
    v = jnp.where((p < size) & (q < size), v_ref[0], 0.0)
    hi = v.astype(jnp.bfloat16)
    v_all[0:depth] = hi
    v_all[depth : 2 * depth] = hi
    v_all[2 * depth : 3 * depth] = (v - hi.astype(jnp.float32)).astype(jnp.bfloat16)
    blocks = [(out, k) for lead, out in zip(LEADS, outs) for k in range(lead)]
    for at in range(0, len(blocks), SIDE):
        acc = jnp.dot(a_all[rows * at : rows * (at + SIDE)], v_all[...], preferred_element_type=jnp.float32)
        for i, (out, k) in enumerate(blocks[at : at + SIDE]):
            out[k, 0] = acc[rows * i : rows * (i + 1)]


def product(pieces, ovov, room, first, count, place, sizes, origin, after):
    rows2, depth = pieces[0][0].shape[1:]
    rows = rows2 // 2
    cols = ovov.shape[2]
    return pl.pallas_call(
        functools.partial(product_kernel, first),
        grid_spec=pltpu.PrefetchScalarGridSpec(
            num_scalar_prefetch=3,
            grid=(count,),
            in_specs=[pl.BlockSpec((1, rows2, depth), lambda g, *_, at=at: (at + g, 0, 0)) for _, at in pieces]
            + [pl.BlockSpec((1, depth, cols), lambda g, *_: (first + g, 0, 0))]
            + [pl.BlockSpec(memory_space=pl.ANY)] * len(after),
            out_specs=[pl.BlockSpec((lead, 1, rows, cols), lambda g, *_: (0, g, 0, 0)) for lead in LEADS],
            scratch_shapes=[
                pltpu.VMEM((16 * rows, 3 * depth), jnp.bfloat16),
                pltpu.VMEM((3 * depth, cols), jnp.bfloat16),
            ],
        ),
        out_shape=[jax.ShapeDtypeStruct((lead, count, rows, cols), jnp.float32) for lead in LEADS],
        compiler_params=pltpu.CompilerParams(vmem_limit_bytes=room),
        cost_estimate=LIGHT,
        name="product",
    )(place, sizes, origin, *[piece for piece, _ in pieces], ovov, *after)


def tie_kernel(*refs):
    pass


def tie(values, after):
    anywhere = pl.BlockSpec(memory_space=pl.ANY)
    return pl.pallas_call(
        tie_kernel,
        in_specs=[anywhere] * (len(values) + len(after)),
        out_specs=[anywhere] * len(values),
        out_shape=[jax.ShapeDtypeStruct(v.shape, v.dtype) for v in values],
        input_output_aliases={i: i for i in range(len(values))},
        compiler_params=pltpu.CompilerParams(vmem_limit_bytes=VMEM),
        cost_estimate=LIGHT,
        name="tie",
    )(*values, *after)


def add_kernel(up, down, recv_p, recv_m, *refs):
    refs[-2][...] = up[...] + recv_p[...]
    refs[-1][...] = down[...] + recv_m[...]


def add_far(up, down, recv_p, recv_m, after):
    lead, count, rows, cols = up.shape
    step = 1 if count % 2 else 2
    spec = pl.BlockSpec((lead, step, rows, cols), lambda g: (0, g, 0, 0))
    return pl.pallas_call(
        add_kernel,
        grid=(count // step,),
        in_specs=[spec] * 4 + [pl.BlockSpec(memory_space=pl.ANY)] * len(after),
        out_specs=[spec] * 2,
        out_shape=[jax.ShapeDtypeStruct(up.shape, jnp.float32)] * 2,
        compiler_params=pltpu.CompilerParams(vmem_limit_bytes=VMEM),
        cost_estimate=LIGHT,
        name="add_far",
    )(up, down, recv_p, recv_m, *after)


def own_kernel(own, n1, n2, p2, m2, *refs):
    outs = refs[-4:]
    outs[0][...] = own[0] + (p2[0] + n2[0])
    outs[1][...] = own[1] + (p2[1] + n2[1])
    outs[2][...] = own[2] + (m2[0] + n1[0])
    outs[3][...] = own[3] + (m2[1] + n1[1])


def add_own(own, n1, n2, p2, m2, after):
    count, rows, cols = own.shape[1:]
    step = 1 if count % 2 else 2

    def spec(lead):
        return pl.BlockSpec((lead, step, rows, cols), lambda g: (0, g, 0, 0))

    return pl.pallas_call(
        own_kernel,
        grid=(count // step,),
        in_specs=[spec(4)] + [spec(2)] * 4 + [pl.BlockSpec(memory_space=pl.ANY)] * len(after),
        out_specs=[pl.BlockSpec((step, rows, cols), lambda g: (g, 0, 0))] * 4,
        out_shape=[jax.ShapeDtypeStruct((count, rows, cols), jnp.float32)] * 4,
        compiler_params=pltpu.CompilerParams(vmem_limit_bytes=VMEM),
        cost_estimate=LIGHT,
        name="add_own",
    )(own, n1, n2, p2, m2, *after)


def finish_kernel(sizes, origin, *refs):
    out = refs[-1]
    rows, irreps, cols = out.shape
    row = origin[0] + lax.broadcasted_iota(jnp.int32, (rows, cols), 0)
    g = 0
    for i in range(0, len(refs) - 1, 4):
        a, b, c, d = refs[i : i + 4]
        for k in range(a.shape[0]):
            out[:, g, :] = jnp.where(row < sizes[g], (a[k] + b[k]) + (c[k] + d[k]), 0.0)
            g += 1


def finish(groups, row_sizes, origin, irreps):
    parts = [part for group in groups for part in group]
    _, rows, cols = parts[0].shape
    return pl.pallas_call(
        finish_kernel,
        grid_spec=pltpu.PrefetchScalarGridSpec(
            num_scalar_prefetch=2,
            grid=(1,),
            in_specs=[pl.BlockSpec(part.shape, lambda r, *_: (0, 0, 0)) for part in parts],
            out_specs=pl.BlockSpec((rows, irreps, cols), lambda r, *_: (0, 0, 0)),
        ),
        out_shape=jax.ShapeDtypeStruct((rows, irreps, cols), jnp.float32),
        compiler_params=pltpu.CompilerParams(vmem_limit_bytes=VMEM),
        cost_estimate=LIGHT,
        name="finish",
    )(row_sizes, origin, *parts)


def local(amplitudes, ovov, row_sizes, pair_sizes):
    ob = lax.axis_index("ob")
    vb = lax.axis_index("vb")
    local_rows, irreps, _ = amplitudes.shape
    obs = lax.axis_size("ob")
    depth, cols = ovov.shape[1:]
    out_rows = local_rows * lax.axis_size("vb")
    place = lax.dynamic_slice(jnp.asarray(PLACES), (vb, ob, 0), (1, 1, 16)).reshape(16)
    origin = jnp.stack([ob * depth, vb * cols]).astype(jnp.int32)

    def exchange(part):
        count = part.shape[1]
        part = jnp.transpose(part.reshape(local_rows, count, obs, depth), (2, 0, 1, 3))
        part = part.reshape(obs, local_rows * count, depth)
        part = lax.all_to_all(part, "ob", split_axis=0, concat_axis=0, tiled=True)
        return jnp.transpose(part.reshape(obs * local_rows, count, depth), (1, 0, 2))

    early, late = exchange(amplitudes[:, :SPLIT]), exchange(amplitudes[:, SPLIT:])

    def swap(piece):
        return lax.ppermute(piece, "vb", SWAP)

    def along_z(held):
        return [lax.ppermute(held, "vb", steps) for steps in Z_STEPS]

    def multiply(held, swapped, moved, moved_swapped, first, after):
        pieces = [(held, 0), (swapped, 0)] + [(piece, 0) for pair in zip(moved, moved_swapped) for piece in pair]
        return product(pieces, ovov, ROOMS[first > 0], first, held.shape[0], place, pair_sizes, origin, after)

    def to_neighbours(p, m):
        return lax.ppermute(p, BOTH, NEAR[1]), lax.ppermute(m, BOTH, NEAR[-1])

    def across(four):
        return [four[0]] + [lax.ppermute(four[k], BOTH, FAR[d]) for k, d in ((1, 1), (2, 2), (3, -1))]

    late_swapped = swap(late)
    moved = along_z(early)
    (late,) = tie([late], moved)
    far_p, far_m, near_p, near_m, up, down, own = multiply(
        early, swap(early), moved, [swap(piece) for piece in moved], 0, [late_swapped]
    )
    far, near = to_neighbours(far_p, far_m), to_neighbours(near_p, near_m)
    up_z, down_z, far_z = along_z(late)
    down_z, far_z = tie([down_z, far_z], [far_p])
    down_swapped, far_swapped = swap(down_z), swap(far_z)
    (up_z,) = tie([up_z], [*far, down_swapped])
    late_far_p, late_far_m, late_near_p, late_near_m, late_up, late_down, late_own = multiply(
        late, late_swapped, (up_z, down_z, far_z), (swap(up_z), down_swapped, far_swapped), SPLIT, []
    )

    handed = to_neighbours(*add_far(up, down, *far, [late_far_p, *near]))
    late_far, late_near = to_neighbours(late_far_p, late_far_m), to_neighbours(late_near_p, late_near_m)
    late_handed = to_neighbours(*add_far(late_up, late_down, *late_far, []))
    sums = across(add_own(own, *near, *handed, late_handed))
    late_sums = across(add_own(late_own, *late_near, *late_handed, []))
    origin = jnp.stack([ob * out_rows, vb * cols]).astype(jnp.int32)
    return finish([sums, late_sums], row_sizes, origin, irreps)


def solution(mesh):
    placed = (P(("vb", "ob"), None, None), P(None, "ob", "vb"), P(), P())
    return jax.shard_map(
        local, mesh=mesh, in_specs=placed, out_specs=P("ob", None, "vb"), check_vma=False
    )
```

```python
import functools

import jax
import jax.numpy as jnp
import numpy as np
from jax import lax
from jax.experimental import pallas as pl
from jax.experimental.pallas import tpu as pltpu
from jax.sharding import PartitionSpec as P

SIDE = 4
VMEM = 16 * 1024 * 1024
ROOMS = (40 * 1024 * 1024, 16 * 1024 * 1024)
LIGHT = pl.CostEstimate(flops=0, bytes_accessed=0, transcendentals=0)
SPLIT = 4


def hops(count, steps):
    pairs = []
    for i in range(count):
        stride, delta = steps(i)
        at = (i // stride) % SIDE
        pairs.append((i, i + ((at + delta) % SIDE - at) * stride))
    return pairs


Z_STEPS = [hops(8, lambda i, d=d: (2, -d if i % 2 else d)) for d in (1, -1, 2)]
SWAP = [(i, i ^ 1) for i in range(8)]
BOTH = ("vb", "ob")
NEAR = {d: hops(128, lambda i, d=d: (1 if i // 16 % 2 else SIDE, d)) for d in (1, -1)}
FAR = {d: hops(128, lambda i, d=d: (SIDE if i // 16 % 2 else 1, d)) for d in (1, 2, -1)}


ORDER = [(2, 0), (2, 1)] + [(2, 2), (2, 3)] + [(1, 2), (1, 3)] + [(3, 0), (3, 1)]
ORDER += [(1, 0), (1, 1)] + [(3, 2), (3, 3)] + [(0, k) for k in range(SIDE)]


SOURCES = [(dz, dc) for dz in (0, -1, 1, 2) for dc in (0, 1)]


def place_table():
    table = np.zeros((8, 16, 16), np.int32)
    for vb in range(8):
        for ob in range(16):
            for a, (dz, dc) in enumerate(SOURCES):
                core = (vb % 2) ^ dc
                source = 2 * ((vb // 2 + (-dz if core else dz)) % SIDE) + core
                for h in range(2):
                    to = 2 * source + h
                    rel = (to // SIDE - ob // SIDE) % SIDE, (to - ob) % SIDE
                    table[vb, ob, 2 * a + h] = ORDER.index(rel[::-1] if vb % 2 else rel)
    return table


PLACES = place_table()
LEADS = (2, 2, 2, 2, 2, 2, 4)


def product_kernel(first, place, sizes, origin, *refs):
    pieces, v_ref, outs, (a_all, v_all) = refs[:8], refs[8], refs[-9:-2], refs[-2:]
    rows = pieces[0].shape[1] // 2
    depth = pieces[0].shape[2]
    for a, piece in enumerate(pieces):
        for h in range(2):
            block = piece[0, h * rows : (h + 1) * rows]
            hi = block.astype(jnp.bfloat16)
            at = pl.ds(pl.multiple_of(place[2 * a + h] * rows, rows), rows)
            a_all[at, 0:depth] = hi
            a_all[at, depth : 2 * depth] = (block - hi.astype(jnp.float32)).astype(jnp.bfloat16)
            a_all[at, 2 * depth : 3 * depth] = hi
    size = sizes[first + pl.program_id(0)]
    shape = v_ref.shape[1:]
    p = origin[0] + lax.broadcasted_iota(jnp.int32, shape, 0)
    q = origin[1] + lax.broadcasted_iota(jnp.int32, shape, 1)
    v = jnp.where((p < size) & (q < size), v_ref[0], 0.0)
    hi = v.astype(jnp.bfloat16)
    v_all[0:depth] = hi
    v_all[depth : 2 * depth] = hi
    v_all[2 * depth : 3 * depth] = (v - hi.astype(jnp.float32)).astype(jnp.bfloat16)
    blocks = [(out, k) for lead, out in zip(LEADS, outs) for k in range(lead)]
    for at in range(0, len(blocks), SIDE):
        acc = jnp.dot(a_all[rows * at : rows * (at + SIDE)], v_all[...], preferred_element_type=jnp.float32)
        for i, (out, k) in enumerate(blocks[at : at + SIDE]):
            out[k, 0] = acc[rows * i : rows * (i + 1)]


def product(pieces, ovov, room, first, count, place, sizes, origin, after):
    rows2, depth = pieces[0][0].shape[1:]
    rows = rows2 // 2
    cols = ovov.shape[2]
    return pl.pallas_call(
        functools.partial(product_kernel, first),
        grid_spec=pltpu.PrefetchScalarGridSpec(
            num_scalar_prefetch=3,
            grid=(count,),
            in_specs=[pl.BlockSpec((1, rows2, depth), lambda g, *_, at=at: (at + g, 0, 0)) for _, at in pieces]
            + [pl.BlockSpec((1, depth, cols), lambda g, *_: (first + g, 0, 0))]
            + [pl.BlockSpec(memory_space=pl.ANY)] * len(after),
            out_specs=[pl.BlockSpec((lead, 1, rows, cols), lambda g, *_: (0, g, 0, 0)) for lead in LEADS],
            scratch_shapes=[
                pltpu.VMEM((16 * rows, 3 * depth), jnp.bfloat16),
                pltpu.VMEM((3 * depth, cols), jnp.bfloat16),
            ],
        ),
        out_shape=[jax.ShapeDtypeStruct((lead, count, rows, cols), jnp.float32) for lead in LEADS],
        compiler_params=pltpu.CompilerParams(vmem_limit_bytes=room),
        cost_estimate=LIGHT,
        name="product",
    )(place, sizes, origin, *[piece for piece, _ in pieces], ovov, *after)


def tie_kernel(*refs):
    pass


def tie(values, after):
    anywhere = pl.BlockSpec(memory_space=pl.ANY)
    return pl.pallas_call(
        tie_kernel,
        in_specs=[anywhere] * (len(values) + len(after)),
        out_specs=[anywhere] * len(values),
        out_shape=[jax.ShapeDtypeStruct(v.shape, v.dtype) for v in values],
        input_output_aliases={i: i for i in range(len(values))},
        compiler_params=pltpu.CompilerParams(vmem_limit_bytes=VMEM),
        cost_estimate=LIGHT,
        name="tie",
    )(*values, *after)


def add_kernel(up, down, recv_p, recv_m, *refs):
    refs[-2][...] = up[...] + recv_p[...]
    refs[-1][...] = down[...] + recv_m[...]


def add_far(up, down, recv_p, recv_m, after):
    lead, count, rows, cols = up.shape
    step = 1 if count % 2 else 2
    spec = pl.BlockSpec((lead, step, rows, cols), lambda g: (0, g, 0, 0))
    return pl.pallas_call(
        add_kernel,
        grid=(count // step,),
        in_specs=[spec] * 4 + [pl.BlockSpec(memory_space=pl.ANY)] * len(after),
        out_specs=[spec] * 2,
        out_shape=[jax.ShapeDtypeStruct(up.shape, jnp.float32)] * 2,
        compiler_params=pltpu.CompilerParams(vmem_limit_bytes=VMEM),
        cost_estimate=LIGHT,
        name="add_far",
    )(up, down, recv_p, recv_m, *after)


def own_kernel(own, n1, n2, p2, m2, *refs):
    outs = refs[-4:]
    outs[0][...] = own[0] + (p2[0] + n2[0])
    outs[1][...] = own[1] + (p2[1] + n2[1])
    outs[2][...] = own[2] + (m2[0] + n1[0])
    outs[3][...] = own[3] + (m2[1] + n1[1])


def add_own(own, n1, n2, p2, m2, after):
    count, rows, cols = own.shape[1:]
    step = 1 if count % 2 else 2

    def spec(lead):
        return pl.BlockSpec((lead, step, rows, cols), lambda g: (0, g, 0, 0))

    return pl.pallas_call(
        own_kernel,
        grid=(count // step,),
        in_specs=[spec(4)] + [spec(2)] * 4 + [pl.BlockSpec(memory_space=pl.ANY)] * len(after),
        out_specs=[pl.BlockSpec((step, rows, cols), lambda g: (g, 0, 0))] * 4,
        out_shape=[jax.ShapeDtypeStruct((count, rows, cols), jnp.float32)] * 4,
        compiler_params=pltpu.CompilerParams(vmem_limit_bytes=VMEM),
        cost_estimate=LIGHT,
        name="add_own",
    )(own, n1, n2, p2, m2, *after)


def sum_kernel(a, b, c, d, out):
    out[...] = (a[...] + b[...]) + (c[...] + d[...])


def add_parts(parts):
    count, rows, cols = parts[0].shape
    spec = pl.BlockSpec((1, rows, cols), lambda g: (g, 0, 0))
    return pl.pallas_call(
        sum_kernel,
        grid=(count,),
        in_specs=[spec] * 4,
        out_specs=spec,
        out_shape=jax.ShapeDtypeStruct(parts[0].shape, jnp.float32),
        compiler_params=pltpu.CompilerParams(vmem_limit_bytes=VMEM),
        cost_estimate=LIGHT,
        name="add_parts",
    )(*parts)


def finish_kernel(sizes, origin, *refs):
    out = refs[-1]
    rows, irreps, cols = out.shape
    row = origin[0] + lax.broadcasted_iota(jnp.int32, (rows, cols), 0)
    summed, a, b, c, d = refs[:-1]
    split = summed.shape[0]
    for g in range(irreps):
        k = g - split
        total = summed[g] if k < 0 else (a[k] + b[k]) + (c[k] + d[k])
        out[:, g, :] = jnp.where(row < sizes[g], total, 0.0)


def finish(parts, row_sizes, origin, irreps):
    _, rows, cols = parts[0].shape
    return pl.pallas_call(
        finish_kernel,
        grid_spec=pltpu.PrefetchScalarGridSpec(
            num_scalar_prefetch=2,
            grid=(1,),
            in_specs=[pl.BlockSpec(part.shape, lambda r, *_: (0, 0, 0)) for part in parts],
            out_specs=pl.BlockSpec((rows, irreps, cols), lambda r, *_: (0, 0, 0)),
        ),
        out_shape=jax.ShapeDtypeStruct((rows, irreps, cols), jnp.float32),
        compiler_params=pltpu.CompilerParams(vmem_limit_bytes=VMEM),
        cost_estimate=LIGHT,
        name="finish",
    )(row_sizes, origin, *parts)


def local(amplitudes, ovov, row_sizes, pair_sizes):
    ob = lax.axis_index("ob")
    vb = lax.axis_index("vb")
    local_rows, irreps, _ = amplitudes.shape
    obs = lax.axis_size("ob")
    depth, cols = ovov.shape[1:]
    out_rows = local_rows * lax.axis_size("vb")
    place = lax.dynamic_slice(jnp.asarray(PLACES), (vb, ob, 0), (1, 1, 16)).reshape(16)
    origin = jnp.stack([ob * depth, vb * cols]).astype(jnp.int32)

    def exchange(part):
        count = part.shape[1]
        part = jnp.transpose(part.reshape(local_rows, count, obs, depth), (2, 0, 1, 3))
        part = part.reshape(obs, local_rows * count, depth)
        part = lax.all_to_all(part, "ob", split_axis=0, concat_axis=0, tiled=True)
        return jnp.transpose(part.reshape(obs * local_rows, count, depth), (1, 0, 2))

    early, late = exchange(amplitudes[:, :SPLIT]), exchange(amplitudes[:, SPLIT:])

    def swap(piece):
        return lax.ppermute(piece, "vb", SWAP)

    def along_z(held):
        return [lax.ppermute(held, "vb", steps) for steps in Z_STEPS]

    def multiply(held, swapped, moved, moved_swapped, first, after):
        pieces = [(held, 0), (swapped, 0)] + [(piece, 0) for pair in zip(moved, moved_swapped) for piece in pair]
        return product(pieces, ovov, ROOMS[first > 0], first, held.shape[0], place, pair_sizes, origin, after)

    def to_neighbours(p, m):
        return lax.ppermute(p, BOTH, NEAR[1]), lax.ppermute(m, BOTH, NEAR[-1])

    def across(four):
        return [four[0]] + [lax.ppermute(four[k], BOTH, FAR[d]) for k, d in ((1, 1), (2, 2), (3, -1))]

    late_swapped = swap(late)
    moved = along_z(early)
    (late,) = tie([late], moved)
    far_p, far_m, near_p, near_m, up, down, own = multiply(
        early, swap(early), moved, [swap(piece) for piece in moved], 0, [late_swapped]
    )
    far, near = to_neighbours(far_p, far_m), to_neighbours(near_p, near_m)
    up_z, down_z, far_z = along_z(late)
    down_z, far_z = tie([down_z, far_z], [far_p])
    down_swapped, far_swapped = swap(down_z), swap(far_z)
    (up_z,) = tie([up_z], [*far, down_swapped])
    late_far_p, late_far_m, late_near_p, late_near_m, late_up, late_down, late_own = multiply(
        late, late_swapped, (up_z, down_z, far_z), (swap(up_z), down_swapped, far_swapped), SPLIT, []
    )

    handed = to_neighbours(*add_far(up, down, *far, [late_far_p, *near]))
    late_far, late_near = to_neighbours(late_far_p, late_far_m), to_neighbours(late_near_p, late_near_m)
    late_handed = to_neighbours(*add_far(late_up, late_down, *late_far, []))
    sums = across(add_own(own, *near, *handed, late_handed))
    late_sums = across(add_own(late_own, *late_near, *late_handed, []))
    origin = jnp.stack([ob * out_rows, vb * cols]).astype(jnp.int32)
    return finish([add_parts(sums), *late_sums], row_sizes, origin, irreps)


def solution(mesh):
    placed = (P(("vb", "ob"), None, None), P(None, "ob", "vb"), P(), P())
    return jax.shard_map(
        local, mesh=mesh, in_specs=placed, out_specs=P("ob", None, "vb"), check_vma=False
    )
```

```python
import functools

import jax
import jax.numpy as jnp
import numpy as np
from jax import lax
from jax.experimental import pallas as pl
from jax.experimental.pallas import tpu as pltpu
from jax.sharding import PartitionSpec as P

SIDE = 4
VMEM = 16 * 1024 * 1024
ROOMS = (40 * 1024 * 1024, 16 * 1024 * 1024)
LIGHT = pl.CostEstimate(flops=0, bytes_accessed=0, transcendentals=0)
SPLIT = 4


def hops(count, steps):
    pairs = []
    for i in range(count):
        stride, delta = steps(i)
        at = (i // stride) % SIDE
        pairs.append((i, i + ((at + delta) % SIDE - at) * stride))
    return pairs


Z_STEPS = [hops(8, lambda i, d=d: (2, -d if i % 2 else d)) for d in (1, -1, 2)]
SWAP = [(i, i ^ 1) for i in range(8)]
BOTH = ("vb", "ob")
NEAR = {d: hops(128, lambda i, d=d: (1 if i // 16 % 2 else SIDE, d)) for d in (1, -1)}
FAR = {d: hops(128, lambda i, d=d: (SIDE if i // 16 % 2 else 1, d)) for d in (1, 2, -1)}


ORDER = [(2, 0), (2, 1)] + [(2, 2), (2, 3)] + [(1, 2), (1, 3)] + [(3, 0), (3, 1)]
ORDER += [(1, 0), (1, 1)] + [(3, 2), (3, 3)] + [(0, k) for k in range(SIDE)]


SOURCES = [(dz, dc) for dz in (0, -1, 1, 2) for dc in (0, 1)]


def place_table():
    table = np.zeros((8, 16, 16), np.int32)
    for vb in range(8):
        for ob in range(16):
            for a, (dz, dc) in enumerate(SOURCES):
                core = (vb % 2) ^ dc
                source = 2 * ((vb // 2 + (-dz if core else dz)) % SIDE) + core
                for h in range(2):
                    to = 2 * source + h
                    rel = (to // SIDE - ob // SIDE) % SIDE, (to - ob) % SIDE
                    table[vb, ob, 2 * a + h] = ORDER.index(rel[::-1] if vb % 2 else rel)
    return table


PLACES = place_table()
LEADS = (2, 2, 2, 2, 2, 2, 4)


def product_kernel(first, place, sizes, origin, *refs):
    pieces, v_ref, outs, (a_all, v_all) = refs[:8], refs[8], refs[-9:-2], refs[-2:]
    rows = pieces[0].shape[1] // 2
    depth = pieces[0].shape[2]
    for a, piece in enumerate(pieces):
        for h in range(2):
            block = piece[0, h * rows : (h + 1) * rows]
            hi = block.astype(jnp.bfloat16)
            at = pl.ds(pl.multiple_of(place[2 * a + h] * rows, rows), rows)
            a_all[at, 0:depth] = hi
            a_all[at, depth : 2 * depth] = (block - hi.astype(jnp.float32)).astype(jnp.bfloat16)
            a_all[at, 2 * depth : 3 * depth] = hi
    size = sizes[first + pl.program_id(0)]
    shape = v_ref.shape[1:]
    p = origin[0] + lax.broadcasted_iota(jnp.int32, shape, 0)
    q = origin[1] + lax.broadcasted_iota(jnp.int32, shape, 1)
    v = jnp.where((p < size) & (q < size), v_ref[0], 0.0)
    hi = v.astype(jnp.bfloat16)
    v_all[0:depth] = hi
    v_all[depth : 2 * depth] = hi
    v_all[2 * depth : 3 * depth] = (v - hi.astype(jnp.float32)).astype(jnp.bfloat16)
    blocks = [(out, k) for lead, out in zip(LEADS, outs) for k in range(lead)]
    for at in range(0, len(blocks), SIDE):
        acc = jnp.dot(a_all[rows * at : rows * (at + SIDE)], v_all[...], preferred_element_type=jnp.float32)
        for i, (out, k) in enumerate(blocks[at : at + SIDE]):
            out[k, 0] = acc[rows * i : rows * (i + 1)]


def product(pieces, ovov, room, first, count, place, sizes, origin, after):
    rows2, depth = pieces[0][0].shape[1:]
    rows = rows2 // 2
    cols = ovov.shape[2]
    return pl.pallas_call(
        functools.partial(product_kernel, first),
        grid_spec=pltpu.PrefetchScalarGridSpec(
            num_scalar_prefetch=3,
            grid=(count,),
            in_specs=[pl.BlockSpec((1, rows2, depth), lambda g, *_, at=at: (at + g, 0, 0)) for _, at in pieces]
            + [pl.BlockSpec((1, depth, cols), lambda g, *_: (first + g, 0, 0))]
            + [pl.BlockSpec(memory_space=pl.ANY)] * len(after),
            out_specs=[pl.BlockSpec((lead, 1, rows, cols), lambda g, *_: (0, g, 0, 0)) for lead in LEADS],
            scratch_shapes=[
                pltpu.VMEM((16 * rows, 3 * depth), jnp.bfloat16),
                pltpu.VMEM((3 * depth, cols), jnp.bfloat16),
            ],
        ),
        out_shape=[jax.ShapeDtypeStruct((lead, count, rows, cols), jnp.float32) for lead in LEADS],
        compiler_params=pltpu.CompilerParams(vmem_limit_bytes=room),
        cost_estimate=LIGHT,
        name="product",
    )(place, sizes, origin, *[piece for piece, _ in pieces], ovov, *after)


def tie_kernel(*refs):
    pass


def tie(values, after):
    anywhere = pl.BlockSpec(memory_space=pl.ANY)
    return pl.pallas_call(
        tie_kernel,
        in_specs=[anywhere] * (len(values) + len(after)),
        out_specs=[anywhere] * len(values),
        out_shape=[jax.ShapeDtypeStruct(v.shape, v.dtype) for v in values],
        input_output_aliases={i: i for i in range(len(values))},
        compiler_params=pltpu.CompilerParams(vmem_limit_bytes=VMEM),
        cost_estimate=LIGHT,
        name="tie",
    )(*values, *after)


def add_kernel(up, down, recv_p, recv_m, *refs):
    refs[-2][...] = up[...] + recv_p[...]
    refs[-1][...] = down[...] + recv_m[...]


def add_far(up, down, recv_p, recv_m, after):
    lead, count, rows, cols = up.shape
    step = 1 if count % 2 else 2
    spec = pl.BlockSpec((lead, step, rows, cols), lambda g: (0, g, 0, 0))
    return pl.pallas_call(
        add_kernel,
        grid=(count // step,),
        in_specs=[spec] * 4 + [pl.BlockSpec(memory_space=pl.ANY)] * len(after),
        out_specs=[spec] * 2,
        out_shape=[jax.ShapeDtypeStruct(up.shape, jnp.float32)] * 2,
        compiler_params=pltpu.CompilerParams(vmem_limit_bytes=VMEM),
        cost_estimate=LIGHT,
        name="add_far",
    )(up, down, recv_p, recv_m, *after)


def own_kernel(own, n1, n2, p2, m2, *refs):
    outs = refs[-4:]
    outs[0][...] = own[0] + (p2[0] + n2[0])
    outs[1][...] = own[1] + (p2[1] + n2[1])
    outs[2][...] = own[2] + (m2[0] + n1[0])
    outs[3][...] = own[3] + (m2[1] + n1[1])


def add_own(own, n1, n2, p2, m2, after):
    count, rows, cols = own.shape[1:]
    step = 1 if count % 2 else 2

    def spec(lead):
        return pl.BlockSpec((lead, step, rows, cols), lambda g: (0, g, 0, 0))

    return pl.pallas_call(
        own_kernel,
        grid=(count // step,),
        in_specs=[spec(4)] + [spec(2)] * 4 + [pl.BlockSpec(memory_space=pl.ANY)] * len(after),
        out_specs=[pl.BlockSpec((step, rows, cols), lambda g: (g, 0, 0))] * 4,
        out_shape=[jax.ShapeDtypeStruct((count, rows, cols), jnp.float32)] * 4,
        compiler_params=pltpu.CompilerParams(vmem_limit_bytes=VMEM),
        cost_estimate=LIGHT,
        name="add_own",
    )(own, n1, n2, p2, m2, *after)


def early_kernel(own, p2, m2, out):
    out[0:2] = own[0:2] + p2[...]
    out[2:4] = own[2:4] + m2[...]


def add_early(own, p2, m2):
    _, count, rows, cols = own.shape

    def spec(lead):
        return pl.BlockSpec((lead, 1, rows, cols), lambda g: (0, g, 0, 0))

    return pl.pallas_call(
        early_kernel,
        grid=(count,),
        in_specs=[spec(4), spec(2), spec(2)],
        out_specs=spec(4),
        out_shape=jax.ShapeDtypeStruct(own.shape, jnp.float32),
        compiler_params=pltpu.CompilerParams(vmem_limit_bytes=VMEM),
        cost_estimate=LIGHT,
        name="add_early",
    )(own, p2, m2)


def last_kernel(own, n1, n2, *outs):
    outs[0][...] = own[0] + n2[0]
    outs[1][...] = own[1] + n2[1]
    outs[2][...] = own[2] + n1[0]
    outs[3][...] = own[3] + n1[1]


def add_last(own, n1, n2):
    _, count, rows, cols = own.shape
    step = 1 if count % 2 else 2

    def spec(lead):
        return pl.BlockSpec((lead, step, rows, cols), lambda g: (0, g, 0, 0))

    return pl.pallas_call(
        last_kernel,
        grid=(count // step,),
        in_specs=[spec(4), spec(2), spec(2)],
        out_specs=[pl.BlockSpec((step, rows, cols), lambda g: (g, 0, 0))] * 4,
        out_shape=[jax.ShapeDtypeStruct((count, rows, cols), jnp.float32)] * 4,
        compiler_params=pltpu.CompilerParams(vmem_limit_bytes=VMEM),
        cost_estimate=LIGHT,
        name="add_last",
    )(own, n1, n2)


def sum_kernel(a, b, c, d, out):
    out[...] = (a[...] + b[...]) + (c[...] + d[...])


def add_parts(parts):
    count, rows, cols = parts[0].shape
    spec = pl.BlockSpec((1, rows, cols), lambda g: (g, 0, 0))
    return pl.pallas_call(
        sum_kernel,
        grid=(count,),
        in_specs=[spec] * 4,
        out_specs=spec,
        out_shape=jax.ShapeDtypeStruct(parts[0].shape, jnp.float32),
        compiler_params=pltpu.CompilerParams(vmem_limit_bytes=VMEM),
        cost_estimate=LIGHT,
        name="add_parts",
    )(*parts)


def finish_kernel(sizes, origin, *refs):
    out = refs[-1]
    rows, irreps, cols = out.shape
    row = origin[0] + lax.broadcasted_iota(jnp.int32, (rows, cols), 0)
    summed, a, b, c, d = refs[:-1]
    split = summed.shape[0]
    for g in range(irreps):
        k = g - split
        total = summed[g] if k < 0 else (a[k] + b[k]) + (c[k] + d[k])
        out[:, g, :] = jnp.where(row < sizes[g], total, 0.0)


def finish(parts, row_sizes, origin, irreps):
    _, rows, cols = parts[0].shape
    return pl.pallas_call(
        finish_kernel,
        grid_spec=pltpu.PrefetchScalarGridSpec(
            num_scalar_prefetch=2,
            grid=(1,),
            in_specs=[pl.BlockSpec(part.shape, lambda r, *_: (0, 0, 0)) for part in parts],
            out_specs=pl.BlockSpec((rows, irreps, cols), lambda r, *_: (0, 0, 0)),
        ),
        out_shape=jax.ShapeDtypeStruct((rows, irreps, cols), jnp.float32),
        compiler_params=pltpu.CompilerParams(vmem_limit_bytes=VMEM),
        cost_estimate=LIGHT,
        name="finish",
    )(row_sizes, origin, *parts)


def local(amplitudes, ovov, row_sizes, pair_sizes):
    ob = lax.axis_index("ob")
    vb = lax.axis_index("vb")
    local_rows, irreps, _ = amplitudes.shape
    obs = lax.axis_size("ob")
    depth, cols = ovov.shape[1:]
    out_rows = local_rows * lax.axis_size("vb")
    place = lax.dynamic_slice(jnp.asarray(PLACES), (vb, ob, 0), (1, 1, 16)).reshape(16)
    origin = jnp.stack([ob * depth, vb * cols]).astype(jnp.int32)

    def exchange(part):
        count = part.shape[1]
        part = jnp.transpose(part.reshape(local_rows, count, obs, depth), (2, 0, 1, 3))
        part = part.reshape(obs, local_rows * count, depth)
        part = lax.all_to_all(part, "ob", split_axis=0, concat_axis=0, tiled=True)
        return jnp.transpose(part.reshape(obs * local_rows, count, depth), (1, 0, 2))

    early, late = exchange(amplitudes[:, :SPLIT]), exchange(amplitudes[:, SPLIT:])

    def swap(piece):
        return lax.ppermute(piece, "vb", SWAP)

    def along_z(held):
        return [lax.ppermute(held, "vb", steps) for steps in Z_STEPS]

    def multiply(held, swapped, moved, moved_swapped, first, after):
        pieces = [(held, 0), (swapped, 0)] + [(piece, 0) for pair in zip(moved, moved_swapped) for piece in pair]
        return product(pieces, ovov, ROOMS[first > 0], first, held.shape[0], place, pair_sizes, origin, after)

    def to_neighbours(p, m):
        return lax.ppermute(p, BOTH, NEAR[1]), lax.ppermute(m, BOTH, NEAR[-1])

    def across(four):
        return [four[0]] + [lax.ppermute(four[k], BOTH, FAR[d]) for k, d in ((1, 1), (2, 2), (3, -1))]

    late_swapped = swap(late)
    moved = along_z(early)
    (late,) = tie([late], moved)
    far_p, far_m, near_p, near_m, up, down, own = multiply(
        early, swap(early), moved, [swap(piece) for piece in moved], 0, [late_swapped]
    )
    far, near = to_neighbours(far_p, far_m), to_neighbours(near_p, near_m)
    up_z, down_z, far_z = along_z(late)
    down_z, far_z = tie([down_z, far_z], [far_p])
    down_swapped, far_swapped = swap(down_z), swap(far_z)
    (up_z,) = tie([up_z], [*far, down_swapped])
    late_far_p, late_far_m, late_near_p, late_near_m, late_up, late_down, late_own = multiply(
        late, late_swapped, (up_z, down_z, far_z), (swap(up_z), down_swapped, far_swapped), SPLIT, []
    )

    handed = to_neighbours(*add_far(up, down, *far, [late_far_p, *near]))
    late_far, late_near = to_neighbours(late_far_p, late_far_m), to_neighbours(late_near_p, late_near_m)
    late_handed = to_neighbours(*add_far(late_up, late_down, *late_far, []))
    sums = across(add_own(own, *near, *handed, late_handed))
    late_sums = across(add_last(add_early(late_own, *late_handed), *late_near))
    origin = jnp.stack([ob * out_rows, vb * cols]).astype(jnp.int32)
    return finish([add_parts(sums), *late_sums], row_sizes, origin, irreps)


def solution(mesh):
    placed = (P(("vb", "ob"), None, None), P(None, "ob", "vb"), P(), P())
    return jax.shard_map(
        local, mesh=mesh, in_specs=placed, out_specs=P("ob", None, "vb"), check_vma=False
    )
```
